32 devices in a mesh: sp: 8 (over z, x), win: 4 (over y, core).
Axes of the slice: x: 2, y: 2, z: 4, core: 2. Of those that a mesh axis runs over, the one named last changes fastest.
Arguments:
- features: bfloat16 [8192, 4096], P(('sp', 'win')), may hold values from -12 to 12
- proj_weight: bfloat16 [4096, 1024], replicated, may hold values from -0.09375 to 0.09375
- partner_offsets: int32 [8, 4], P('sp'), may hold values from 1 to 6, as said below
- ortholog_index: int32 [8192, 4], P(('sp', 'win')), may hold values from 0 to 255
Outputs:
- window_loss: float32 [8192], P(('sp', 'win'))
- weight_grad: float32 [4096, 1024], P(('sp', 'win'))
The draws below stay inside these ranges and needn't reach their ends.
Inputs may be any that keep to these rules, and one draw needn't show every extreme that they name: `partner_offsets`: each row holds 4 different offsets; every offset from 1 to 6 occurs in some row.
All inputs are finite; a program needn't handle non-finite values.
Results may differ from the reference program's by a relative error of at most 0.00585.
The reference program's roundings to bfloat16 on the way (of `projected`, `whitener`, `centered`, `white`, `weights`, `grad_white` and `grad_projected`) count: a program that leaves them out, or rounds other values in their place, can miss the bound.
Values may be sent and summed in bfloat16 or wider, within the bound.
No kernel may reach another device: no remote copies, remote signals or barrier semaphores. Data moves between devices by JAX's collectives and lax.ppermute only.
A program may use at most 128 MiB of HBM per device.

```python
import math
import jax
import jax.numpy as jnp
from jax import lax

F = 4096
E = 1024
TOK_DEV = 256
PARTNERS = 4
MAXOFF = 6
ITERS = 3
GROUPS = 8
TOTAL = 8192
N_WIN = 4


def draw_features(key, part):
    key = jax.random.fold_in(key, 11)
    subkeys = jax.random.split(key, 3)
    row_scale = jnp.exp(jax.random.uniform(subkeys[1], (TOTAL, 1), jnp.float32, math.log(0.5), math.log(5.0)))
    col_scale = jnp.exp(jax.random.uniform(subkeys[2], (1, F), jnp.float32, math.log(0.3), math.log(3.0)))
    values = jax.random.normal(subkeys[0], (TOTAL, F), jnp.float32) * row_scale * col_scale
    return jnp.clip(values, -12.0, 12.0).astype(jnp.bfloat16)


def shuffle_rest(subkey):
    return jax.random.permutation(subkey, MAXOFF - 1)


def shuffle_order(subkey):
    return jax.random.permutation(subkey, PARTNERS)


def draw_partner_offsets(key, part):
    key = jax.random.fold_in(key, 23)
    first, second = jax.random.split(key)
    leading = jnp.arange(GROUPS, dtype=jnp.int32) % MAXOFF
    remaining = jax.vmap(shuffle_rest)(jax.random.split(first, GROUPS))
    others = (leading[:, None] + 1 + remaining[:, :PARTNERS - 1]) % MAXOFF
    table = jnp.concatenate([leading[:, None], others], axis=1) + 1
    ordering = jax.vmap(shuffle_order)(jax.random.split(second, GROUPS))
    return jnp.take_along_axis(table, ordering, axis=1).astype(jnp.int32)


def set_ends(result, own_key, low, largest):
    spot = [jax.random.randint(jax.random.fold_in(own_key, axis), (), 0, length) for axis, length in enumerate(result.shape)]
    longest = result.shape.index(max(result.shape))
    next_to = spot[:longest] + [(spot[longest] + 1) % result.shape[longest]] + spot[longest + 1:]
    return result.at[tuple(spot)].set(low).at[tuple(next_to)].set(largest)


def gaussian(rng, extent, width, limit, kind=jnp.bfloat16):
    return jnp.clip(width * jax.random.normal(rng, extent, jnp.float32), -limit, limit).astype(kind)


def setup_inputs(seed: int = 0) -> dict:
    key_list = jax.random.split(jax.random.key(seed), 5)
    features = draw_features(jax.random.fold_in(key_list[4], 71), 0)
    proj_weight = gaussian(key_list[1], (F, E), F ** -0.5, 0.09375)
    partner_offsets = draw_partner_offsets(jax.random.fold_in(key_list[4], 71), 0)
    ortholog_index = set_ends(jax.random.randint(key_list[3], (TOTAL, PARTNERS), 0, TOK_DEV), jax.random.fold_in(key_list[3], 1), 0, TOK_DEV - 1).astype(jnp.int32)
    return dict(features=features, proj_weight=proj_weight, partner_offsets=partner_offsets, ortholog_index=ortholog_index)


logit_scale = 0.125

def reference(features, proj_weight, partner_offsets, ortholog_index):
    total_rows = features.shape[0]
    highest = lax.Precision.HIGHEST
    projected = jnp.dot(features, proj_weight, preferred_element_type=jnp.float32).astype(jnp.bfloat16)
    projected_wide = projected.astype(jnp.float32)
    mean_row = lax.optimization_barrier(jnp.sum(projected_wide, axis=0)) / total_rows
    centered_wide = projected_wide - mean_row
    covariance = jnp.dot(centered_wide.T, centered_wide, precision=highest, preferred_element_type=jnp.float32) / total_rows
    frobenius = jnp.sqrt(jnp.sum(covariance * covariance))
    scaled = covariance / frobenius
    identity = jnp.eye(E, dtype=jnp.float32)
    iterate = 0.5 * (3.0 * identity - scaled)
    for number in range(ITERS - 1):
        moved = jnp.dot(scaled, iterate, precision=highest, preferred_element_type=jnp.float32)
        quad = jnp.dot(iterate, moved, precision=highest, preferred_element_type=jnp.float32)
        iterate = jnp.dot(iterate, 0.5 * (3.0 * identity - quad), precision=highest, preferred_element_type=jnp.float32)
    whitener = (iterate / jnp.sqrt(frobenius)).astype(jnp.bfloat16)
    centered = centered_wide.astype(jnp.bfloat16)
    white = jnp.dot(centered, whitener, preferred_element_type=jnp.float32).astype(jnp.bfloat16)
    blocks = white.reshape(GROUPS, N_WIN, TOK_DEV, E)
    blocks_wide = blocks.astype(jnp.float32)
    ortho_blocks = ortholog_index.reshape(GROUPS, N_WIN, TOK_DEV, PARTNERS)
    group_ids = jnp.arange(GROUPS, dtype=jnp.int32)
    positions = jnp.arange(TOK_DEV, dtype=jnp.int32)
    loss_total = jnp.zeros((GROUPS, N_WIN, TOK_DEV), jnp.float32)
    grad_total = jnp.zeros((GROUPS, N_WIN, TOK_DEV, E), jnp.float32)
    for partner in range(PARTNERS):
        target = ((group_ids + partner_offsets[:, partner]) % GROUPS).astype(jnp.int32)
        others = blocks_wide[target]
        logits = jnp.einsum('gwie,gwje->gwij', blocks_wide, others, precision=highest) * logit_scale
        peak_value = lax.optimization_barrier(jnp.max(logits, axis=-1, keepdims=True))
        log_total = peak_value + jnp.log(lax.optimization_barrier(jnp.sum(jnp.exp(logits - peak_value), axis=-1, keepdims=True)))
        hit_table = (positions == ortho_blocks[..., partner][..., None]).astype(jnp.float32)
        picked = lax.optimization_barrier(jnp.sum(hit_table * logits, axis=-1))
        loss_total = loss_total + (log_total[..., 0] - picked)
        probabilities = jnp.exp(logits - log_total)
        weights = ((probabilities - hit_table) / PARTNERS).astype(jnp.bfloat16)
        grad_total = grad_total + jnp.einsum('gwij,gwje->gwie', weights.astype(jnp.float32), others, precision=highest)
    window_loss = (loss_total / PARTNERS).reshape(total_rows)
    grad_white = (grad_total * logit_scale).reshape(total_rows, E).astype(jnp.bfloat16)
    grad_projected = jnp.dot(grad_white, whitener.T, preferred_element_type=jnp.float32).astype(jnp.bfloat16)
    weight_grad = jnp.dot(features.T, grad_projected, preferred_element_type=jnp.float32)
    return (window_loss, weight_grad)
```

```python
import jax
import jax.numpy as jnp
from jax import lax
from jax.experimental import pallas as pl
from jax.experimental.pallas import tpu as pltpu
from jax.sharding import PartitionSpec as P

PARTNERS = 4
LOGIT_SCALE = 0.125
AXES = ("sp", "win")
LANES = 128
F32 = jnp.float32
BF16 = jnp.bfloat16
VMEM_LIMIT = 60 * 2**20
HIGHEST = lax.Precision.HIGHEST


def dot(a, b, contract=(1, 0), precision=None):
    return lax.dot_general(
        a,
        b,
        (((contract[0],), (contract[1],)), ((), ())),
        precision=precision,
        preferred_element_type=F32,
    )


def params(semantics=None):
    return pltpu.CompilerParams(
        vmem_limit_bytes=VMEM_LIMIT, dimension_semantics=semantics
    )


def vmem():
    return pl.BlockSpec(memory_space=pltpu.VMEM)


def smem():
    return pl.BlockSpec(memory_space=pltpu.SMEM)


def xor_permute(piece, mask):
    devices = lax.axis_size(AXES)
    return lax.ppermute(piece, AXES, [(i, i ^ mask) for i in range(devices)])


def project_kernel(
    me_ref, features_ref, weight_ref, projected_ref, total_ref, send_ref, keep_ref, acc, wide
):
    step = pl.program_id(0)
    rows, embed = acc.shape
    packed = keep_ref.shape[1]
    blocks = embed // LANES

    @pl.when(step == 0)
    def _():
        acc[...] = jnp.zeros_like(acc)

    acc[...] += dot(features_ref[...], weight_ref[...])

    @pl.when(step == pl.num_programs(0) - 1)
    def _():
        projected = acc[...].astype(BF16)
        projected_ref[...] = projected
        total = jnp.sum(projected.astype(F32), axis=0, keepdims=True)
        total_ref[...] = total
        acc[0:8, :] = jnp.concatenate([total, jnp.zeros((7, embed), F32)], axis=0)
        wide[:, :embed] = projected
        wide[:, embed:] = projected[:, : packed - LANES]
        core = me_ref[0] & 1
        for side, out in ((0, keep_ref), (1, send_ref)):
            for r in range(blocks // 2):
                block = (core ^ side) * (blocks // 2) + r
                start = pl.multiple_of(block * LANES, LANES)
                gram = dot(wide[:, pl.ds(start, LANES)], wide[:, pl.ds(start, packed)], (0, 0))
                means = acc[0:8, pl.ds(start, LANES)] * (1.0 / rows)
                totals = jnp.concatenate(
                    [
                        acc[
                            0:8,
                            pl.ds(
                                pl.multiple_of((block + k) % blocks * LANES, LANES), LANES
                            ),
                        ]
                        for k in range(packed // LANES)
                    ],
                    axis=1,
                )
                gram = gram - dot(means, totals, (0, 0), HIGHEST)
                out[r * LANES : (r + 1) * LANES, :] = gram.astype(out.dtype)


def project(me, features, weight):
    rows, depth = features.shape
    embed = weight.shape[1]
    packed = embed // 2 + LANES
    tile = 512
    return pl.pallas_call(
        project_kernel,
        grid_spec=pltpu.PrefetchScalarGridSpec(
            num_scalar_prefetch=1,
            grid=(depth // tile,),
            in_specs=[
                pl.BlockSpec((rows, tile), lambda k, me: (0, k)),
                pl.BlockSpec((tile, embed), lambda k, me: (k, 0)),
            ],
            out_specs=[
                pl.BlockSpec((rows, embed), lambda k, me: (0, 0)),
                pl.BlockSpec((1, embed), lambda k, me: (0, 0)),
                pl.BlockSpec((embed // 2, packed), lambda k, me: (0, 0)),
                pl.BlockSpec((embed // 2, packed), lambda k, me: (0, 0)),
            ],
            scratch_shapes=[
                pltpu.VMEM((rows, embed), F32),
                pltpu.VMEM((rows, embed + packed - LANES), BF16),
            ],
        ),
        out_shape=[
            jax.ShapeDtypeStruct((rows, embed), BF16),
            jax.ShapeDtypeStruct((1, embed), F32),
            jax.ShapeDtypeStruct((embed // 2, packed), BF16),
            jax.ShapeDtypeStruct((embed // 2, packed), F32),
        ],
        compiler_params=params(("arbitrary",)),
        cost_estimate=pl.CostEstimate(
            flops=2 * rows * depth * embed, bytes_accessed=2 * depth * embed, transcendentals=0
        ),
        name="project",
    )(me, features, weight)


def split(value):
    high = value.astype(BF16)
    return high, (value - high.astype(F32)).astype(BF16)


def make_whiten_kernel(rows):
    def kernel(
        place_ref,
        totals_ref,
        packed_ref,
        whitener_ref,
        mean_ref,
        scaled,
        s_hi,
        s_lo,
        a_hi,
        a_lo,
        b_hi,
        b_lo,
        rest,
    ):
        place = place_ref[0]
        embed = scaled.shape[0]
        blocks = embed // LANES
        half = blocks // 2
        pieces, depth, packed = packed_ref.shape
        per_block = LANES // depth
        devices = totals_ref.shape[0]
        total_rows = rows * devices
        tile = 256
        tiles = embed // tile

        mean = jnp.sum(totals_ref[...], axis=0, keepdims=True) * (1.0 / total_rows)
        mean_ref[...] = mean
        shift = totals_ref[...] * (1.0 / rows) - mean

        for i in range(blocks):
            for part in range(per_block):
                piece = (i * per_block + part) ^ place
                wide = packed_ref[piece].astype(F32)
                lines = pl.ds(i * LANES + part * depth, depth)
                for k in range(half + 1):
                    if k == half and i >= half:
                        continue
                    j = (i + k) % blocks
                    scaled[lines, j * LANES : (j + 1) * LANES] = wide[
                        :, k * LANES : (k + 1) * LANES
                    ]
        for i in range(blocks):
            for k in range(1, half + 1):
                if k == half and i >= half:
                    continue
                j = (i + k) % blocks
                scaled[j * LANES : (j + 1) * LANES, i * LANES : (i + 1) * LANES] = scaled[
                    i * LANES : (i + 1) * LANES, j * LANES : (j + 1) * LANES
                ].T
        squares = jnp.zeros((1, 1), F32)
        for t in range(tiles):
            lines = slice(t * tile, (t + 1) * tile)
            between = dot(shift[:, lines], shift, (0, 0), HIGHEST)
            covariance = (scaled[lines, :] + rows * between) * (1.0 / total_rows)
            scaled[lines, :] = covariance
            squares = squares + jnp.sum(
                jnp.sum(covariance * covariance, axis=0, keepdims=True), axis=1, keepdims=True
            )
        frobenius = jnp.sqrt(squares)
        inverse = 1.0 / frobenius
        root = lax.rsqrt(frobenius)

        @pl.loop(0, tiles)
        def _(t):
            lines = pl.ds(pl.multiple_of(t * tile, tile), tile)
            value = scaled[lines, :] * inverse
            scaled[lines, :] = value
            s_hi[lines, :], s_lo[lines, :] = split(value)

        def product(left, right, finish):
            @pl.loop(0, tiles)
            def _(t):
                lines = pl.ds(pl.multiple_of(t * tile, tile), tile)
                left_hi = left[0][lines, :]
                value = dot(left_hi, right[0][...])
                value += dot(left_hi, right[1][...])
                value += dot(left[1][lines, :], right[0][...])
                finish(lines, value)

        def second(lines, value):
            rest[lines, :] = value
            a_hi[lines, :], a_lo[lines, :] = split(value)
            b_hi[lines, :], b_lo[lines, :] = split(value - 9.0 * scaled[lines, :])

        product((s_hi, s_lo), (s_hi, s_lo), second)

        def fourth(lines, value):
            value = (value + 27.0 * rest[lines, :] - 39.0 * scaled[lines, :]) * (1.0 / 16.0)
            rest[lines, :] = value

        product((a_hi, a_lo), (b_hi, b_lo), fourth)

        @pl.loop(0, tiles)
        def _(t):
            lines = pl.ds(pl.multiple_of(t * tile, tile), tile)
            a_hi[lines, :], a_lo[lines, :] = split(rest[lines, :])

        def moved(lines, value):
            scaled[lines, :] = 2.25 * 2.25 * scaled[lines, :] + 4.5 * value
            b_hi[lines, :], b_lo[lines, :] = split(value)

        product((s_hi, s_lo), (a_hi, a_lo), moved)

        def quad(lines, value):
            value = value + scaled[lines, :]
            scaled[lines, :] = value
            s_hi[lines, :], s_lo[lines, :] = split(value)

        product((a_hi, a_lo), (b_hi, b_lo), quad)

        def last(lines, value):
            at = lax.broadcasted_iota(jnp.int32, value.shape, 0) + lines.start
            eye = at == lax.broadcasted_iota(jnp.int32, value.shape, 1)
            value = 0.5 * (3.0 * rest[lines, :] - 2.25 * scaled[lines, :] - value)
            value = value + jnp.where(eye, 0.5 * 3.0 * 2.25, 0.0)
            whitener_ref[lines, :] = (value * root).astype(BF16)

        product((a_hi, a_lo), (s_hi, s_lo), last)

    return kernel


def whiten(place, totals, packed, rows):
    embed = totals.shape[1]
    square = (embed, embed)
    return pl.pallas_call(
        make_whiten_kernel(rows),
        in_specs=[smem(), vmem(), vmem()],
        out_specs=[vmem(), vmem()],
        out_shape=[
            jax.ShapeDtypeStruct(square, BF16),
            jax.ShapeDtypeStruct((1, embed), F32),
        ],
        scratch_shapes=[pltpu.VMEM(square, F32)]
        + [pltpu.VMEM(square, BF16)] * 6
        + [pltpu.VMEM(square, F32)],
        compiler_params=params(),
        cost_estimate=pl.CostEstimate(
            flops=15 * 2 * embed**3, bytes_accessed=2 * embed**2, transcendentals=0
        ),
        name="whiten",
    )(place, totals, packed)


def contrast_kernel(
    me_ref,
    offsets_ref,
    projected_ref,
    mean_ref,
    whitener_ref,
    features_ref,
    ortholog_ref,
    loss_ref,
    send_ref,
    keep_ref,
    white,
    total,
):
    groups, rows, embed = projected_ref.shape
    shares = send_ref.shape[0] + 1
    share = keep_ref.shape[0]
    group = me_ref[0] // shares
    window = me_ref[0] % shares

    @pl.loop(0, groups)
    def _(g):
        centered = (projected_ref[g].astype(F32) - mean_ref[...]).astype(BF16)
        white[g] = dot(centered, whitener_ref[...]).astype(BF16)

    total[...] = jnp.zeros_like(total)
    places = lax.broadcasted_iota(jnp.int32, (rows, rows), 0)

    @pl.loop(0, groups)
    def _(step):
        g = step ^ group
        own = white[g]
        loss = jnp.zeros((1, rows), F32)
        grad = jnp.zeros((rows, embed), F32)
        for k in range(PARTNERS):
            other = white[(g + offsets_ref[g, k]) % groups]
            logits = dot(other, own, (1, 1)) * LOGIT_SCALE
            peak = jnp.max(logits, axis=0, keepdims=True)
            powers = jnp.exp(logits - peak)
            sums = jnp.sum(powers, axis=0, keepdims=True)
            hit = places == ortholog_ref[g, k : k + 1, :]
            picked = jnp.sum(jnp.where(hit, logits, 0.0), axis=0, keepdims=True)
            loss = loss + (peak + jnp.log(sums) - picked)
            weights = (powers * (1.0 / sums) - hit.astype(F32)) * (1.0 / PARTNERS)
            grad = grad + dot(weights.astype(BF16), other, (0, 0))
        loss_ref[pl.ds(g, 1), :] = loss * (1.0 / PARTNERS)
        grad_white = (grad * LOGIT_SCALE).astype(BF16)
        total[...] += dot(features_ref[step], grad_white, (0, 0))

    for r in range(shares):
        piece = total[pl.ds(pl.multiple_of((window ^ r) * share, share), share), :]
        if r == 0:
            keep_ref[...] = piece
        else:
            send_ref[r - 1] = piece.astype(BF16)


def contrast(me, offsets, projected, mean, whitener, features, ortholog, shares):
    groups, rows, embed = projected.shape
    columns = features.shape[2]
    share = columns // shares
    return pl.pallas_call(
        contrast_kernel,
        in_specs=[smem(), smem()] + [vmem()] * 5,
        out_specs=[vmem()] * 3,
        out_shape=[
            jax.ShapeDtypeStruct((groups, rows), F32),
            jax.ShapeDtypeStruct((shares - 1, share, embed), BF16),
            jax.ShapeDtypeStruct((share, embed), F32),
        ],
        scratch_shapes=[
            pltpu.VMEM((groups, rows, embed), BF16),
            pltpu.VMEM((columns, embed), F32),
        ],
        compiler_params=params(),
        cost_estimate=pl.CostEstimate(
            flops=groups * rows * 2 * embed * (embed + 2 * PARTNERS * rows + columns),
            bytes_accessed=2 * groups * rows * embed,
            transcendentals=groups * PARTNERS * rows * rows,
        ),
        name="contrast",
    )(me, offsets, projected, mean, whitener, features, ortholog)


def shards(features, proj_weight, partner_offsets, ortholog_index):
    rows, depth = features.shape
    embed = proj_weight.shape[1]
    groups = lax.axis_size("sp")
    shares = lax.axis_size("win")
    devices = groups * shares
    group = lax.axis_index("sp")
    me = (group * shares + lax.axis_index("win")).astype(jnp.int32)
    me_scalar = me.reshape(1)

    table = jnp.concatenate(
        [ortholog_index.T, jnp.pad(partner_offsets.T, ((0, 0), (0, LANES - 1)))], axis=1
    )
    table = lax.all_gather(table, "sp")
    ortholog = table[:, :, :rows]
    offsets = table[:, :, rows]

    columns = depth // groups
    slices = [lax.dynamic_slice_in_dim(features, group * columns, columns, 1)]
    for k in range(1, groups):
        piece = lax.dynamic_slice_in_dim(features, (group ^ k) * columns, columns, 1)
        slices.append(xor_permute(piece, k * shares))
    feature_slices = jnp.stack(slices)

    projected, total, send, keep = project(me_scalar, features, proj_weight)
    projected_all = lax.all_gather(projected, "sp")
    totals = lax.all_gather(total[0], AXES)

    packed = keep.shape[1]
    part = keep + xor_permute(send, 1).astype(F32)
    stages = []
    low = 1
    place = me & 1
    while part.shape[0] > 32:
        bits = 2
        count = 1 << bits
        stages.append((low, count))
        pieces = part.reshape(count, part.shape[0] // count, packed)
        own = (me >> low) & (count - 1)
        part = lax.dynamic_index_in_dim(pieces, own, 0, keepdims=False)
        for r in range(1, count):
            sent = lax.dynamic_index_in_dim(pieces, own ^ r, 0, keepdims=False).astype(BF16)
            part = part + xor_permute(sent, r << low).astype(F32)
        place = place * count + own
        low += bits
    extra = devices >> low
    mine = part
    for r in range(1, extra):
        part = part + xor_permute(mine.astype(BF16), r << low).astype(F32)
    part = part.astype(BF16)
    depth_piece = part.shape[0]
    for low, count in reversed(stages):
        part = jnp.concatenate(
            [part] + [xor_permute(part, r << low) for r in range(1, count)], axis=0
        )
    part = jnp.concatenate([part, xor_permute(part, 1)], axis=0)
    part = part.reshape(embed // depth_piece, depth_piece, packed)

    whitener, mean = whiten(place.reshape(1), totals, part, rows)
    loss, send, keep = contrast(
        me_scalar, offsets, projected_all, mean, whitener, feature_slices, ortholog, shares
    )
    for r in range(1, shares):
        keep = keep + xor_permute(send[r - 1], r).astype(F32)
    high, low = split(keep)
    weight_grad = dot(high, whitener, (1, 1)) + dot(low, whitener, (1, 1))
    window_loss = lax.dynamic_index_in_dim(loss, group, 0, keepdims=False)
    return window_loss, weight_grad


def solution(mesh):
    return jax.shard_map(
        shards,
        mesh=mesh,
        in_specs=(P(("sp", "win"), None), P(), P("sp", None), P(("sp", "win"), None)),
        out_specs=(P(("sp", "win")), P(("sp", "win"), None)),
        check_vma=False,
    )
```

```python
import jax
import jax.numpy as jnp
from jax import lax
from jax.experimental import pallas as pl
from jax.experimental.pallas import tpu as pltpu
from jax.sharding import PartitionSpec as P

PARTNERS = 4
LOGIT_SCALE = 0.125
AXES = ("sp", "win")
LANES = 128
F32 = jnp.float32
BF16 = jnp.bfloat16
HIGHEST = lax.Precision.HIGHEST


def dot(a, b, contract=(1, 0), precision=None):
    return lax.dot_general(
        a,
        b,
        (((contract[0],), (contract[1],)), ((), ())),
        precision=precision,
        preferred_element_type=F32,
    )


def params(mebibytes, semantics=None):
    return pltpu.CompilerParams(
        vmem_limit_bytes=mebibytes * 2**20, dimension_semantics=semantics
    )


def vmem():
    return pl.BlockSpec(memory_space=pltpu.VMEM)


def smem():
    return pl.BlockSpec(memory_space=pltpu.SMEM)


def xor_permute(piece, mask):
    devices = lax.axis_size(AXES)
    return lax.ppermute(piece, AXES, [(i, i ^ mask) for i in range(devices)])


def project_kernel(
    me_ref, features_ref, weight_ref, projected_ref, total_ref, send_ref, keep_ref, acc, wide
):
    step = pl.program_id(0)
    rows, embed = acc.shape
    packed = keep_ref.shape[1]
    blocks = embed // LANES

    @pl.when(step == 0)
    def _():
        acc[...] = jnp.zeros_like(acc)

    acc[...] += dot(features_ref[...], weight_ref[...])

    @pl.when(step == pl.num_programs(0) - 1)
    def _():
        projected = acc[...].astype(BF16)
        projected_ref[...] = projected
        total = jnp.sum(projected.astype(F32), axis=0, keepdims=True)
        total_ref[...] = total
        wide[:, :embed] = projected
        wide[:, embed:] = projected[:, : packed - LANES]
        ones = jnp.ones((rows, LANES), BF16)
        means = total * (1.0 / rows)
        acc[0:8, :] = jnp.broadcast_to(means, (8, embed))
        core = me_ref[0] & 1
        for side, out in ((0, keep_ref), (1, send_ref)):
            for r in range(blocks // 2):
                block = (core ^ side) * (blocks // 2) + r
                start = pl.multiple_of(block * LANES, LANES)
                own = wide[:, pl.ds(start, LANES)]
                gram = dot(own, wide[:, pl.ds(start, packed)], (0, 0))
                sums = dot(own, ones, (0, 0))
                for k in range(packed // LANES):
                    other = pl.multiple_of((block + k) % blocks * LANES, LANES)
                    at = slice(k * LANES, (k + 1) * LANES)
                    value = gram[:, at] - sums * acc[0:1, pl.ds(other, LANES)]
                    out[r * LANES : (r + 1) * LANES, at] = value.astype(out.dtype)


def project(me, features, weight):
    rows, depth = features.shape
    embed = weight.shape[1]
    packed = embed // 2 + LANES
    tile = 512
    return pl.pallas_call(
        project_kernel,
        grid_spec=pltpu.PrefetchScalarGridSpec(
            num_scalar_prefetch=1,
            grid=(depth // tile,),
            in_specs=[
                pl.BlockSpec((rows, tile), lambda k, me: (0, k)),
                pl.BlockSpec((tile, embed), lambda k, me: (k, 0)),
            ],
            out_specs=[
                pl.BlockSpec((rows, embed), lambda k, me: (0, 0)),
                pl.BlockSpec((1, embed), lambda k, me: (0, 0)),
                pl.BlockSpec((embed // 2, packed), lambda k, me: (0, 0)),
                pl.BlockSpec((embed // 2, packed), lambda k, me: (0, 0)),
            ],
            scratch_shapes=[
                pltpu.VMEM((rows, embed), F32),
                pltpu.VMEM((rows, embed + packed - LANES), BF16),
            ],
        ),
        out_shape=[
            jax.ShapeDtypeStruct((rows, embed), BF16),
            jax.ShapeDtypeStruct((1, embed), F32),
            jax.ShapeDtypeStruct((embed // 2, packed), BF16),
            jax.ShapeDtypeStruct((embed // 2, packed), F32),
        ],
        compiler_params=params(16, ("arbitrary",)),
        cost_estimate=pl.CostEstimate(
            flops=2 * rows * depth * embed, bytes_accessed=2 * depth * embed, transcendentals=0
        ),
        name="project",
    )(me, features, weight)


def split(value):
    high = value.astype(BF16)
    return high, (value - high.astype(F32)).astype(BF16)


def make_whiten_kernel(rows):
    def kernel(
        place_ref, totals_ref, packed_ref, whitener_ref, mean_ref, scaled, rest, first, left, right
    ):
        place = place_ref[0]
        embed = scaled.shape[0]
        blocks = embed // LANES
        half = blocks // 2
        depth = packed_ref.shape[1]
        per_block = LANES // depth
        total_rows = rows * totals_ref.shape[0]
        tile = 256
        tiles = embed // tile

        mean = jnp.sum(totals_ref[...], axis=0, keepdims=True) * (1.0 / total_rows)
        mean_ref[...] = mean
        shift_high, shift_low = split(totals_ref[...] * (1.0 / rows) - mean)
        shift_left = jnp.concatenate([shift_high, shift_high, shift_low], axis=0)
        shift_right = jnp.concatenate([shift_high, shift_low, shift_high], axis=0)

        for i in range(blocks):
            for part in range(per_block):
                piece = (i * per_block + part) ^ place
                wide = packed_ref[piece].astype(F32)
                lines = pl.ds(i * LANES + part * depth, depth)
                for k in range(half + 1):
                    if k == half and i >= half:
                        continue
                    j = (i + k) % blocks
                    scaled[lines, j * LANES : (j + 1) * LANES] = wide[
                        :, k * LANES : (k + 1) * LANES
                    ]
        for i in range(blocks):
            for k in range(1, half + 1):
                if k == half and i >= half:
                    continue
                j = (i + k) % blocks
                scaled[j * LANES : (j + 1) * LANES, i * LANES : (i + 1) * LANES] = scaled[
                    i * LANES : (i + 1) * LANES, j * LANES : (j + 1) * LANES
                ].T
        squares = jnp.zeros((1, embed), F32)
        for t in range(tiles):
            lines = slice(t * tile, (t + 1) * tile)
            between = dot(shift_left[:, lines], shift_right, (0, 0))
            covariance = (scaled[lines, :] + rows * between) * (1.0 / total_rows)
            scaled[lines, :] = covariance
            first[lines, :] = covariance.astype(BF16)
            squares = squares + jnp.sum(covariance * covariance, axis=0, keepdims=True)
        frobenius = jnp.sqrt(jnp.sum(squares, axis=1, keepdims=True))
        inverse = 1.0 / frobenius
        root = lax.rsqrt(frobenius)

        def product(one, two, finish):
            @pl.loop(0, tiles)
            def _(t):
                lines = pl.ds(pl.multiple_of(t * tile, tile), tile)
                finish(lines, dot(one[lines, :], two[...]))

        def second(lines, value):
            value = value * (inverse * inverse)
            own = scaled[lines, :] * inverse
            scaled[lines, :] = own
            rest[lines, :] = 27.0 * value - 39.0 * own
            left[lines, :] = value.astype(BF16)
            right[lines, :] = (value - 9.0 * own).astype(BF16)

        product(first, first, second)

        def fourth(lines, value):
            value = (value + rest[lines, :]) * (1.0 / 16.0)
            rest[lines, :] = value
            whitener_ref[lines, :] = value.astype(BF16)

        product(left, right, fourth)

        def moved(lines, value):
            value = value * inverse
            scaled[lines, :] = 2.25 * 2.25 * scaled[lines, :] + 4.5 * value
            right[lines, :] = value.astype(BF16)

        product(first, whitener_ref, moved)

        def quad(lines, value):
            value = value + scaled[lines, :]
            rest[lines, :] = 3.0 * rest[lines, :] - 2.25 * value
            left[lines, :] = value.astype(BF16)

        product(whitener_ref, right, quad)
        first[...] = whitener_ref[...]

        def last(lines, value):
            at = lax.broadcasted_iota(jnp.int32, value.shape, 0) + lines.start
            eye = at == lax.broadcasted_iota(jnp.int32, value.shape, 1)
            value = 0.5 * (rest[lines, :] - value)
            value = value + jnp.where(eye, 0.5 * 3.0 * 2.25, 0.0)
            whitener_ref[lines, :] = (value * root).astype(BF16)

        product(first, left, last)

    return kernel


def whiten(place, totals, packed, rows):
    embed = totals.shape[1]
    square = (embed, embed)
    return pl.pallas_call(
        make_whiten_kernel(rows),
        in_specs=[smem(), vmem(), vmem()],
        out_specs=[vmem(), vmem()],
        out_shape=[
            jax.ShapeDtypeStruct(square, BF16),
            jax.ShapeDtypeStruct((1, embed), F32),
        ],
        scratch_shapes=[pltpu.VMEM(square, F32)] * 2 + [pltpu.VMEM(square, BF16)] * 3,
        compiler_params=params(24),
        cost_estimate=pl.CostEstimate(
            flops=5 * 2 * embed**3, bytes_accessed=2 * embed**2, transcendentals=0
        ),
        name="whiten",
    )(place, totals, packed)


def contrast_kernel(
    group_ref, offsets_ref, projected_ref, mean_ref, whitener_ref, ortholog_ref, loss_ref, grad_ref, white
):
    groups, rows, embed = projected_ref.shape
    group = group_ref[0]

    @pl.loop(0, groups)
    def _(g):
        centered = (projected_ref[g].astype(F32) - mean_ref[...]).astype(BF16)
        white[g] = dot(centered, whitener_ref[...]).astype(BF16)

    places = lax.broadcasted_iota(jnp.int32, (rows, rows), 0)

    @pl.loop(0, groups)
    def _(step):
        g = step ^ group
        own = white[g]
        loss = jnp.zeros((1, rows), F32)
        grad = jnp.zeros((rows, embed), F32)
        for k in range(PARTNERS):
            other = white[(g + offsets_ref[step, k]) % groups]
            logits = dot(other, own, (1, 1)) * LOGIT_SCALE
            peak = jnp.max(logits, axis=0, keepdims=True)
            powers = jnp.exp(logits - peak)
            sums = jnp.sum(powers, axis=0, keepdims=True)
            hit = places == ortholog_ref[step, k : k + 1, :]
            picked = jnp.sum(jnp.where(hit, logits, 0.0), axis=0, keepdims=True)
            loss = loss + (peak + jnp.log(sums) - picked)
            weights = (powers * (1.0 / sums) - hit.astype(F32)) * (1.0 / PARTNERS)
            grad = grad + dot(weights.astype(BF16), other, (0, 0))
        grad_ref[step] = (grad * LOGIT_SCALE).astype(BF16)

        @pl.when(step == 0)
        def _():
            loss_ref[...] = loss * (1.0 / PARTNERS)


def contrast(group, offsets, projected, mean, whitener, ortholog):
    groups, rows, embed = projected.shape
    return pl.pallas_call(
        contrast_kernel,
        in_specs=[smem(), smem()] + [vmem()] * 4,
        out_specs=[vmem()] * 2,
        out_shape=[
            jax.ShapeDtypeStruct((1, rows), F32),
            jax.ShapeDtypeStruct((groups, rows, embed), BF16),
        ],
        scratch_shapes=[pltpu.VMEM((groups, rows, embed), BF16)],
        compiler_params=params(12 + 6 * groups * rows * embed // 2**20),
        cost_estimate=pl.CostEstimate(
            flops=groups * rows * 2 * embed * (embed + 2 * PARTNERS * rows),
            bytes_accessed=4 * groups * rows * embed,
            transcendentals=groups * PARTNERS * rows * rows,
        ),
        name="contrast",
    )(group, offsets, projected, mean, whitener, ortholog)


def gather_kernel(window_ref, grad_ref, *refs):
    groups = grad_ref.shape[0]
    feature_refs = refs[:groups]
    outs, total = refs[groups:-1], refs[-1]
    share = outs[0].shape[0]
    window = window_ref[0]

    def columns(at):
        value = dot(feature_refs[0][:, at], grad_ref[0], (0, 0))
        for k in range(1, groups):
            value = value + dot(feature_refs[k][:, at], grad_ref[k], (0, 0))
        return value

    if share % LANES:
        total[...] = columns(slice(None))
    for r, out in enumerate(outs):
        at = pl.ds(pl.multiple_of((window ^ r) * share, share), share)
        value = total[at, :] if share % LANES else columns(at)
        out[...] = value.astype(out.dtype)


def weight_pieces(window, grad, feature_slices, shares):
    groups, rows, embed = grad.shape
    columns = feature_slices[0].shape[1]
    share = columns // shares
    return pl.pallas_call(
        gather_kernel,
        in_specs=[smem()] + [vmem()] * (1 + groups),
        out_specs=[vmem()] * shares,
        out_shape=[
            jax.ShapeDtypeStruct((share, embed), BF16 if r else F32) for r in range(shares)
        ],
        scratch_shapes=[pltpu.VMEM((columns if share % LANES else 8, embed), F32)],
        compiler_params=params(24),
        cost_estimate=pl.CostEstimate(
            flops=groups * rows * 2 * embed * columns,
            bytes_accessed=2 * groups * rows * (embed + columns),
            transcendentals=0,
        ),
        name="weight_pieces",
    )(window, grad, *feature_slices)


def finish_kernel(*refs):
    keep_ref, whitener_ref, out_ref = refs[0], refs[-2], refs[-1]
    value = keep_ref[...]
    for ref in refs[1:-2]:
        value = value + ref[...].astype(F32)
    high, low = split(value)
    out_ref[...] = dot(high, whitener_ref[...], (1, 1)) + dot(low, whitener_ref[...], (1, 1))


def finish(pieces, whitener):
    return pl.pallas_call(
        finish_kernel,
        in_specs=[vmem()] * (len(pieces) + 1),
        out_specs=vmem(),
        out_shape=jax.ShapeDtypeStruct(pieces[0].shape, F32),
        compiler_params=params(12),
        name="finish",
    )(*pieces, whitener)


def shards(features, proj_weight, partner_offsets, ortholog_index):
    rows, depth = features.shape
    embed = proj_weight.shape[1]
    groups = lax.axis_size("sp")
    shares = lax.axis_size("win")
    devices = groups * shares
    group = lax.axis_index("sp")
    me = (group * shares + lax.axis_index("win")).astype(jnp.int32)
    me_scalar = me.reshape(1)

    table = jnp.concatenate(
        [ortholog_index.T, jnp.pad(partner_offsets.T, ((0, 0), (0, LANES - 1)))], axis=1
    )
    table = jnp.stack([table] + [xor_permute(table, k * shares) for k in range(1, groups)])
    ortholog = table[:, :, :rows]
    offsets = table[:, :, rows]

    projected, total, send, keep = project(me_scalar, features, proj_weight)
    projected_all = lax.all_gather(projected, "sp")

    packed = keep.shape[1]
    totals = total
    part = keep + xor_permute(send, 1).astype(F32)
    totals = jnp.concatenate([totals, xor_permute(totals, 1)], axis=0)
    stages = []
    low = 1
    place = me & 1
    while part.shape[0] > 32:
        bits = 2
        count = 1 << bits
        stages.append((low, count))
        pieces = part.reshape(count, part.shape[0] // count, packed)
        own = (me >> low) & (count - 1)
        part = lax.dynamic_index_in_dim(pieces, own, 0, keepdims=False)
        for r in range(1, count):
            sent = lax.dynamic_index_in_dim(pieces, own ^ r, 0, keepdims=False).astype(BF16)
            part = part + xor_permute(sent, r << low).astype(F32)
        totals = jnp.concatenate(
            [totals] + [xor_permute(totals, r << low) for r in range(1, count)], axis=0
        )
        place = place * count + own
        low += bits
    extra = devices >> low
    mine = part
    for r in range(1, extra):
        part = part + xor_permute(mine.astype(BF16), r << low).astype(F32)
    totals = jnp.concatenate(
        [totals] + [xor_permute(totals, r << low) for r in range(1, extra)], axis=0
    )
    part = part.astype(BF16)
    depth_piece = part.shape[0]
    for low, count in reversed(stages):
        part = jnp.concatenate(
            [part] + [xor_permute(part, r << low) for r in range(1, count)], axis=0
        )
    part = jnp.concatenate([part, xor_permute(part, 1)], axis=0)
    part = part.reshape(embed // depth_piece, depth_piece, packed)

    columns = depth // groups
    slices = [
        lax.dynamic_slice_in_dim(features, (group ^ k) * columns, columns, 1) for k in range(groups)
    ]
    part, *slices = lax.optimization_barrier((part, *slices))
    for k in range(1, groups):
        slices[k] = xor_permute(slices[k], k * shares)

    whitener, mean = whiten(place.reshape(1), totals, part, rows)
    loss, grad = contrast(group.reshape(1), offsets, projected_all, mean, whitener, ortholog)
    window = lax.axis_index("win").reshape(1)
    pieces = weight_pieces(window, grad, slices, shares)
    pieces = [pieces[0]] + [xor_permute(pieces[r], r) for r in range(1, shares)]
    return loss[0], finish(pieces, whitener)


def solution(mesh):
    return jax.shard_map(
        shards,
        mesh=mesh,
        in_specs=(P(("sp", "win"), None), P(), P("sp", None), P(("sp", "win"), None)),
        out_specs=(P(("sp", "win")), P(("sp", "win"), None)),
        check_vma=False,
    )
```

```python
import jax
import jax.numpy as jnp
from jax import lax
from jax.experimental import pallas as pl
from jax.experimental.pallas import tpu as pltpu
from jax.sharding import PartitionSpec as P

PARTNERS = 4
LOGIT_SCALE = 0.125
AXES = ("sp", "win")
LANES = 128
TAIL = 16
F32 = jnp.float32
BF16 = jnp.bfloat16
HIGHEST = lax.Precision.HIGHEST


def dot(a, b, contract=(1, 0), precision=None):
    return lax.dot_general(
        a,
        b,
        (((contract[0],), (contract[1],)), ((), ())),
        precision=precision,
        preferred_element_type=F32,
    )


def params(mebibytes, semantics=None):
    return pltpu.CompilerParams(
        vmem_limit_bytes=mebibytes * 2**20, dimension_semantics=semantics
    )


def vmem():
    return pl.BlockSpec(memory_space=pltpu.VMEM)


def smem():
    return pl.BlockSpec(memory_space=pltpu.SMEM)


def xor_permute(piece, mask):
    devices = lax.axis_size(AXES)
    return lax.ppermute(piece, AXES, [(i, i ^ mask) for i in range(devices)])


def split(value):
    high = value.astype(BF16)
    return high, (value - high.astype(F32)).astype(BF16)


def pack_sums(sums, packed, rows):
    high = sums.astype(BF16).astype(F32)
    pad = jnp.zeros((sums.shape[0], 2 * packed - sums.shape[1]), F32)
    lines = []
    for half in (high, sums - high):
        lines += [half[:, :packed], jnp.concatenate([half[:, packed:], pad], axis=1)]
    if rows > 4 * sums.shape[0]:
        lines.append(jnp.zeros((rows - 4 * sums.shape[0], packed), F32))
    return jnp.concatenate(lines, axis=0).astype(BF16)


def unpack_sums(block, count, embed):
    wide = block.astype(F32)
    packed = wide.shape[1]
    low = 2 * count
    left = wide[0:count] + wide[low : low + count]
    right = wide[count:low] + wide[low + count : low + 2 * count]
    return jnp.concatenate([left, right[:, : embed - packed]], axis=1)


def project_kernel(
    me_ref,
    offsets_ref,
    features_ref,
    weight_ref,
    ortholog_ref,
    block_ref,
    slices_ref,
    send_ref,
    keep_ref,
    acc,
    wide,
):
    step = pl.program_id(0)
    rows, embed = acc.shape
    half, packed = keep_ref.shape
    blocks = embed // LANES

    @pl.when(step == 0)
    def _():
        acc[...] = jnp.zeros_like(acc)

    slices_ref[0] = features_ref[...]
    acc[...] += dot(features_ref[...], weight_ref[...])

    @pl.when(step == pl.num_programs(0) - 1)
    def _():
        projected = acc[...].astype(BF16)
        block_ref[0:rows, :] = projected
        line = lax.broadcasted_iota(jnp.int32, (TAIL, embed), 0)
        lane = lax.broadcasted_iota(jnp.int32, (TAIL, embed), 1)
        table = jnp.zeros((TAIL, embed), F32)
        for k in range(PARTNERS):
            table = jnp.where((line == 1) & (lane == k), offsets_ref[0, k].astype(F32), table)
        hits = jnp.concatenate(
            [ortholog_ref[k : k + 1, :].astype(F32) for k in range(PARTNERS)]
            + ([jnp.zeros((1, embed - PARTNERS * rows), F32)] if embed > PARTNERS * rows else []),
            axis=1,
        )
        block_ref[rows:, :] = jnp.where(line == 0, hits, table).astype(BF16)

        total = jnp.sum(projected.astype(F32), axis=0, keepdims=True)
        send_ref[half:, :] = pack_sums(total, packed, TAIL)
        wide[:, :embed] = projected
        wide[:, embed:] = projected[:, : packed - LANES]
        ones = jnp.ones((rows, LANES), BF16)
        acc[0:8, :] = jnp.broadcast_to(total * (1.0 / rows), (8, embed))
        core = me_ref[0] & 1
        for side, out in ((0, keep_ref), (1, send_ref)):
            for r in range(blocks // 2):
                block = (core ^ side) * (blocks // 2) + r
                start = pl.multiple_of(block * LANES, LANES)
                own = wide[:, pl.ds(start, LANES)]
                gram = dot(own, wide[:, pl.ds(start, packed)], (0, 0))
                sums = dot(own, ones, (0, 0))
                for k in range(packed // LANES):
                    other = pl.multiple_of((block + k) % blocks * LANES, LANES)
                    at = slice(k * LANES, (k + 1) * LANES)
                    value = gram[:, at] - sums * acc[0:1, pl.ds(other, LANES)]
                    out[r * LANES : (r + 1) * LANES, at] = value.astype(out.dtype)


def project(me, offsets, features, weight, ortholog, groups):
    rows, depth = features.shape
    embed = weight.shape[1]
    packed = embed // 2 + LANES
    tile = depth // groups
    fixed = lambda k, *_: (0, 0)
    return pl.pallas_call(
        project_kernel,
        grid_spec=pltpu.PrefetchScalarGridSpec(
            num_scalar_prefetch=2,
            grid=(groups,),
            in_specs=[
                pl.BlockSpec((rows, tile), lambda k, *_: (0, k)),
                pl.BlockSpec((tile, embed), lambda k, *_: (k, 0)),
                pl.BlockSpec((PARTNERS, rows), fixed),
            ],
            out_specs=[
                pl.BlockSpec((rows + TAIL, embed), fixed),
                pl.BlockSpec((1, rows, tile), lambda k, *_: (k, 0, 0)),
                pl.BlockSpec((embed // 2 + TAIL, packed), fixed),
                pl.BlockSpec((embed // 2, packed), fixed),
            ],
            scratch_shapes=[
                pltpu.VMEM((rows, embed), F32),
                pltpu.VMEM((rows, embed + packed - LANES), BF16),
            ],
        ),
        out_shape=[
            jax.ShapeDtypeStruct((rows + TAIL, embed), BF16),
            jax.ShapeDtypeStruct((groups, rows, tile), BF16),
            jax.ShapeDtypeStruct((embed // 2 + TAIL, packed), BF16),
            jax.ShapeDtypeStruct((embed // 2, packed), F32),
        ],
        compiler_params=params(40, ("arbitrary",)),
        cost_estimate=pl.CostEstimate(
            flops=2 * rows * depth * embed, bytes_accessed=2 * depth * embed, transcendentals=0
        ),
        name="project",
    )(me, offsets, features, weight, ortholog)


def make_stage_kernel(seen, arrivals, count, embed):
    def kernel(own_ref, keep_ref, sent_ref, *refs):
        arrived, next_keep, outs = refs[:arrivals], refs[arrivals], refs[arrivals + 1 :]
        full, packed = keep_ref.shape
        share = full // count
        own = own_ref[0]
        sums = [unpack_sums(ref[full:, :], seen, embed) for ref in (sent_ref, *arrived)]
        block = pack_sums(jnp.concatenate(sums, axis=0), packed, outs[0].shape[0] - share)
        for r in range(count):
            at = pl.ds(pl.multiple_of((own ^ r) * share, share), share)
            value = keep_ref[at, :]
            for ref in arrived:
                value = value + ref[at, :].astype(F32)
            if r == 0:
                next_keep[...] = value
            else:
                outs[r - 1][:share, :] = value.astype(BF16)
                outs[r - 1][share:, :] = block

    return kernel


def stage(own, keep, sent, arrived, seen, count, embed):
    full, packed = keep.shape
    share = full // count
    held = seen * (1 + len(arrived))
    tail = -(-4 * held // TAIL) * TAIL
    out = pl.pallas_call(
        make_stage_kernel(seen, len(arrived), count, embed),
        in_specs=[smem()] + [vmem()] * (2 + len(arrived)),
        out_specs=[vmem()] * count,
        out_shape=[jax.ShapeDtypeStruct((share, packed), F32)]
        + [jax.ShapeDtypeStruct((share + tail, packed), BF16)] * (count - 1),
        compiler_params=params(16),
        cost_estimate=pl.CostEstimate(
            flops=full * packed, bytes_accessed=4 * full * packed, transcendentals=0
        ),
        name="stage",
    )(own.reshape(1), keep, sent, *arrived)
    return out[0], out[1:], held


def make_whiten_kernel(rows):
    def kernel(
        place_ref,
        sums_ref,
        near_ref,
        far_ref,
        whitener_ref,
        mean_ref,
        scaled,
        rest,
        first,
        left,
        right,
    ):
        place = place_ref[0]
        embed = scaled.shape[0]
        blocks = embed // LANES
        half = blocks // 2
        pieces, depth = near_ref.shape[:2]
        per_block = LANES // depth
        count = sums_ref.shape[1] // 4
        totals = jnp.concatenate(
            [unpack_sums(sums_ref[k], count, embed) for k in range(sums_ref.shape[0])], axis=0
        )
        total_rows = rows * totals.shape[0]
        tile = 256
        tiles = embed // tile

        mean = jnp.sum(totals, axis=0, keepdims=True) * (1.0 / total_rows)
        mean_ref[...] = mean
        shift_high, shift_low = split(totals * (1.0 / rows) - mean)
        shift_left = jnp.concatenate([shift_high, shift_high, shift_low], axis=0)
        shift_right = jnp.concatenate([shift_high, shift_low, shift_high], axis=0)

        def unpack(source_ref, side):
            for i in range(side * half, (side + 1) * half):
                for part in range(per_block):
                    piece = ((i - side * half) * per_block + part) ^ (place & (pieces - 1))
                    wide = source_ref[piece].astype(F32)
                    lines = pl.ds(i * LANES + part * depth, depth)
                    for k in range(half + 1):
                        if k == half and side:
                            continue
                        j = (i + k) % blocks
                        scaled[lines, j * LANES : (j + 1) * LANES] = wide[
                            :, k * LANES : (k + 1) * LANES
                        ]

        for core in range(2):

            @pl.when(place // pieces == core)
            def _():
                unpack(near_ref, core)
                unpack(far_ref, 1 - core)

        for i in range(blocks):
            for k in range(1, half + 1):
                if k == half and i >= half:
                    continue
                j = (i + k) % blocks
                scaled[j * LANES : (j + 1) * LANES, i * LANES : (i + 1) * LANES] = scaled[
                    i * LANES : (i + 1) * LANES, j * LANES : (j + 1) * LANES
                ].T
        squares = jnp.zeros((1, embed), F32)
        for t in range(tiles):
            lines = slice(t * tile, (t + 1) * tile)
            between = dot(shift_left[:, lines], shift_right, (0, 0))
            covariance = (scaled[lines, :] + rows * between) * (1.0 / total_rows)
            scaled[lines, :] = covariance
            first[lines, :] = covariance.astype(BF16)
            squares = squares + jnp.sum(covariance * covariance, axis=0, keepdims=True)
        frobenius = jnp.sqrt(jnp.sum(squares, axis=1, keepdims=True))
        inverse = 1.0 / frobenius
        root = lax.rsqrt(frobenius)

        def product(one, two, finish):
            @pl.loop(0, tiles)
            def _(t):
                lines = pl.ds(pl.multiple_of(t * tile, tile), tile)
                finish(lines, dot(one[lines, :], two[...]))

        def second(lines, value):
            value = value * (inverse * inverse)
            own = scaled[lines, :] * inverse
            scaled[lines, :] = own
            rest[lines, :] = 27.0 * value - 39.0 * own
            left[lines, :] = value.astype(BF16)
            right[lines, :] = (value - 9.0 * own).astype(BF16)

        product(first, first, second)

        def fourth(lines, value):
            value = (value + rest[lines, :]) * (1.0 / 16.0)
            rest[lines, :] = value
            whitener_ref[lines, :] = value.astype(BF16)

        product(left, right, fourth)

        def moved(lines, value):
            value = value * inverse
            scaled[lines, :] = 2.25 * 2.25 * scaled[lines, :] + 4.5 * value
            right[lines, :] = value.astype(BF16)

        product(first, whitener_ref, moved)

        def quad(lines, value):
            value = value + scaled[lines, :]
            rest[lines, :] = 3.0 * rest[lines, :] - 2.25 * value
            left[lines, :] = value.astype(BF16)

        product(whitener_ref, right, quad)
        first[...] = whitener_ref[...]

        def last(lines, value):
            at = lax.broadcasted_iota(jnp.int32, value.shape, 0) + lines.start
            eye = at == lax.broadcasted_iota(jnp.int32, value.shape, 1)
            value = 0.5 * (rest[lines, :] - value)
            value = value + jnp.where(eye, 0.5 * 3.0 * 2.25, 0.0)
            whitener_ref[lines, :] = (value * root).astype(BF16)

        product(first, left, last)

    return kernel


def whiten(place, sums, near, far, rows, embed):
    square = (embed, embed)
    return pl.pallas_call(
        make_whiten_kernel(rows),
        in_specs=[smem()] + [vmem()] * 3,
        out_specs=[vmem(), vmem()],
        out_shape=[
            jax.ShapeDtypeStruct(square, BF16),
            jax.ShapeDtypeStruct((1, embed), F32),
        ],
        scratch_shapes=[pltpu.VMEM(square, F32)] * 2 + [pltpu.VMEM(square, BF16)] * 3,
        compiler_params=params(24),
        cost_estimate=pl.CostEstimate(
            flops=5 * 2 * embed**3, bytes_accessed=2 * embed**2, transcendentals=0
        ),
        name="whiten",
    )(place, sums, near, far)


def contrast_kernel(
    group_ref, offsets_ref, blocks_ref, mean_ref, whitener_ref, loss_ref, grad_ref, white
):
    groups, rows, embed = white.shape
    group = group_ref[0]

    @pl.loop(0, groups)
    def _(g):
        centered = (blocks_ref[g, 0:rows, :].astype(F32) - mean_ref[...]).astype(BF16)
        white[g] = dot(centered, whitener_ref[...]).astype(BF16)

    places = lax.broadcasted_iota(jnp.int32, (rows, rows), 0).astype(F32)

    @pl.loop(0, groups)
    def _(g):
        own = white[g]
        table = blocks_ref[g, rows:, :].astype(F32)
        loss = jnp.zeros((1, rows), F32)
        grad = jnp.zeros((rows, embed), F32)
        for k in range(PARTNERS):
            other = white[(g + offsets_ref[g, k]) % groups]
            logits = dot(other, own, (1, 1)) * LOGIT_SCALE
            peak = jnp.max(logits, axis=0, keepdims=True)
            powers = jnp.exp(logits - peak)
            sums = jnp.sum(powers, axis=0, keepdims=True)
            hit = places == table[0:1, k * rows : (k + 1) * rows]
            picked = jnp.sum(jnp.where(hit, logits, 0.0), axis=0, keepdims=True)
            loss = loss + (peak + jnp.log(sums) - picked)
            weights = (powers * (1.0 / sums) - hit.astype(F32)) * (1.0 / PARTNERS)
            grad = grad + dot(weights.astype(BF16), other, (0, 0))
        grad_ref[g] = (grad * LOGIT_SCALE).astype(BF16)

        @pl.when(g == group)
        def _():
            loss_ref[...] = loss * (1.0 / PARTNERS)


def contrast(group, offsets, blocks, mean, whitener):
    groups, rows, embed = blocks.shape
    rows -= TAIL
    return pl.pallas_call(
        contrast_kernel,
        in_specs=[smem(), smem()] + [vmem()] * 3,
        out_specs=[vmem()] * 2,
        out_shape=[
            jax.ShapeDtypeStruct((1, rows), F32),
            jax.ShapeDtypeStruct((groups, rows, embed), BF16),
        ],
        scratch_shapes=[pltpu.VMEM((groups, rows, embed), BF16)],
        compiler_params=params(12 + 6 * groups * rows * embed // 2**20),
        cost_estimate=pl.CostEstimate(
            flops=groups * rows * 2 * embed * (embed + 2 * PARTNERS * rows),
            bytes_accessed=4 * groups * rows * embed,
            transcendentals=groups * PARTNERS * rows * rows,
        ),
        name="contrast",
    )(group, offsets, blocks, mean, whitener)


def gather_kernel(window_ref, grad_ref, features_ref, *refs):
    groups = grad_ref.shape[0]
    outs, total = refs[:-1], refs[-1]
    share = outs[0].shape[0]
    window = window_ref[0]

    def columns(at):
        value = dot(features_ref[0, :, at], grad_ref[0], (0, 0))
        for k in range(1, groups):
            value = value + dot(features_ref[k, :, at], grad_ref[k], (0, 0))
        return value

    if share % LANES:
        total[...] = columns(slice(None))
    for r, out in enumerate(outs):
        at = pl.ds(pl.multiple_of((window ^ r) * share, share), share)
        value = total[at, :] if share % LANES else columns(at)
        out[...] = value.astype(out.dtype)


def weight_pieces(window, grad, feature_slices, shares):
    groups, rows, embed = grad.shape
    columns = feature_slices.shape[2]
    share = columns // shares
    return pl.pallas_call(
        gather_kernel,
        in_specs=[smem()] + [vmem()] * 2,
        out_specs=[vmem()] * shares,
        out_shape=[
            jax.ShapeDtypeStruct((share, embed), BF16 if r else F32) for r in range(shares)
        ],
        scratch_shapes=[pltpu.VMEM((columns if share % LANES else 8, embed), F32)],
        compiler_params=params(24),
        cost_estimate=pl.CostEstimate(
            flops=groups * rows * 2 * embed * columns,
            bytes_accessed=2 * groups * rows * (embed + columns),
            transcendentals=0,
        ),
        name="weight_pieces",
    )(window, grad, feature_slices)


def finish_kernel(*refs):
    keep_ref, whitener_ref, out_ref = refs[0], refs[-2], refs[-1]
    value = keep_ref[...]
    for ref in refs[1:-2]:
        value = value + ref[...].astype(F32)
    high, low = split(value)
    out_ref[...] = dot(high, whitener_ref[...], (1, 1)) + dot(low, whitener_ref[...], (1, 1))


def finish(pieces, whitener):
    return pl.pallas_call(
        finish_kernel,
        in_specs=[vmem()] * (len(pieces) + 1),
        out_specs=vmem(),
        out_shape=jax.ShapeDtypeStruct(pieces[0].shape, F32),
        compiler_params=params(12),
        name="finish",
    )(*pieces, whitener)


def shards(features, proj_weight, partner_offsets, ortholog_index):
    rows, depth = features.shape
    embed = proj_weight.shape[1]
    groups = lax.axis_size("sp")
    shares = lax.axis_size("win")
    devices = groups * shares
    group = lax.axis_index("sp").astype(jnp.int32)
    window = lax.axis_index("win").astype(jnp.int32)
    me = group * shares + window

    block, slices, send, keep = project(
        me.reshape(1), partner_offsets, features, proj_weight, ortholog_index.T, groups
    )
    blocks = lax.all_gather(block, "sp")

    arrived = [xor_permute(send, 1)]
    sent = send
    seen = 1
    stages = []
    low = 1
    place = me & 1
    while keep.shape[0] > 32:
        count = 4
        own = (me >> low) & (count - 1)
        keep, sends, seen = stage(own, keep, sent, arrived, seen, count, embed)
        arrived = [xor_permute(piece, (r + 1) << low) for r, piece in enumerate(sends)]
        sent = sends[0]
        stages.append((low, count))
        place = place * count + own
        low += 2
    size = keep.shape[0]
    part = keep
    for piece in arrived:
        part = part + piece[:size].astype(F32)
    sums = jnp.stack([sent[size:]] + [piece[size:] for piece in arrived])
    extra = devices >> low
    if extra > 1:
        mine = jnp.concatenate([part.astype(BF16), sums.reshape(-1, sums.shape[2])])
        others = [xor_permute(mine, r << low) for r in range(1, extra)]
        for piece in others:
            part = part + piece[:size].astype(F32)
        sums = jnp.concatenate([sums] + [piece[size:].reshape(sums.shape) for piece in others])
    part = part.astype(BF16)
    for low, count in reversed(stages):
        part = jnp.concatenate(
            [part] + [xor_permute(part, r << low) for r in range(1, count)], axis=0
        )
    part = part.reshape(-1, size, part.shape[1])
    other = xor_permute(part, 1)

    other, slices = lax.optimization_barrier((other, slices))
    slices = lax.all_to_all(slices, "sp", 0, 0)

    whitener, mean = whiten(place.reshape(1), sums, part, other, rows, embed)
    offsets = blocks[:, rows + 1, :PARTNERS].astype(jnp.int32)
    loss, grad = contrast(group.reshape(1), offsets, blocks, mean, whitener)
    pieces = weight_pieces(window.reshape(1), grad, slices, shares)
    pieces = [pieces[0]] + [xor_permute(pieces[r], r) for r in range(1, shares)]
    return loss[0], finish(pieces, whitener)


def solution(mesh):
    return jax.shard_map(
        shards,
        mesh=mesh,
        in_specs=(P(("sp", "win"), None), P(), P("sp", None), P(("sp", "win"), None)),
        out_specs=(P(("sp", "win")), P(("sp", "win"), None)),
        check_vma=False,
    )
```

```python
import jax
import jax.numpy as jnp
from jax import lax
from jax.experimental import pallas as pl
from jax.experimental.pallas import tpu as pltpu
from jax.sharding import PartitionSpec as P

PARTNERS = 4
LOGIT_SCALE = 0.125
AXES = ("sp", "win")
LANES = 128
TAIL = 16
STREAMS = 4
F32 = jnp.float32
BF16 = jnp.bfloat16
HIGHEST = lax.Precision.HIGHEST


def dot(a, b, contract=(1, 0), precision=None):
    return lax.dot_general(
        a,
        b,
        (((contract[0],), (contract[1],)), ((), ())),
        precision=precision,
        preferred_element_type=F32,
    )


def params(mebibytes, semantics=None):
    return pltpu.CompilerParams(
        vmem_limit_bytes=mebibytes * 2**20, dimension_semantics=semantics
    )


def vmem():
    return pl.BlockSpec(memory_space=pltpu.VMEM)


def smem():
    return pl.BlockSpec(memory_space=pltpu.SMEM)


def xor_permute(piece, mask):
    devices = lax.axis_size(AXES)
    return lax.ppermute(piece, AXES, [(i, i ^ mask) for i in range(devices)])


def split(value):
    high = value.astype(BF16)
    return high, (value - high.astype(F32)).astype(BF16)


def pack_sums(sums, packed, rows):
    high = sums.astype(BF16).astype(F32)
    pad = jnp.zeros((sums.shape[0], 2 * packed - sums.shape[1]), F32)
    lines = []
    for half in (high, sums - high):
        lines += [half[:, :packed], jnp.concatenate([half[:, packed:], pad], axis=1)]
    if rows > 4 * sums.shape[0]:
        lines.append(jnp.zeros((rows - 4 * sums.shape[0], packed), F32))
    return jnp.concatenate(lines, axis=0).astype(BF16)


def unpack_sums(block, count, embed):
    wide = block.astype(F32)
    packed = wide.shape[1]
    low = 2 * count
    left = wide[0:count] + wide[low : low + count]
    right = wide[count:low] + wide[low + count : low + 2 * count]
    return jnp.concatenate([left, right[:, : embed - packed]], axis=1)


def project_kernel(
    me_ref,
    offsets_ref,
    features_ref,
    ortholog_ref,
    *refs,
):
    weight_refs = refs[:STREAMS]
    block_ref, send_ref, keep_ref, acc, wide = refs[STREAMS:]
    step = pl.program_id(0)
    rows, embed = acc.shape
    half, packed = keep_ref.shape
    blocks = embed // LANES

    @pl.when(step == 0)
    def _():
        acc[...] = jnp.zeros_like(acc)

    part = features_ref.shape[1] // STREAMS
    value = acc[...]
    for k, weight_ref in enumerate(weight_refs):
        value += dot(features_ref[:, k * part : (k + 1) * part], weight_ref[...])
    acc[...] = value

    @pl.when(step == pl.num_programs(0) - 1)
    def _():
        projected = acc[...].astype(BF16)
        block_ref[0:rows, :] = projected
        line = lax.broadcasted_iota(jnp.int32, (TAIL, embed), 0)
        lane = lax.broadcasted_iota(jnp.int32, (TAIL, embed), 1)
        table = jnp.zeros((TAIL, embed), F32)
        for k in range(PARTNERS):
            table = jnp.where((line == 1) & (lane == k), offsets_ref[0, k].astype(F32), table)
        hits = jnp.concatenate(
            [ortholog_ref[k : k + 1, :].astype(F32) for k in range(PARTNERS)]
            + ([jnp.zeros((1, embed - PARTNERS * rows), F32)] if embed > PARTNERS * rows else []),
            axis=1,
        )
        block_ref[rows:, :] = jnp.where(line == 0, hits, table).astype(BF16)

        total = jnp.sum(projected.astype(F32), axis=0, keepdims=True)
        send_ref[half:, :] = pack_sums(total, packed, TAIL)
        wide[:, :embed] = projected
        wide[:, embed:] = projected[:, : packed - LANES]
        ones = jnp.ones((rows, LANES), BF16)
        acc[0:8, :] = jnp.broadcast_to(total * (1.0 / rows), (8, embed))
        core = me_ref[0] & 1
        for side, out in ((0, keep_ref), (1, send_ref)):
            for r in range(blocks // 2):
                block = (core ^ side) * (blocks // 2) + r
                start = pl.multiple_of(block * LANES, LANES)
                own = wide[:, pl.ds(start, LANES)]
                gram = dot(own, wide[:, pl.ds(start, packed)], (0, 0))
                sums = dot(own, ones, (0, 0))
                for k in range(packed // LANES):
                    other = pl.multiple_of((block + k) % blocks * LANES, LANES)
                    at = slice(k * LANES, (k + 1) * LANES)
                    value = gram[:, at] - sums * acc[0:1, pl.ds(other, LANES)]
                    out[r * LANES : (r + 1) * LANES, at] = value.astype(out.dtype)


def project(me, offsets, features, weight, ortholog):
    rows, depth = features.shape
    embed = weight.shape[1]
    packed = embed // 2 + LANES
    steps = 4
    tile = depth // steps
    fixed = lambda k, *_: (0, 0)
    streams = [
        pl.BlockSpec((tile // STREAMS, embed), lambda k, *_, j=j: (STREAMS * k + j, 0))
        for j in range(STREAMS)
    ]
    return pl.pallas_call(
        project_kernel,
        grid_spec=pltpu.PrefetchScalarGridSpec(
            num_scalar_prefetch=2,
            grid=(steps,),
            in_specs=[
                pl.BlockSpec((rows, tile), lambda k, *_: (0, k)),
                pl.BlockSpec((PARTNERS, rows), fixed),
            ]
            + streams,
            out_specs=[
                pl.BlockSpec((rows + TAIL, embed), fixed),
                pl.BlockSpec((embed // 2 + TAIL, packed), fixed),
                pl.BlockSpec((embed // 2, packed), fixed),
            ],
            scratch_shapes=[
                pltpu.VMEM((rows, embed), F32),
                pltpu.VMEM((rows, embed + packed - LANES), BF16),
            ],
        ),
        out_shape=[
            jax.ShapeDtypeStruct((rows + TAIL, embed), BF16),
            jax.ShapeDtypeStruct((embed // 2 + TAIL, packed), BF16),
            jax.ShapeDtypeStruct((embed // 2, packed), F32),
        ],
        compiler_params=params(48, ("arbitrary",)),
        cost_estimate=pl.CostEstimate(
            flops=2 * rows * depth * embed, bytes_accessed=2 * depth * embed, transcendentals=0
        ),
        name="project",
    )(me, offsets, features, ortholog, *([weight] * STREAMS))


def make_stage_kernel(seen, arrivals, count, embed):
    def kernel(own_ref, keep_ref, sent_ref, *refs):
        arrived, next_keep, outs = refs[:arrivals], refs[arrivals], refs[arrivals + 1 :]
        full, packed = keep_ref.shape
        share = full // count
        own = own_ref[0]
        sums = [unpack_sums(ref[full:, :], seen, embed) for ref in (sent_ref, *arrived)]
        block = pack_sums(jnp.concatenate(sums, axis=0), packed, outs[0].shape[0] - share)
        for r in range(count):
            at = pl.ds(pl.multiple_of((own ^ r) * share, share), share)
            value = keep_ref[at, :]
            for ref in arrived:
                value = value + ref[at, :].astype(F32)
            if r == 0:
                next_keep[...] = value
            else:
                outs[r - 1][:share, :] = value.astype(BF16)
                outs[r - 1][share:, :] = block

    return kernel


def stage(own, keep, sent, arrived, seen, count, embed):
    full, packed = keep.shape
    share = full // count
    held = seen * (1 + len(arrived))
    tail = -(-4 * held // TAIL) * TAIL
    out = pl.pallas_call(
        make_stage_kernel(seen, len(arrived), count, embed),
        in_specs=[smem()] + [vmem()] * (2 + len(arrived)),
        out_specs=[vmem()] * count,
        out_shape=[jax.ShapeDtypeStruct((share, packed), F32)]
        + [jax.ShapeDtypeStruct((share + tail, packed), BF16)] * (count - 1),
        compiler_params=params(16),
        cost_estimate=pl.CostEstimate(
            flops=full * packed, bytes_accessed=4 * full * packed, transcendentals=0
        ),
        name="stage",
    )(own.reshape(1), keep, sent, *arrived)
    return out[0], out[1:], held


def make_whiten_kernel(rows):
    def kernel(
        place_ref,
        sums_ref,
        near_ref,
        far_ref,
        whitener_ref,
        mean_ref,
        scaled,
        rest,
        first,
        left,
        right,
    ):
        place = place_ref[0]
        embed = scaled.shape[0]
        blocks = embed // LANES
        half = blocks // 2
        pieces, depth = near_ref.shape[:2]
        per_block = LANES // depth
        count = sums_ref.shape[1] // 4
        totals = jnp.concatenate(
            [unpack_sums(sums_ref[k], count, embed) for k in range(sums_ref.shape[0])], axis=0
        )
        total_rows = rows * totals.shape[0]
        tile = 512
        tiles = embed // tile

        mean = jnp.sum(totals, axis=0, keepdims=True) * (1.0 / total_rows)
        mean_ref[...] = mean
        shift_high, shift_low = split(totals * (1.0 / rows) - mean)
        shift_left = jnp.concatenate([shift_high, shift_high, shift_low], axis=0)
        shift_right = jnp.concatenate([shift_high, shift_low, shift_high], axis=0)

        def unpack(source_ref, side):
            for i in range(side * half, (side + 1) * half):
                for part in range(per_block):
                    piece = ((i - side * half) * per_block + part) ^ (place & (pieces - 1))
                    wide = source_ref[piece].astype(F32)
                    lines = pl.ds(i * LANES + part * depth, depth)
                    for k in range(half + 1):
                        if k == half and side:
                            continue
                        j = (i + k) % blocks
                        scaled[lines, j * LANES : (j + 1) * LANES] = wide[
                            :, k * LANES : (k + 1) * LANES
                        ]

        for core in range(2):

            @pl.when(place // pieces == core)
            def _():
                unpack(near_ref, core)
                unpack(far_ref, 1 - core)

        for i in range(blocks):
            for k in range(1, half + 1):
                if k == half and i >= half:
                    continue
                j = (i + k) % blocks
                scaled[j * LANES : (j + 1) * LANES, i * LANES : (i + 1) * LANES] = scaled[
                    i * LANES : (i + 1) * LANES, j * LANES : (j + 1) * LANES
                ].T
        squares = jnp.zeros((1, embed), F32)
        for t in range(tiles):
            lines = slice(t * tile, (t + 1) * tile)
            between = dot(shift_left[:, lines], shift_right, (0, 0))
            covariance = (scaled[lines, :] + rows * between) * (1.0 / total_rows)
            scaled[lines, :] = covariance
            first[lines, :] = covariance.astype(BF16)
            squares = squares + jnp.sum(covariance * covariance, axis=0, keepdims=True)
        frobenius = jnp.sqrt(jnp.sum(squares, axis=1, keepdims=True))
        inverse = 1.0 / frobenius
        root = lax.rsqrt(frobenius)

        def product(one, two, finish):
            @pl.loop(0, tiles)
            def _(t):
                lines = pl.ds(pl.multiple_of(t * tile, tile), tile)
                finish(lines, dot(one[lines, :], two[...]))

        def second(lines, value):
            value = value * (inverse * inverse)
            own = scaled[lines, :] * inverse
            scaled[lines, :] = own
            rest[lines, :] = 27.0 * value - 39.0 * own
            left[lines, :] = value.astype(BF16)
            right[lines, :] = (value - 9.0 * own).astype(BF16)

        product(first, first, second)

        def fourth(lines, value):
            value = (value + rest[lines, :]) * (1.0 / 16.0)
            rest[lines, :] = value
            whitener_ref[lines, :] = value.astype(BF16)

        product(left, right, fourth)

        def moved(lines, value):
            value = value * inverse
            scaled[lines, :] = 2.25 * 2.25 * scaled[lines, :] + 4.5 * value
            right[lines, :] = value.astype(BF16)

        product(first, whitener_ref, moved)

        def quad(lines, value):
            value = value + scaled[lines, :]
            rest[lines, :] = 3.0 * rest[lines, :] - 2.25 * value
            left[lines, :] = value.astype(BF16)

        product(whitener_ref, right, quad)
        first[...] = whitener_ref[...]

        def last(lines, value):
            at = lax.broadcasted_iota(jnp.int32, value.shape, 0) + lines.start
            eye = at == lax.broadcasted_iota(jnp.int32, value.shape, 1)
            value = 0.5 * (rest[lines, :] - value)
            value = value + jnp.where(eye, 0.5 * 3.0 * 2.25, 0.0)
            whitener_ref[lines, :] = (value * root).astype(BF16)

        product(first, left, last)

    return kernel


def whiten(place, sums, near, far, rows, embed):
    square = (embed, embed)
    return pl.pallas_call(
        make_whiten_kernel(rows),
        in_specs=[smem()] + [vmem()] * 3,
        out_specs=[vmem(), vmem()],
        out_shape=[
            jax.ShapeDtypeStruct(square, BF16),
            jax.ShapeDtypeStruct((1, embed), F32),
        ],
        scratch_shapes=[pltpu.VMEM(square, F32)] * 2 + [pltpu.VMEM(square, BF16)] * 3,
        compiler_params=params(32),
        cost_estimate=pl.CostEstimate(
            flops=5 * 2 * embed**3, bytes_accessed=2 * embed**2, transcendentals=0
        ),
        name="whiten",
    )(place, sums, near, far)


def contrast_kernel(
    group_ref, offsets_ref, blocks_ref, mean_ref, whitener_ref, loss_ref, grad_ref, white, others
):
    groups, rows, embed = white.shape
    group = group_ref[0]

    @pl.loop(0, groups // 2)
    def _(pair):
        centered = [
            (blocks_ref[2 * pair + side, 0:rows, :].astype(F32) - mean_ref[...]).astype(BF16)
            for side in range(2)
        ]
        value = dot(jnp.concatenate(centered, axis=0), whitener_ref[...]).astype(BF16)
        for side in range(2):
            white[2 * pair + side] = value[side * rows : (side + 1) * rows]

    places = lax.broadcasted_iota(jnp.int32, (rows, rows), 0).astype(F32)

    @pl.loop(0, groups)
    def _(g):
        table = blocks_ref[g, rows:, :].astype(F32)
        for k in range(PARTNERS):
            others[k * rows : (k + 1) * rows, :] = white[(g + offsets_ref[g, k]) % groups]
        logits = dot(others[...], white[g], (1, 1)) * LOGIT_SCALE
        loss = jnp.zeros((1, rows), F32)
        weights = []
        for k in range(PARTNERS):
            own = logits[k * rows : (k + 1) * rows]
            peak = jnp.max(own, axis=0, keepdims=True)
            powers = jnp.exp(own - peak)
            sums = jnp.sum(powers, axis=0, keepdims=True)
            hit = places == table[0:1, k * rows : (k + 1) * rows]
            picked = jnp.sum(jnp.where(hit, own, 0.0), axis=0, keepdims=True)
            loss = loss + (peak + jnp.log(sums) - picked)
            share = powers * (1.0 / (PARTNERS * sums))
            weights.append(jnp.where(hit, share - 1.0 / PARTNERS, share).astype(BF16))
        grad = dot(jnp.concatenate(weights, axis=0), others[...], (0, 0))
        grad_ref[g] = (grad * LOGIT_SCALE).astype(BF16)

        @pl.when(g == group)
        def _():
            loss_ref[...] = loss * (1.0 / PARTNERS)


def contrast(group, offsets, blocks, mean, whitener):
    groups, rows, embed = blocks.shape
    rows -= TAIL
    return pl.pallas_call(
        contrast_kernel,
        in_specs=[smem(), smem()] + [vmem()] * 3,
        out_specs=[vmem()] * 2,
        out_shape=[
            jax.ShapeDtypeStruct((1, rows), F32),
            jax.ShapeDtypeStruct((groups, rows, embed), BF16),
        ],
        scratch_shapes=[
            pltpu.VMEM((groups, rows, embed), BF16),
            pltpu.VMEM((PARTNERS * rows, embed), BF16),
        ],
        compiler_params=params(20 + 6 * groups * rows * embed // 2**20),
        cost_estimate=pl.CostEstimate(
            flops=groups * rows * 2 * embed * (embed + 2 * PARTNERS * rows),
            bytes_accessed=4 * groups * rows * embed,
            transcendentals=groups * PARTNERS * rows * rows,
        ),
        name="contrast",
    )(group, offsets, blocks, mean, whitener)


def gather_kernel(window_ref, grad_ref, features_ref, *refs):
    groups = grad_ref.shape[0]
    outs, total = refs[:-1], refs[-1]
    share = outs[0].shape[0]
    window = window_ref[0]

    def columns(at):
        value = dot(features_ref[0, :, at], grad_ref[0], (0, 0))
        for k in range(1, groups):
            value = value + dot(features_ref[k, :, at], grad_ref[k], (0, 0))
        return value

    if share % LANES:
        total[...] = columns(slice(None))
    for r, out in enumerate(outs):
        at = pl.ds(pl.multiple_of((window ^ r) * share, share), share)
        value = total[at, :] if share % LANES else columns(at)
        out[...] = value.astype(out.dtype)


def weight_pieces(window, grad, feature_slices, shares):
    groups, rows, embed = grad.shape
    columns = feature_slices.shape[2]
    share = columns // shares
    return pl.pallas_call(
        gather_kernel,
        in_specs=[smem()] + [vmem()] * 2,
        out_specs=[vmem()] * shares,
        out_shape=[
            jax.ShapeDtypeStruct((share, embed), BF16 if r else F32) for r in range(shares)
        ],
        scratch_shapes=[pltpu.VMEM((columns if share % LANES else 8, embed), F32)],
        compiler_params=params(24),
        cost_estimate=pl.CostEstimate(
            flops=groups * rows * 2 * embed * columns,
            bytes_accessed=2 * groups * rows * (embed + columns),
            transcendentals=0,
        ),
        name="weight_pieces",
    )(window, grad, feature_slices)


def finish_kernel(*refs):
    keep_ref, whitener_ref, out_ref = refs[0], refs[-2], refs[-1]
    value = keep_ref[...]
    for ref in refs[1:-2]:
        value = value + ref[...].astype(F32)
    high, low = split(value)
    out_ref[...] = dot(high, whitener_ref[...], (1, 1)) + dot(low, whitener_ref[...], (1, 1))


def finish(pieces, whitener):
    return pl.pallas_call(
        finish_kernel,
        in_specs=[vmem()] * (len(pieces) + 1),
        out_specs=vmem(),
        out_shape=jax.ShapeDtypeStruct(pieces[0].shape, F32),
        compiler_params=params(12),
        name="finish",
    )(*pieces, whitener)


def shards(features, proj_weight, partner_offsets, ortholog_index):
    rows, depth = features.shape
    embed = proj_weight.shape[1]
    groups = lax.axis_size("sp")
    shares = lax.axis_size("win")
    devices = groups * shares
    group = lax.axis_index("sp").astype(jnp.int32)
    window = lax.axis_index("win").astype(jnp.int32)
    me = group * shares + window

    slices = features.reshape(rows, groups, depth // groups).transpose(1, 0, 2)
    slices, me_scalar = lax.optimization_barrier((slices, me.reshape(1)))
    slices = lax.all_to_all(slices, "sp", 0, 0)

    block, send, keep = project(
        me_scalar, partner_offsets, features, proj_weight, ortholog_index.T
    )
    blocks = lax.all_gather(block, "sp")

    arrived = [xor_permute(send, 1)]
    sent = send
    seen = 1
    stages = []
    low = 1
    place = me & 1
    while keep.shape[0] > 32:
        count = 4
        own = (me >> low) & (count - 1)
        keep, sends, seen = stage(own, keep, sent, arrived, seen, count, embed)
        arrived = [xor_permute(piece, (r + 1) << low) for r, piece in enumerate(sends)]
        sent = sends[0]
        stages.append((low, count))
        place = place * count + own
        low += 2
    size = keep.shape[0]
    part = keep
    for piece in arrived:
        part = part + piece[:size].astype(F32)
    sums = jnp.stack([sent[size:]] + [piece[size:] for piece in arrived])
    extra = devices >> low
    if extra > 1:
        mine = jnp.concatenate([part.astype(BF16), sums.reshape(-1, sums.shape[2])])
        others = [xor_permute(mine, r << low) for r in range(1, extra)]
        for piece in others:
            part = part + piece[:size].astype(F32)
        sums = jnp.concatenate([sums] + [piece[size:].reshape(sums.shape) for piece in others])
    part = part.astype(BF16)
    for low, count in reversed(stages):
        part = jnp.concatenate(
            [part] + [xor_permute(part, r << low) for r in range(1, count)], axis=0
        )
    part = part.reshape(-1, size, part.shape[1])
    other = xor_permute(part, 1)

    other, slices = lax.optimization_barrier((other, slices))
    whitener, mean = whiten(place.reshape(1), sums, part, other, rows, embed)
    offsets = blocks[:, rows + 1, :PARTNERS].astype(jnp.int32)
    loss, grad = contrast(group.reshape(1), offsets, blocks, mean, whitener)
    pieces = weight_pieces(window.reshape(1), grad, slices, shares)
    pieces = [pieces[0]] + [xor_permute(pieces[r], r) for r in range(1, shares)]
    return loss[0], finish(pieces, whitener)


def solution(mesh):
    return jax.shard_map(
        shards,
        mesh=mesh,
        in_specs=(P(("sp", "win"), None), P(), P("sp", None), P(("sp", "win"), None)),
        out_specs=(P(("sp", "win")), P(("sp", "win"), None)),
        check_vma=False,
    )
```

```python
import functools

import jax
import jax.numpy as jnp
from jax import lax
from jax.experimental import pallas as pl
from jax.experimental.pallas import tpu as pltpu
from jax.sharding import PartitionSpec as P

PARTNERS = 4
LOGIT_SCALE = 0.125
AXES = ("sp", "win")
LANES = 128
TAIL = 16
SHARED = 4
STREAMS = 4
F32 = jnp.float32
BF16 = jnp.bfloat16
HIGHEST = lax.Precision.HIGHEST


def dot(a, b, contract=(1, 0), precision=None):
    return lax.dot_general(
        a,
        b,
        (((contract[0],), (contract[1],)), ((), ())),
        precision=precision,
        preferred_element_type=F32,
    )


def params(mebibytes, semantics=None):
    return pltpu.CompilerParams(
        vmem_limit_bytes=mebibytes * 2**20, dimension_semantics=semantics
    )


def vmem():
    return pl.BlockSpec(memory_space=pltpu.VMEM)


def smem():
    return pl.BlockSpec(memory_space=pltpu.SMEM)


def xor_permute(piece, mask):
    devices = lax.axis_size(AXES)
    return lax.ppermute(piece, AXES, [(i, i ^ mask) for i in range(devices)])


def split(value):
    high = value.astype(BF16)
    return high, (value - high.astype(F32)).astype(BF16)


def pack_sums(sums, packed, rows):
    high = sums.astype(BF16).astype(F32)
    pad = jnp.zeros((sums.shape[0], 2 * packed - sums.shape[1]), F32)
    lines = []
    for half in (high, sums - high):
        lines += [half[:, :packed], jnp.concatenate([half[:, packed:], pad], axis=1)]
    if rows > 4 * sums.shape[0]:
        lines.append(jnp.zeros((rows - 4 * sums.shape[0], packed), F32))
    return jnp.concatenate(lines, axis=0).astype(BF16)


def unpack_sums(block, count, embed):
    wide = block.astype(F32)
    packed = wide.shape[1]
    low = 2 * count
    left = wide[0:count] + wide[low : low + count]
    right = wide[count:low] + wide[low + count : low + 2 * count]
    return jnp.concatenate([left, right[:, : embed - packed]], axis=1)


def project_kernel(
    chunk,
    me_ref,
    offsets_ref,
    features_ref,
    ortholog_ref,
    *refs,
):
    weight_refs = refs[:STREAMS]
    block_ref, send_ref, keep_ref = refs[STREAMS : STREAMS + 3]
    slice_refs = refs[STREAMS + 3 : -2]
    acc, wide = refs[-2:]
    step = pl.program_id(0)
    rows, embed = acc.shape
    half, packed = keep_ref.shape
    blocks = embed // LANES

    @pl.when(step == 0)
    def _():
        acc[...] = jnp.zeros_like(acc)

    tile = features_ref.shape[1]
    chunks = tile // chunk
    for number in range(chunks):
        target = step * chunks + number
        at = pl.ds(pl.multiple_of(target // SHARED * chunk, chunk), chunk)
        for k, slice_ref in enumerate(slice_refs):

            @pl.when((target ^ me_ref[1]) % SHARED == k)
            def _():
                slice_ref[:, at] = features_ref[:, number * chunk : (number + 1) * chunk]

    part = features_ref.shape[1] // STREAMS
    value = acc[...]
    for k, weight_ref in enumerate(weight_refs):
        value += dot(features_ref[:, k * part : (k + 1) * part], weight_ref[...])
    acc[...] = value

    @pl.when(step == pl.num_programs(0) - 1)
    def _():
        projected = acc[...].astype(BF16)
        block_ref[0:rows, :] = projected
        line = lax.broadcasted_iota(jnp.int32, (TAIL, embed), 0)
        lane = lax.broadcasted_iota(jnp.int32, (TAIL, embed), 1)
        table = jnp.zeros((TAIL, embed), F32)
        for k in range(PARTNERS):
            table = jnp.where((line == 1) & (lane == k), offsets_ref[0, k].astype(F32), table)
        hits = jnp.concatenate(
            [ortholog_ref[k : k + 1, :].astype(F32) for k in range(PARTNERS)]
            + ([jnp.zeros((1, embed - PARTNERS * rows), F32)] if embed > PARTNERS * rows else []),
            axis=1,
        )
        block_ref[rows:, :] = jnp.where(line == 0, hits, table).astype(BF16)

        total = jnp.sum(projected.astype(F32), axis=0, keepdims=True)
        send_ref[half:, :] = pack_sums(total, packed, TAIL)
        wide[:, :embed] = projected
        wide[:, embed:] = projected[:, : packed - LANES]
        ones = jnp.ones((rows, LANES), BF16)
        acc[0:8, :] = jnp.broadcast_to(total * (1.0 / rows), (8, embed))
        core = me_ref[0] & 1
        for side, out in ((0, keep_ref), (1, send_ref)):
            for r in range(blocks // 2):
                block = (core ^ side) * (blocks // 2) + r
                start = pl.multiple_of(block * LANES, LANES)
                own = wide[:, pl.ds(start, LANES)]
                gram = dot(own, wide[:, pl.ds(start, packed)], (0, 0))
                sums = dot(own, ones, (0, 0))
                for k in range(packed // LANES):
                    other = pl.multiple_of((block + k) % blocks * LANES, LANES)
                    at = slice(k * LANES, (k + 1) * LANES)
                    value = gram[:, at] - sums * acc[0:1, pl.ds(other, LANES)]
                    out[r * LANES : (r + 1) * LANES, at] = value.astype(out.dtype)


def project(me, offsets, features, weight, ortholog, groups):
    rows, depth = features.shape
    embed = weight.shape[1]
    packed = embed // 2 + LANES
    steps = 4
    tile = depth // steps
    fixed = lambda k, *_: (0, 0)
    streams = [
        pl.BlockSpec((tile // STREAMS, embed), lambda k, *_, j=j: (STREAMS * k + j, 0))
        for j in range(STREAMS)
    ]
    return pl.pallas_call(
        functools.partial(project_kernel, depth // groups),
        grid_spec=pltpu.PrefetchScalarGridSpec(
            num_scalar_prefetch=2,
            grid=(steps,),
            in_specs=[
                pl.BlockSpec((rows, tile), lambda k, *_: (0, k)),
                pl.BlockSpec((PARTNERS, rows), fixed),
            ]
            + streams,
            out_specs=[
                pl.BlockSpec((rows + TAIL, embed), fixed),
                pl.BlockSpec((embed // 2 + TAIL, packed), fixed),
                pl.BlockSpec((embed // 2, packed), fixed),
            ]
            + [pl.BlockSpec((rows, depth // SHARED), fixed)] * SHARED,
            scratch_shapes=[
                pltpu.VMEM((rows, embed), F32),
                pltpu.VMEM((rows, embed + packed - LANES), BF16),
            ],
        ),
        out_shape=[
            jax.ShapeDtypeStruct((rows + TAIL, embed), BF16),
            jax.ShapeDtypeStruct((embed // 2 + TAIL, packed), BF16),
            jax.ShapeDtypeStruct((embed // 2, packed), F32),
        ]
        + [jax.ShapeDtypeStruct((rows, depth // SHARED), BF16)] * SHARED,
        compiler_params=params(24, ("arbitrary",)),
        cost_estimate=pl.CostEstimate(
            flops=2 * rows * depth * embed, bytes_accessed=2 * depth * embed, transcendentals=0
        ),
        name="project",
    )(me, offsets, features, ortholog, *([weight] * STREAMS))


def make_stage_kernel(seen, arrivals, count, embed):
    def kernel(own_ref, keep_ref, sent_ref, *refs):
        arrived, next_keep, outs = refs[:arrivals], refs[arrivals], refs[arrivals + 1 :]
        full, packed = keep_ref.shape
        share = full // count
        own = own_ref[0]
        sums = [unpack_sums(ref[full:, :], seen, embed) for ref in (sent_ref, *arrived)]
        block = pack_sums(jnp.concatenate(sums, axis=0), packed, outs[0].shape[0] - share)
        for r in range(count):
            at = pl.ds(pl.multiple_of((own ^ r) * share, share), share)
            value = keep_ref[at, :]
            for ref in arrived:
                value = value + ref[at, :].astype(F32)
            if r == 0:
                next_keep[...] = value
            else:
                outs[r - 1][:share, :] = value.astype(BF16)
                outs[r - 1][share:, :] = block

    return kernel


def stage(own, keep, sent, arrived, seen, count, embed):
    full, packed = keep.shape
    share = full // count
    held = seen * (1 + len(arrived))
    tail = -(-4 * held // TAIL) * TAIL
    out = pl.pallas_call(
        make_stage_kernel(seen, len(arrived), count, embed),
        in_specs=[smem()] + [vmem()] * (2 + len(arrived)),
        out_specs=[vmem()] * count,
        out_shape=[jax.ShapeDtypeStruct((share, packed), F32)]
        + [jax.ShapeDtypeStruct((share + tail, packed), BF16)] * (count - 1),
        compiler_params=params(16),
        cost_estimate=pl.CostEstimate(
            flops=full * packed, bytes_accessed=4 * full * packed, transcendentals=0
        ),
        name="stage",
    )(own.reshape(1), keep, sent, *arrived)
    return out[0], out[1:], held


def make_whiten_kernel(rows):
    def kernel(
        place_ref,
        sums_ref,
        near_ref,
        far_ref,
        whitener_ref,
        mean_ref,
        scaled,
        rest,
        first,
        left,
        right,
    ):
        place = place_ref[0]
        embed = scaled.shape[0]
        blocks = embed // LANES
        half = blocks // 2
        pieces, depth = near_ref.shape[:2]
        per_block = LANES // depth
        count = sums_ref.shape[1] // 4
        totals = jnp.concatenate(
            [unpack_sums(sums_ref[k], count, embed) for k in range(sums_ref.shape[0])], axis=0
        )
        total_rows = rows * totals.shape[0]
        tile = 512
        tiles = embed // tile

        mean = jnp.sum(totals, axis=0, keepdims=True) * (1.0 / total_rows)
        mean_ref[...] = mean
        shift_high, shift_low = split(totals * (1.0 / rows) - mean)
        shift_left = jnp.concatenate([shift_high, shift_high, shift_low], axis=0)
        shift_right = jnp.concatenate([shift_high, shift_low, shift_high], axis=0)

        def unpack(source_ref, side):
            for i in range(side * half, (side + 1) * half):
                for part in range(per_block):
                    piece = ((i - side * half) * per_block + part) ^ (place & (pieces - 1))
                    wide = source_ref[piece].astype(F32)
                    lines = pl.ds(i * LANES + part * depth, depth)
                    for k in range(half + 1):
                        if k == half and side:
                            continue
                        j = (i + k) % blocks
                        scaled[lines, j * LANES : (j + 1) * LANES] = wide[
                            :, k * LANES : (k + 1) * LANES
                        ]

        for core in range(2):

            @pl.when(place // pieces == core)
            def _():
                unpack(near_ref, core)
                unpack(far_ref, 1 - core)

        for i in range(blocks):
            for k in range(1, half + 1):
                if k == half and i >= half:
                    continue
                j = (i + k) % blocks
                scaled[j * LANES : (j + 1) * LANES, i * LANES : (i + 1) * LANES] = scaled[
                    i * LANES : (i + 1) * LANES, j * LANES : (j + 1) * LANES
                ].T
        squares = jnp.zeros((1, embed), F32)
        for t in range(tiles):
            lines = slice(t * tile, (t + 1) * tile)
            between = dot(shift_left[:, lines], shift_right, (0, 0))
            covariance = (scaled[lines, :] + rows * between) * (1.0 / total_rows)
            scaled[lines, :] = covariance
            first[lines, :] = covariance.astype(BF16)
            squares = squares + jnp.sum(covariance * covariance, axis=0, keepdims=True)
        frobenius = jnp.sqrt(jnp.sum(squares, axis=1, keepdims=True))
        inverse = 1.0 / frobenius
        root = lax.rsqrt(frobenius)

        def product(one, two, finish):
            @pl.loop(0, tiles)
            def _(t):
                lines = pl.ds(pl.multiple_of(t * tile, tile), tile)
                finish(lines, dot(one[lines, :], two[...]))

        def second(lines, value):
            value = value * (inverse * inverse)
            own = scaled[lines, :] * inverse
            scaled[lines, :] = own
            rest[lines, :] = 27.0 * value - 39.0 * own
            left[lines, :] = value.astype(BF16)
            right[lines, :] = (value - 9.0 * own).astype(BF16)

        product(first, first, second)

        def fourth(lines, value):
            value = (value + rest[lines, :]) * (1.0 / 16.0)
            rest[lines, :] = value
            whitener_ref[lines, :] = value.astype(BF16)

        product(left, right, fourth)

        def moved(lines, value):
            value = value * inverse
            scaled[lines, :] = 2.25 * 2.25 * scaled[lines, :] + 4.5 * value
            right[lines, :] = value.astype(BF16)

        product(first, whitener_ref, moved)

        def quad(lines, value):
            value = value + scaled[lines, :]
            rest[lines, :] = 3.0 * rest[lines, :] - 2.25 * value
            left[lines, :] = value.astype(BF16)

        product(whitener_ref, right, quad)
        first[...] = whitener_ref[...]

        def last(lines, value):
            at = lax.broadcasted_iota(jnp.int32, value.shape, 0) + lines.start
            eye = at == lax.broadcasted_iota(jnp.int32, value.shape, 1)
            value = 0.5 * (rest[lines, :] - value)
            value = value + jnp.where(eye, 0.5 * 3.0 * 2.25, 0.0)
            whitener_ref[lines, :] = (value * root).astype(BF16)

        product(first, left, last)

    return kernel


def whiten(place, sums, near, far, rows, embed):
    square = (embed, embed)
    return pl.pallas_call(
        make_whiten_kernel(rows),
        in_specs=[smem()] + [vmem()] * 3,
        out_specs=[vmem(), vmem()],
        out_shape=[
            jax.ShapeDtypeStruct(square, BF16),
            jax.ShapeDtypeStruct((1, embed), F32),
        ],
        scratch_shapes=[pltpu.VMEM(square, F32)] * 2 + [pltpu.VMEM(square, BF16)] * 3,
        compiler_params=params(32),
        cost_estimate=pl.CostEstimate(
            flops=5 * 2 * embed**3, bytes_accessed=2 * embed**2, transcendentals=0
        ),
        name="whiten",
    )(place, sums, near, far)


def contrast_kernel(
    group_ref, offsets_ref, blocks_ref, mean_ref, whitener_ref, loss_ref, grad_ref, white, others
):
    groups, rows, embed = white.shape
    group = group_ref[0]

    @pl.loop(0, groups // 2)
    def _(pair):
        centered = [
            (blocks_ref[2 * pair + side, 0:rows, :].astype(F32) - mean_ref[...]).astype(BF16)
            for side in range(2)
        ]
        value = dot(jnp.concatenate(centered, axis=0), whitener_ref[...]).astype(BF16)
        for side in range(2):
            white[2 * pair + side] = value[side * rows : (side + 1) * rows]

    places = lax.broadcasted_iota(jnp.int32, (rows, rows), 0).astype(F32)

    @pl.loop(0, SHARED)
    def _(step):
        g = step ^ group
        table = blocks_ref[g, rows:, :].astype(F32)
        for k in range(PARTNERS):
            others[k * rows : (k + 1) * rows, :] = white[(g + offsets_ref[g, k]) % groups]
        logits = dot(others[...], white[g], (1, 1)) * LOGIT_SCALE
        loss = jnp.zeros((1, rows), F32)
        weights = []
        for k in range(PARTNERS):
            own = logits[k * rows : (k + 1) * rows]
            peak = jnp.max(own, axis=0, keepdims=True)
            powers = jnp.exp(own - peak)
            sums = jnp.sum(powers, axis=0, keepdims=True)
            hit = places == table[0:1, k * rows : (k + 1) * rows]
            picked = jnp.sum(jnp.where(hit, own, 0.0), axis=0, keepdims=True)
            loss = loss + (peak + jnp.log(sums) - picked)
            share = powers * (1.0 / (PARTNERS * sums))
            weights.append(jnp.where(hit, share - 1.0 / PARTNERS, share).astype(BF16))
        grad = dot(jnp.concatenate(weights, axis=0), others[...], (0, 0))
        grad_ref[step] = (grad * LOGIT_SCALE).astype(BF16)

        @pl.when(step == 0)
        def _():
            loss_ref[...] = loss * (1.0 / PARTNERS)


def contrast(group, offsets, blocks, mean, whitener):
    groups, rows, embed = blocks.shape
    rows -= TAIL
    return pl.pallas_call(
        contrast_kernel,
        in_specs=[smem(), smem()] + [vmem()] * 3,
        out_specs=[vmem()] * 2,
        out_shape=[
            jax.ShapeDtypeStruct((1, rows), F32),
            jax.ShapeDtypeStruct((SHARED, rows, embed), BF16),
        ],
        scratch_shapes=[
            pltpu.VMEM((groups, rows, embed), BF16),
            pltpu.VMEM((PARTNERS * rows, embed), BF16),
        ],
        compiler_params=params(20 + 6 * groups * rows * embed // 2**20),
        cost_estimate=pl.CostEstimate(
            flops=rows * 2 * embed * (groups * embed + SHARED * 2 * PARTNERS * rows),
            bytes_accessed=4 * groups * rows * embed,
            transcendentals=SHARED * PARTNERS * rows * rows,
        ),
        name="contrast",
    )(group, offsets, blocks, mean, whitener)


def pieces_kernel(bits, shares, place_ref, grad_ref, *refs):
    feature_refs = refs[:SHARED]
    keep_ref, send_ref, total = refs[SHARED:]
    count = 1 << len(bits)
    share = 2 * keep_ref.shape[0] // count

    def columns(at):
        value = dot(feature_refs[0][:, at], grad_ref[0], (0, 0))
        for k in range(1, SHARED):
            value = value + dot(feature_refs[k][:, at], grad_ref[k], (0, 0))
        return value

    if share % LANES:
        total[...] = columns(slice(None))
    for t in reversed(range(count)):
        mask = sum(bit for s, bit in enumerate(bits) if t >> (len(bits) - 1 - s) & 1)
        at = pl.ds(pl.multiple_of((place_ref[0] ^ mask) * share, share), share)
        value = total[at, :] if share % LANES else columns(at)
        if t < count // 2:
            keep_ref[t * share : (t + 1) * share, :] = value
        else:
            line = t - count // 2
            send_ref[line * share : (line + 1) * share, :] = value.astype(BF16)


def weight_pieces(place, grad, slices, bits, shares):
    embed = grad.shape[2]
    rows, columns = slices[0].shape
    aligned = (columns >> len(bits)) % LANES == 0
    return pl.pallas_call(
        functools.partial(pieces_kernel, bits, shares),
        in_specs=[smem()] + [vmem()] * (1 + SHARED),
        out_specs=[vmem()] * 2,
        out_shape=[
            jax.ShapeDtypeStruct((columns // 2, embed), F32),
            jax.ShapeDtypeStruct((columns // 2, embed), BF16),
        ],
        scratch_shapes=[pltpu.VMEM((8 if aligned else columns, embed), F32)],
        compiler_params=params(24),
        cost_estimate=pl.CostEstimate(
            flops=SHARED * rows * 2 * embed * columns,
            bytes_accessed=2 * SHARED * rows * (embed + columns),
            transcendentals=0,
        ),
        name="weight_pieces",
    )(place, grad, *slices)


def halve_kernel(keep_ref, arrived_ref, next_ref, send_ref):
    half = next_ref.shape[0]
    next_ref[...] = keep_ref[:half, :] + arrived_ref[:half, :].astype(F32)
    send_ref[...] = (keep_ref[half:, :] + arrived_ref[half:, :].astype(F32)).astype(BF16)


def halve(keep, arrived):
    rows, embed = keep.shape
    return pl.pallas_call(
        halve_kernel,
        in_specs=[vmem()] * 2,
        out_specs=[vmem()] * 2,
        out_shape=[
            jax.ShapeDtypeStruct((rows // 2, embed), F32),
            jax.ShapeDtypeStruct((rows // 2, embed), BF16),
        ],
        compiler_params=params(16),
        name="halve",
    )(keep, arrived)


def finish_kernel(*refs):
    keep_ref, whitener_ref, out_ref = refs[0], refs[-2], refs[-1]
    value = keep_ref[...]
    for ref in refs[1:-2]:
        value = value + ref[...].astype(F32)
    high, low = split(value)
    out_ref[...] = dot(high, whitener_ref[...], (1, 1)) + dot(low, whitener_ref[...], (1, 1))


def finish(pieces, whitener):
    return pl.pallas_call(
        finish_kernel,
        in_specs=[vmem()] * (len(pieces) + 1),
        out_specs=vmem(),
        out_shape=jax.ShapeDtypeStruct(pieces[0].shape, F32),
        compiler_params=params(12),
        name="finish",
    )(*pieces, whitener)


def shards(features, proj_weight, partner_offsets, ortholog_index):
    rows, depth = features.shape
    embed = proj_weight.shape[1]
    groups = lax.axis_size("sp")
    shares = lax.axis_size("win")
    devices = groups * shares
    group = lax.axis_index("sp").astype(jnp.int32)
    window = lax.axis_index("win").astype(jnp.int32)
    me = group * shares + window

    block, send, keep, *slices = project(
        jnp.stack([me, group]), partner_offsets, features, proj_weight, ortholog_index.T, groups
    )
    blocks = lax.all_gather(block, "sp")

    arrived = [xor_permute(send, 1)]
    sent = send
    seen = 1
    stages = []
    low = 1
    place = me & 1
    while keep.shape[0] > 32:
        count = 4
        own = (me >> low) & (count - 1)
        keep, sends, seen = stage(own, keep, sent, arrived, seen, count, embed)
        arrived = [xor_permute(piece, (r + 1) << low) for r, piece in enumerate(sends)]
        sent = sends[0]
        stages.append((low, count))
        place = place * count + own
        low += 2
    size = keep.shape[0]
    part = keep
    for piece in arrived:
        part = part + piece[:size].astype(F32)
    sums = jnp.stack([sent[size:]] + [piece[size:] for piece in arrived])
    extra = devices >> low
    if extra > 1:
        mine = jnp.concatenate([part.astype(BF16), sums.reshape(-1, sums.shape[2])])
        others = [xor_permute(mine, r << low) for r in range(1, extra)]
        for piece in others:
            part = part + piece[:size].astype(F32)
        sums = jnp.concatenate([sums] + [piece[size:].reshape(sums.shape) for piece in others])
    part = part.astype(BF16)
    for number, (low, count) in enumerate(reversed(stages)):
        if number == len(stages) - 1:
            part, *slices = lax.optimization_barrier((part, *slices))
            for k in range(1, SHARED):
                slices[k] = xor_permute(slices[k], k * shares)
        part = jnp.concatenate(
            [part] + [xor_permute(part, r << low) for r in range(1, count)], axis=0
        )
    part = part.reshape(-1, size, part.shape[1])
    other = xor_permute(part, 1)

    whitener, mean = whiten(place.reshape(1), sums, part, other, rows, embed)
    offsets = blocks[:, rows + 1, :PARTNERS].astype(jnp.int32)
    loss, grad = contrast(group.reshape(1), offsets, blocks, mean, whitener)
    bits = [bit for bit in (1 << n for n in range(devices.bit_length() - 1))]
    bits = [bit for bit in bits if bit < shares or bit >= SHARED * shares]
    far = group // SHARED * shares + window
    inner = [bit if bit < shares else bit // SHARED for bit in bits]
    keep, send = weight_pieces(far.reshape(1), grad, slices, inner, shares)
    for number, bit in enumerate(bits):
        arrived = xor_permute(send, bit)
        if number < len(bits) - 1:
            keep, send = halve(keep, arrived)
    return loss[0], finish([keep, arrived], whitener)


def solution(mesh):
    return jax.shard_map(
        shards,
        mesh=mesh,
        in_specs=(P(("sp", "win"), None), P(), P("sp", None), P(("sp", "win"), None)),
        out_specs=(P(("sp", "win")), P(("sp", "win"), None)),
        check_vma=False,
    )
```

```python
import jax
import jax.numpy as jnp
from jax import lax
from jax.experimental import pallas as pl
from jax.experimental.pallas import tpu as pltpu
from jax.sharding import PartitionSpec as P

PARTNERS = 4
LOGIT_SCALE = 0.125
AXES = ("sp", "win")
LANES = 128
TAIL = 16
CHUNKS = 8
F32 = jnp.float32
BF16 = jnp.bfloat16
HIGHEST = lax.Precision.HIGHEST


def dot(a, b, contract=(1, 0), precision=None):
    return lax.dot_general(
        a,
        b,
        (((contract[0],), (contract[1],)), ((), ())),
        precision=precision,
        preferred_element_type=F32,
    )


def params(mebibytes, semantics=None):
    return pltpu.CompilerParams(
        vmem_limit_bytes=mebibytes * 2**20, dimension_semantics=semantics
    )


def vmem():
    return pl.BlockSpec(memory_space=pltpu.VMEM)


def smem():
    return pl.BlockSpec(memory_space=pltpu.SMEM)


def xor_permute(piece, mask):
    devices = lax.axis_size(AXES)
    return lax.ppermute(piece, AXES, [(i, i ^ mask) for i in range(devices)])


def split(value):
    high = value.astype(BF16)
    return high, (value - high.astype(F32)).astype(BF16)


def pack_sums(sums, packed, rows):
    high = sums.astype(BF16).astype(F32)
    pad = jnp.zeros((sums.shape[0], 2 * packed - sums.shape[1]), F32)
    lines = []
    for half in (high, sums - high):
        lines += [half[:, :packed], jnp.concatenate([half[:, packed:], pad], axis=1)]
    if rows > 4 * sums.shape[0]:
        lines.append(jnp.zeros((rows - 4 * sums.shape[0], packed), F32))
    return jnp.concatenate(lines, axis=0).astype(BF16)


def unpack_sums(block, count, embed):
    wide = block.astype(F32)
    packed = wide.shape[1]
    low = 2 * count
    left = wide[0:count] + wide[low : low + count]
    right = wide[count:low] + wide[low + count : low + 2 * count]
    return jnp.concatenate([left, right[:, : embed - packed]], axis=1)


def project_kernel(
    me_ref,
    offsets_ref,
    features_hbm,
    weight_hbm,
    ortholog_hbm,
    block_ref,
    slices_ref,
    send_ref,
    keep_ref,
    features_ref,
    weight_ref,
    ortholog_ref,
    means,
    wide,
    sems,
):
    groups, rows, columns = slices_ref.shape
    depth, embed = weight_ref.shape
    half, packed = keep_ref.shape
    blocks = embed // LANES
    tile = depth // CHUNKS

    copies = []
    for n in range(CHUNKS):
        at = pl.ds(n * tile, tile)
        copies.append(
            (
                pltpu.make_async_copy(features_hbm.at[:, at], features_ref.at[:, at], sems.at[0, n]),
                pltpu.make_async_copy(weight_hbm.at[at, :], weight_ref.at[at, :], sems.at[1, n]),
            )
        )
        for copy in copies[-1]:
            copy.start()
    table_copy = pltpu.make_async_copy(ortholog_hbm, ortholog_ref, sems.at[0, CHUNKS])
    table_copy.start()

    total = jnp.zeros((rows, embed), F32)
    for n in range(CHUNKS):
        for copy in copies[n]:
            copy.wait()
        at = slice(n * tile, (n + 1) * tile)
        total = total + dot(features_ref[:, at], weight_ref[at, :])
    for g in range(groups):
        slices_ref[g] = features_ref[:, g * columns : (g + 1) * columns]
    projected = total.astype(BF16)
    block_ref[0:rows, :] = projected

    table_copy.wait()
    line = lax.broadcasted_iota(jnp.int32, (TAIL, embed), 0)
    lane = lax.broadcasted_iota(jnp.int32, (TAIL, embed), 1)
    table = jnp.zeros((TAIL, embed), F32)
    for k in range(PARTNERS):
        table = jnp.where((line == 1) & (lane == k), offsets_ref[0, k].astype(F32), table)
    hits = jnp.concatenate(
        [ortholog_ref[k : k + 1, :].astype(F32) for k in range(PARTNERS)]
        + ([jnp.zeros((1, embed - PARTNERS * rows), F32)] if embed > PARTNERS * rows else []),
        axis=1,
    )
    block_ref[rows:, :] = jnp.where(line == 0, hits, table).astype(BF16)

    sums = jnp.sum(projected.astype(F32), axis=0, keepdims=True)
    send_ref[half:, :] = pack_sums(sums, packed, TAIL)
    wide[:, :embed] = projected
    wide[:, embed:] = projected[:, : packed - LANES]
    ones = jnp.ones((rows, LANES), BF16)
    means[...] = jnp.broadcast_to(sums * (1.0 / rows), means.shape)
    core = me_ref[0] & 1
    for side, out in ((1, send_ref), (0, keep_ref)):
        for r in range(blocks // 2):
            block = (core ^ side) * (blocks // 2) + r
            start = pl.multiple_of(block * LANES, LANES)
            own = wide[:, pl.ds(start, LANES)]
            gram = dot(own, wide[:, pl.ds(start, packed)], (0, 0))
            sums = dot(own, ones, (0, 0))
            for k in range(packed // LANES):
                other = pl.multiple_of((block + k) % blocks * LANES, LANES)
                at = slice(k * LANES, (k + 1) * LANES)
                value = gram[:, at] - sums * means[0:1, pl.ds(other, LANES)]
                out[r * LANES : (r + 1) * LANES, at] = value.astype(out.dtype)


def project(me, offsets, features, weight, ortholog, groups):
    rows, depth = features.shape
    embed = weight.shape[1]
    packed = embed // 2 + LANES
    hbm = pl.BlockSpec(memory_space=pltpu.HBM)
    return pl.pallas_call(
        project_kernel,
        in_specs=[smem(), smem(), hbm, hbm, hbm],
        out_specs=[vmem()] * 4,
        out_shape=[
            jax.ShapeDtypeStruct((rows + TAIL, embed), BF16),
            jax.ShapeDtypeStruct((groups, rows, depth // groups), BF16),
            jax.ShapeDtypeStruct((embed // 2 + TAIL, packed), BF16),
            jax.ShapeDtypeStruct((embed // 2, packed), F32),
        ],
        scratch_shapes=[
            pltpu.VMEM((rows, depth), BF16),
            pltpu.VMEM((depth, embed), BF16),
            pltpu.VMEM((PARTNERS, rows), jnp.int32),
            pltpu.VMEM((8, embed), F32),
            pltpu.VMEM((rows, embed + packed - LANES), BF16),
            pltpu.SemaphoreType.DMA((2, CHUNKS + 1)),
        ],
        compiler_params=params(49),
        cost_estimate=pl.CostEstimate(
            flops=2 * rows * depth * embed, bytes_accessed=2 * depth * embed, transcendentals=0
        ),
        name="project",
    )(me, offsets, features, weight, ortholog)


def make_stage_kernel(seen, arrivals, count, embed):
    def kernel(own_ref, keep_ref, sent_ref, *refs):
        arrived, next_keep, outs = refs[:arrivals], refs[arrivals], refs[arrivals + 1 :]
        full, packed = keep_ref.shape
        share = full // count
        own = own_ref[0]
        sums = [unpack_sums(ref[full:, :], seen, embed) for ref in (sent_ref, *arrived)]
        block = pack_sums(jnp.concatenate(sums, axis=0), packed, outs[0].shape[0] - share)
        for r in range(count):
            at = pl.ds(pl.multiple_of((own ^ r) * share, share), share)
            value = keep_ref[at, :]
            for ref in arrived:
                value = value + ref[at, :].astype(F32)
            if r == 0:
                next_keep[...] = value
            else:
                outs[r - 1][:share, :] = value.astype(BF16)
                outs[r - 1][share:, :] = block

    return kernel


def stage(own, keep, sent, arrived, seen, count, embed):
    full, packed = keep.shape
    share = full // count
    held = seen * (1 + len(arrived))
    tail = -(-4 * held // TAIL) * TAIL
    out = pl.pallas_call(
        make_stage_kernel(seen, len(arrived), count, embed),
        in_specs=[smem()] + [vmem()] * (2 + len(arrived)),
        out_specs=[vmem()] * count,
        out_shape=[jax.ShapeDtypeStruct((share, packed), F32)]
        + [jax.ShapeDtypeStruct((share + tail, packed), BF16)] * (count - 1),
        compiler_params=params(16),
        cost_estimate=pl.CostEstimate(
            flops=full * packed, bytes_accessed=4 * full * packed, transcendentals=0
        ),
        name="stage",
    )(own.reshape(1), keep, sent, *arrived)
    return out[0], out[1:], held


def make_whiten_kernel(rows):
    def kernel(
        place_ref,
        sums_ref,
        near_ref,
        far_ref,
        whitener_ref,
        mean_ref,
        scaled,
        rest,
        first,
        left,
        right,
    ):
        place = place_ref[0]
        embed = scaled.shape[0]
        blocks = embed // LANES
        half = blocks // 2
        pieces, depth = near_ref.shape[:2]
        per_block = LANES // depth
        count = sums_ref.shape[1] // 4
        totals = jnp.concatenate(
            [unpack_sums(sums_ref[k], count, embed) for k in range(sums_ref.shape[0])], axis=0
        )
        total_rows = rows * totals.shape[0]
        tile = 512
        tiles = embed // tile

        mean = jnp.sum(totals, axis=0, keepdims=True) * (1.0 / total_rows)
        mean_ref[...] = mean
        shift_high, shift_low = split(totals * (1.0 / rows) - mean)
        shift_left = jnp.concatenate([shift_high, shift_high, shift_low], axis=0)
        shift_right = jnp.concatenate([shift_high, shift_low, shift_high], axis=0)

        def unpack(source_ref, side):
            for i in range(side * half, (side + 1) * half):
                for part in range(per_block):
                    column = (i - side * half) ^ (place % pieces // per_block)
                    piece = (part ^ (place % per_block)) * half + column
                    wide = source_ref[piece].astype(F32)
                    lines = pl.ds(i * LANES + part * depth, depth)
                    for k in range(half + 1):
                        if k == half and side:
                            continue
                        j = (i + k) % blocks
                        scaled[lines, j * LANES : (j + 1) * LANES] = wide[
                            :, k * LANES : (k + 1) * LANES
                        ]

        for core in range(2):

            @pl.when(place // pieces == core)
            def _():
                unpack(near_ref, core)
                unpack(far_ref, 1 - core)

        for i in range(blocks):
            for k in range(1, half + 1):
                if k == half and i >= half:
                    continue
                j = (i + k) % blocks
                scaled[j * LANES : (j + 1) * LANES, i * LANES : (i + 1) * LANES] = scaled[
                    i * LANES : (i + 1) * LANES, j * LANES : (j + 1) * LANES
                ].T
        squares = jnp.zeros((1, embed), F32)
        for t in range(tiles):
            lines = slice(t * tile, (t + 1) * tile)
            between = dot(shift_left[:, lines], shift_right, (0, 0))
            covariance = (scaled[lines, :] + rows * between) * (1.0 / total_rows)
            scaled[lines, :] = covariance
            first[lines, :] = covariance.astype(BF16)
            squares = squares + jnp.sum(covariance * covariance, axis=0, keepdims=True)
        frobenius = jnp.sqrt(jnp.sum(squares, axis=1, keepdims=True))
        inverse = 1.0 / frobenius
        root = lax.rsqrt(frobenius)

        def product(one, two, finish):
            @pl.loop(0, tiles)
            def _(t):
                lines = pl.ds(pl.multiple_of(t * tile, tile), tile)
                finish(lines, dot(one[lines, :], two[...]))

        def second(lines, value):
            value = value * (inverse * inverse)
            own = scaled[lines, :] * inverse
            scaled[lines, :] = own
            rest[lines, :] = 27.0 * value - 39.0 * own
            left[lines, :] = value.astype(BF16)
            right[lines, :] = (value - 9.0 * own).astype(BF16)

        product(first, first, second)

        def fourth(lines, value):
            value = (value + rest[lines, :]) * (1.0 / 16.0)
            rest[lines, :] = value
            whitener_ref[lines, :] = value.astype(BF16)

        product(left, right, fourth)

        def moved(lines, value):
            value = value * inverse
            scaled[lines, :] = 2.25 * 2.25 * scaled[lines, :] + 4.5 * value
            right[lines, :] = value.astype(BF16)

        product(first, whitener_ref, moved)

        def quad(lines, value):
            value = value + scaled[lines, :]
            rest[lines, :] = 3.0 * rest[lines, :] - 2.25 * value
            left[lines, :] = value.astype(BF16)

        product(whitener_ref, right, quad)
        first[...] = whitener_ref[...]

        def last(lines, value):
            at = lax.broadcasted_iota(jnp.int32, value.shape, 0) + lines.start
            eye = at == lax.broadcasted_iota(jnp.int32, value.shape, 1)
            value = 0.5 * (rest[lines, :] - value)
            value = value + jnp.where(eye, 0.5 * 3.0 * 2.25, 0.0)
            whitener_ref[lines, :] = (value * root).astype(BF16)

        product(first, left, last)

    return kernel


def whiten(place, sums, near, far, rows, embed):
    square = (embed, embed)
    return pl.pallas_call(
        make_whiten_kernel(rows),
        in_specs=[smem()] + [vmem()] * 3,
        out_specs=[vmem(), vmem()],
        out_shape=[
            jax.ShapeDtypeStruct(square, BF16),
            jax.ShapeDtypeStruct((1, embed), F32),
        ],
        scratch_shapes=[pltpu.VMEM(square, F32)] * 2 + [pltpu.VMEM(square, BF16)] * 3,
        compiler_params=params(24),
        cost_estimate=pl.CostEstimate(
            flops=5 * 2 * embed**3, bytes_accessed=2 * embed**2, transcendentals=0
        ),
        name="whiten",
    )(place, sums, near, far)


def contrast_kernel(group_ref, mean_ref, whitener_ref, *refs):
    loss_ref, grad_ref, white, others, tables, numbers, offsets_ref, sem = refs[-8:]
    block_refs = refs[:-8]
    groups, rows, embed = white.shape
    group = group_ref[0]

    for k in range(0, groups, 2):
        pair = block_refs[k : k + 2]
        centered = [(ref[0:rows, :].astype(F32) - mean_ref[...]).astype(BF16) for ref in pair]
        value = dot(jnp.concatenate(centered, axis=0), whitener_ref[...]).astype(BF16)
        for side, ref in enumerate(pair):
            white[group ^ (k + side)] = value[side * rows : (side + 1) * rows]
            table = ref[rows:, :].astype(F32)[0:8]
            tables[group ^ (k + side)] = table
            numbers[group ^ (k + side)] = table[:, 0:LANES].astype(jnp.int32)
    copy = pltpu.make_async_copy(numbers, offsets_ref, sem)
    copy.start()
    copy.wait()

    places = lax.broadcasted_iota(jnp.int32, (rows, rows), 0).astype(F32)

    @pl.loop(0, groups)
    def _(g):
        for k in range(PARTNERS):
            others[k * rows : (k + 1) * rows, :] = white[(g + offsets_ref[g, 1, k]) % groups]
        logits = dot(others[...], white[g], (1, 1)) * LOGIT_SCALE
        loss = jnp.zeros((1, rows), F32)
        weights = []
        for k in range(PARTNERS):
            own = logits[k * rows : (k + 1) * rows]
            peak = jnp.max(own, axis=0, keepdims=True)
            powers = jnp.exp(own - peak)
            sums = jnp.sum(powers, axis=0, keepdims=True)
            hit = places == tables[g, 0:1, k * rows : (k + 1) * rows]
            picked = jnp.sum(jnp.where(hit, own, 0.0), axis=0, keepdims=True)
            loss = loss + (peak + jnp.log(sums) - picked)
            share = powers * (1.0 / (PARTNERS * sums))
            weights.append(jnp.where(hit, share - 1.0 / PARTNERS, share).astype(BF16))
        grad = dot(jnp.concatenate(weights, axis=0), others[...], (0, 0))
        grad_ref[g] = (grad * LOGIT_SCALE).astype(BF16)

        @pl.when(g == group)
        def _():
            loss_ref[...] = loss * (1.0 / PARTNERS)


def contrast(group, blocks, mean, whitener):
    groups = len(blocks)
    rows, embed = blocks[0].shape
    rows -= TAIL
    return pl.pallas_call(
        contrast_kernel,
        in_specs=[smem()] + [vmem()] * (2 + groups),
        out_specs=[vmem()] * 2,
        out_shape=[
            jax.ShapeDtypeStruct((1, rows), F32),
            jax.ShapeDtypeStruct((groups, rows, embed), BF16),
        ],
        scratch_shapes=[
            pltpu.VMEM((groups, rows, embed), BF16),
            pltpu.VMEM((PARTNERS * rows, embed), BF16),
            pltpu.VMEM((groups, 8, embed), F32),
            pltpu.VMEM((groups, 8, LANES), jnp.int32),
            pltpu.SMEM((groups, 8, LANES), jnp.int32),
            pltpu.SemaphoreType.DMA,
        ],
        compiler_params=params(min(58, 12 + 6 * groups * rows * embed // 2**20)),
        cost_estimate=pl.CostEstimate(
            flops=groups * rows * 2 * embed * (embed + 2 * PARTNERS * rows),
            bytes_accessed=4 * groups * rows * embed,
            transcendentals=groups * PARTNERS * rows * rows,
        ),
        name="contrast",
    )(group, mean, whitener, *blocks)


def gather_kernel(window_ref, grad_ref, features_ref, *refs):
    groups = grad_ref.shape[0]
    outs, total = refs[:-1], refs[-1]
    share = outs[0].shape[0]
    window = window_ref[0]

    def columns(at):
        value = dot(features_ref[0, :, at], grad_ref[0], (0, 0))
        for k in range(1, groups):
            value = value + dot(features_ref[k, :, at], grad_ref[k], (0, 0))
        return value

    if share % LANES:
        total[...] = columns(slice(None))
    for r, out in enumerate(outs):
        at = pl.ds(pl.multiple_of((window ^ r) * share, share), share)
        value = total[at, :] if share % LANES else columns(at)
        out[...] = value.astype(out.dtype)


def weight_pieces(window, grad, feature_slices, shares):
    groups, rows, embed = grad.shape
    columns = feature_slices.shape[2]
    share = columns // shares
    return pl.pallas_call(
        gather_kernel,
        in_specs=[smem()] + [vmem()] * 2,
        out_specs=[vmem()] * shares,
        out_shape=[
            jax.ShapeDtypeStruct((share, embed), BF16 if r else F32) for r in range(shares)
        ],
        scratch_shapes=[pltpu.VMEM((columns if share % LANES else 8, embed), F32)],
        compiler_params=params(24),
        cost_estimate=pl.CostEstimate(
            flops=groups * rows * 2 * embed * columns,
            bytes_accessed=2 * groups * rows * (embed + columns),
            transcendentals=0,
        ),
        name="weight_pieces",
    )(window, grad, feature_slices)


def finish_kernel(*refs):
    keep_ref, whitener_ref, out_ref = refs[0], refs[-2], refs[-1]
    value = keep_ref[...]
    for ref in refs[1:-2]:
        value = value + ref[...].astype(F32)
    high, low = split(value)
    out_ref[...] = dot(high, whitener_ref[...], (1, 1)) + dot(low, whitener_ref[...], (1, 1))


def finish(pieces, whitener):
    return pl.pallas_call(
        finish_kernel,
        in_specs=[vmem()] * (len(pieces) + 1),
        out_specs=vmem(),
        out_shape=jax.ShapeDtypeStruct(pieces[0].shape, F32),
        compiler_params=params(12),
        name="finish",
    )(*pieces, whitener)


def shards(features, proj_weight, partner_offsets, ortholog_index):
    rows, depth = features.shape
    embed = proj_weight.shape[1]
    groups = lax.axis_size("sp")
    shares = lax.axis_size("win")
    devices = groups * shares
    group = lax.axis_index("sp").astype(jnp.int32)
    window = lax.axis_index("win").astype(jnp.int32)
    me = group * shares + window

    block, slices, send, keep = project(
        me.reshape(1), partner_offsets, features, proj_weight, ortholog_index.T, groups
    )

    direct = groups == 8
    blocks = {0: block}
    if direct:
        blocks[4] = xor_permute(block, 4 * shares)
        blocks[2] = xor_permute(block, 2 * shares)
    else:
        gathered = lax.all_gather(block, "sp")
        for k in range(groups):
            blocks[k] = lax.dynamic_index_in_dim(gathered, group ^ k, 0, keepdims=False)

    arrived = [xor_permute(send, 1)]
    sent = send
    seen = 1
    stages = []
    low = 1
    place = me & 1
    while keep.shape[0] > 32:
        count = 4
        own = (me >> low) & (count - 1)
        keep, sends, seen = stage(own, keep, sent, arrived, seen, count, embed)
        if direct and low == 1:
            *sends, block = lax.optimization_barrier((*sends, block))
            blocks[1] = xor_permute(block, shares)
        arrived = [xor_permute(piece, (r + 1) << low) for r, piece in enumerate(sends)]
        sent = sends[0]
        stages.append((low, count))
        place = place * count + own
        low += 2
    size = keep.shape[0]
    part = keep
    for piece in arrived:
        part = part + piece[:size].astype(F32)
    sums = jnp.stack([sent[size:]] + [piece[size:] for piece in arrived])
    extra = devices >> low
    if extra > 1:
        mine = jnp.concatenate([part.astype(BF16), sums.reshape(-1, sums.shape[2])])
        others = [xor_permute(mine, r << low) for r in range(1, extra)]
        for piece in others:
            part = part + piece[:size].astype(F32)
        sums = jnp.concatenate([sums] + [piece[size:].reshape(sums.shape) for piece in others])
    part = part.astype(BF16)
    for number, (low, count) in enumerate(stages):
        if direct and number == 0:
            part, blocks[4], blocks[2] = lax.optimization_barrier((part, blocks[4], blocks[2]))
            blocks[6] = xor_permute(blocks[4], 2 * shares)
            blocks[5] = xor_permute(blocks[4], shares)
            blocks[3] = xor_permute(blocks[2], shares)
        part = jnp.concatenate(
            [part] + [xor_permute(part, r << low) for r in range(1, count)], axis=0
        )
    part = part.reshape(-1, size, part.shape[1])
    if direct:
        part, blocks[6] = lax.optimization_barrier((part, blocks[6]))
        blocks[7] = xor_permute(blocks[6], shares)
    other = xor_permute(part, 1)

    other, slices = lax.optimization_barrier((other, slices))
    slices = lax.all_to_all(slices, "sp", 0, 0)

    whitener, mean = whiten(place.reshape(1), sums, part, other, rows, embed)
    blocks = [blocks[k] for k in range(groups)]
    loss, grad = contrast(group.reshape(1), blocks, mean, whitener)
    pieces = weight_pieces(window.reshape(1), grad, slices, shares)
    pieces = [pieces[0]] + [xor_permute(pieces[r], r) for r in range(1, shares)]
    return loss[0], finish(pieces, whitener)


def solution(mesh):
    return jax.shard_map(
        shards,
        mesh=mesh,
        in_specs=(P(("sp", "win"), None), P(), P("sp", None), P(("sp", "win"), None)),
        out_specs=(P(("sp", "win")), P(("sp", "win"), None)),
        check_vma=False,
    )
```

```python
import functools

import jax
import jax.numpy as jnp
from jax import lax
from jax.experimental import pallas as pl
from jax.experimental.pallas import tpu as pltpu
from jax.sharding import PartitionSpec as P

PARTNERS = 4
LOGIT_SCALE = 0.125
AXES = ("sp", "win")
LANES = 128
TAIL = 16
CHUNKS = 8
F32 = jnp.float32
BF16 = jnp.bfloat16
HIGHEST = lax.Precision.HIGHEST


def dot(a, b, contract=(1, 0), precision=None):
    return lax.dot_general(
        a,
        b,
        (((contract[0],), (contract[1],)), ((), ())),
        precision=precision,
        preferred_element_type=F32,
    )


def params(mebibytes, semantics=None):
    return pltpu.CompilerParams(
        vmem_limit_bytes=mebibytes * 2**20, dimension_semantics=semantics
    )


def vmem():
    return pl.BlockSpec(memory_space=pltpu.VMEM)


def smem():
    return pl.BlockSpec(memory_space=pltpu.SMEM)


def xor_permute(piece, mask):
    devices = lax.axis_size(AXES)
    return lax.ppermute(piece, AXES, [(i, i ^ mask) for i in range(devices)])


def split(value):
    high = value.astype(BF16)
    return high, (value - high.astype(F32)).astype(BF16)


def cut_kernel(group_ref, features_hbm, near_ref, far_ref, sems):
    halves, _, columns = near_ref.shape
    copies = []
    for r in range(halves):
        for side, out in ((1, far_ref), (0, near_ref)):
            start = pl.multiple_of((group_ref[0] ^ (2 * r + side)) * columns, columns)
            copy = pltpu.make_async_copy(
                features_hbm.at[:, pl.ds(start, columns)], out.at[r], sems.at[side, r]
            )
            copy.start()
            copies.append(copy)
    for copy in copies:
        copy.wait()


def cut(group, features, groups):
    rows, depth = features.shape
    half = jax.ShapeDtypeStruct((groups // 2, rows, depth // groups), BF16)
    return pl.pallas_call(
        cut_kernel,
        in_specs=[smem(), pl.BlockSpec(memory_space=pltpu.HBM)],
        out_specs=[vmem()] * 2,
        out_shape=[half, half],
        scratch_shapes=[pltpu.SemaphoreType.DMA((2, groups // 2))],
        compiler_params=params(56),
        name="cut",
    )(group, features)


def pack_sums(sums, packed, rows):
    high = sums.astype(BF16).astype(F32)
    pad = jnp.zeros((sums.shape[0], 2 * packed - sums.shape[1]), F32)
    lines = []
    for half in (high, sums - high):
        lines += [half[:, :packed], jnp.concatenate([half[:, packed:], pad], axis=1)]
    if rows > 4 * sums.shape[0]:
        lines.append(jnp.zeros((rows - 4 * sums.shape[0], packed), F32))
    return jnp.concatenate(lines, axis=0).astype(BF16)


def unpack_sums(block, count, embed):
    wide = block.astype(F32)
    packed = wide.shape[1]
    low = 2 * count
    left = wide[0:count] + wide[low : low + count]
    right = wide[count:low] + wide[low + count : low + 2 * count]
    return jnp.concatenate([left, right[:, : embed - packed]], axis=1)


def project_kernel(
    me_ref,
    offsets_ref,
    features_hbm,
    weight_hbm,
    ortholog_hbm,
    block_ref,
    send_ref,
    keep_ref,
    features_ref,
    weight_ref,
    ortholog_ref,
    means,
    wide,
    sems,
):
    rows = features_ref.shape[0]
    depth, embed = weight_ref.shape
    half, packed = keep_ref.shape
    blocks = embed // LANES
    tile = depth // CHUNKS

    copies = []
    for n in range(CHUNKS):
        at = pl.ds(n * tile, tile)
        copies.append(
            (
                pltpu.make_async_copy(features_hbm.at[:, at], features_ref.at[:, at], sems.at[0, n]),
                pltpu.make_async_copy(weight_hbm.at[at, :], weight_ref.at[at, :], sems.at[1, n]),
            )
        )
        for copy in copies[-1]:
            copy.start()
    table_copy = pltpu.make_async_copy(ortholog_hbm, ortholog_ref, sems.at[0, CHUNKS])
    table_copy.start()

    total = jnp.zeros((rows, embed), F32)
    for n in range(CHUNKS):
        for copy in copies[n]:
            copy.wait()
        at = slice(n * tile, (n + 1) * tile)
        total = total + dot(features_ref[:, at], weight_ref[at, :])
    projected = total.astype(BF16)
    block_ref[0:rows, :] = projected

    table_copy.wait()
    line = lax.broadcasted_iota(jnp.int32, (TAIL, embed), 0)
    lane = lax.broadcasted_iota(jnp.int32, (TAIL, embed), 1)
    table = jnp.zeros((TAIL, embed), F32)
    for k in range(PARTNERS):
        table = jnp.where((line == 1) & (lane == k), offsets_ref[0, k].astype(F32), table)
    hits = jnp.concatenate(
        [ortholog_ref[k : k + 1, :].astype(F32) for k in range(PARTNERS)]
        + ([jnp.zeros((1, embed - PARTNERS * rows), F32)] if embed > PARTNERS * rows else []),
        axis=1,
    )
    block_ref[rows:, :] = jnp.where(line == 0, hits, table).astype(BF16)

    sums = jnp.sum(projected.astype(F32), axis=0, keepdims=True)
    send_ref[half:, :] = pack_sums(sums, packed, TAIL)
    wide[:, :embed] = projected
    wide[:, embed:] = projected[:, : packed - LANES]
    ones = jnp.ones((rows, LANES), BF16)
    means[...] = jnp.broadcast_to(sums * (1.0 / rows), means.shape)
    core = me_ref[0] & 1
    for side, out in ((1, send_ref), (0, keep_ref)):
        for r in range(blocks // 2):
            block = (core ^ side) * (blocks // 2) + r
            start = pl.multiple_of(block * LANES, LANES)
            own = wide[:, pl.ds(start, LANES)]
            gram = dot(own, wide[:, pl.ds(start, packed)], (0, 0))
            sums = dot(own, ones, (0, 0))
            for k in range(packed // LANES):
                other = pl.multiple_of((block + k) % blocks * LANES, LANES)
                at = slice(k * LANES, (k + 1) * LANES)
                value = gram[:, at] - sums * means[0:1, pl.ds(other, LANES)]
                out[r * LANES : (r + 1) * LANES, at] = value.astype(out.dtype)


def project(me, offsets, features, weight, ortholog):
    rows, depth = features.shape
    embed = weight.shape[1]
    packed = embed // 2 + LANES
    hbm = pl.BlockSpec(memory_space=pltpu.HBM)
    return pl.pallas_call(
        project_kernel,
        in_specs=[smem(), smem(), hbm, hbm, hbm],
        out_specs=[vmem()] * 3,
        out_shape=[
            jax.ShapeDtypeStruct((rows + TAIL, embed), BF16),
            jax.ShapeDtypeStruct((embed // 2 + TAIL, packed), BF16),
            jax.ShapeDtypeStruct((embed // 2, packed), F32),
        ],
        scratch_shapes=[
            pltpu.VMEM((rows, depth), BF16),
            pltpu.VMEM((depth, embed), BF16),
            pltpu.VMEM((PARTNERS, rows), jnp.int32),
            pltpu.VMEM((8, embed), F32),
            pltpu.VMEM((rows, embed + packed - LANES), BF16),
            pltpu.SemaphoreType.DMA((2, CHUNKS + 1)),
        ],
        compiler_params=params(49),
        cost_estimate=pl.CostEstimate(
            flops=2 * rows * depth * embed, bytes_accessed=2 * depth * embed, transcendentals=0
        ),
        name="project",
    )(me, offsets, features, weight, ortholog)


def make_stage_kernel(seen, arrivals, count, embed):
    def kernel(own_ref, keep_ref, sent_ref, *refs):
        arrived, next_keep, outs = refs[:arrivals], refs[arrivals], refs[arrivals + 1 :]
        full, packed = keep_ref.shape
        share = full // count
        own = own_ref[0]
        sums = [unpack_sums(ref[full:, :], seen, embed) for ref in (sent_ref, *arrived)]
        block = pack_sums(jnp.concatenate(sums, axis=0), packed, outs[0].shape[0] - share)
        for r in range(count):
            at = pl.ds(pl.multiple_of((own ^ r) * share, share), share)
            value = keep_ref[at, :]
            for ref in arrived:
                value = value + ref[at, :].astype(F32)
            if r == 0:
                next_keep[...] = value
            else:
                outs[r - 1][:share, :] = value.astype(BF16)
                outs[r - 1][share:, :] = block

    return kernel


def stage(own, keep, sent, arrived, seen, count, embed):
    full, packed = keep.shape
    share = full // count
    held = seen * (1 + len(arrived))
    tail = -(-4 * held // TAIL) * TAIL
    out = pl.pallas_call(
        make_stage_kernel(seen, len(arrived), count, embed),
        in_specs=[smem()] + [vmem()] * (2 + len(arrived)),
        out_specs=[vmem()] * count,
        out_shape=[jax.ShapeDtypeStruct((share, packed), F32)]
        + [jax.ShapeDtypeStruct((share + tail, packed), BF16)] * (count - 1),
        compiler_params=params(16),
        cost_estimate=pl.CostEstimate(
            flops=full * packed, bytes_accessed=4 * full * packed, transcendentals=0
        ),
        name="stage",
    )(own.reshape(1), keep, sent, *arrived)
    return out[0], out[1:], held


def make_whiten_kernel(rows, count):
    def kernel(
        place_ref,
        near_ref,
        far_ref,
        *refs,
    ):
        sums_refs = refs[:-7]
        whitener_ref, mean_ref, scaled, rest, first, left, right = refs[-7:]
        place = place_ref[0]
        embed = scaled.shape[0]
        blocks = embed // LANES
        half = blocks // 2
        pieces, depth = near_ref.shape[:2]
        per_block = LANES // depth
        totals = jnp.concatenate(
            [
                unpack_sums(ref[start : start + 4 * count, :], count, embed)
                for ref in sums_refs
                for start in range(depth, ref.shape[0], 4 * count)
            ],
            axis=0,
        )
        total_rows = rows * totals.shape[0]
        tile = 512
        tiles = embed // tile

        mean = jnp.sum(totals, axis=0, keepdims=True) * (1.0 / total_rows)
        mean_ref[...] = mean
        shift_high, shift_low = split(totals * (1.0 / rows) - mean)
        shift_left = jnp.concatenate([shift_high, shift_high, shift_low], axis=0)
        shift_right = jnp.concatenate([shift_high, shift_low, shift_high], axis=0)

        def unpack(source_ref, side):
            for i in range(side * half, (side + 1) * half):
                for part in range(per_block):
                    piece = ((i - side * half) * per_block + part) ^ (place % pieces)
                    wide = source_ref[piece].astype(F32)
                    lines = pl.ds(i * LANES + part * depth, depth)
                    for k in range(half + 1):
                        if k == half and side:
                            continue
                        j = (i + k) % blocks
                        scaled[lines, j * LANES : (j + 1) * LANES] = wide[
                            :, k * LANES : (k + 1) * LANES
                        ]

        for core in range(2):

            @pl.when(place // pieces == core)
            def _():
                unpack(near_ref, core)
                unpack(far_ref, 1 - core)

        for i in range(blocks):
            for k in range(1, half + 1):
                if k == half and i >= half:
                    continue
                j = (i + k) % blocks
                scaled[j * LANES : (j + 1) * LANES, i * LANES : (i + 1) * LANES] = scaled[
                    i * LANES : (i + 1) * LANES, j * LANES : (j + 1) * LANES
                ].T
        squares = jnp.zeros((1, embed), F32)
        for t in range(tiles):
            lines = slice(t * tile, (t + 1) * tile)
            between = dot(shift_left[:, lines], shift_right, (0, 0))
            covariance = (scaled[lines, :] + rows * between) * (1.0 / total_rows)
            scaled[lines, :] = covariance
            first[lines, :] = covariance.astype(BF16)
            squares = squares + jnp.sum(covariance * covariance, axis=0, keepdims=True)
        frobenius = jnp.sqrt(jnp.sum(squares, axis=1, keepdims=True))
        inverse = 1.0 / frobenius
        root = lax.rsqrt(frobenius)

        def product(one, two, finish):
            @pl.loop(0, tiles)
            def _(t):
                lines = pl.ds(pl.multiple_of(t * tile, tile), tile)
                finish(lines, dot(one[lines, :], two[...]))

        def second(lines, value):
            value = value * (inverse * inverse)
            own = scaled[lines, :] * inverse
            scaled[lines, :] = own
            rest[lines, :] = 27.0 * value - 39.0 * own
            left[lines, :] = value.astype(BF16)
            right[lines, :] = (value - 9.0 * own).astype(BF16)

        product(first, first, second)

        def fourth(lines, value):
            value = (value + rest[lines, :]) * (1.0 / 16.0)
            rest[lines, :] = value
            whitener_ref[lines, :] = value.astype(BF16)

        product(left, right, fourth)

        def moved(lines, value):
            value = value * inverse
            scaled[lines, :] = 2.25 * 2.25 * scaled[lines, :] + 4.5 * value
            right[lines, :] = value.astype(BF16)

        product(first, whitener_ref, moved)

        def quad(lines, value):
            value = value + scaled[lines, :]
            rest[lines, :] = 3.0 * rest[lines, :] - 2.25 * value
            left[lines, :] = value.astype(BF16)

        product(whitener_ref, right, quad)
        first[...] = whitener_ref[...]

        def last(lines, value):
            at = lax.broadcasted_iota(jnp.int32, value.shape, 0) + lines.start
            eye = at == lax.broadcasted_iota(jnp.int32, value.shape, 1)
            value = 0.5 * (rest[lines, :] - value)
            value = value + jnp.where(eye, 0.5 * 3.0 * 2.25, 0.0)
            whitener_ref[lines, :] = (value * root).astype(BF16)

        product(first, left, last)

    return kernel


def whiten(place, near, far, sums, count, rows, embed):
    square = (embed, embed)
    return pl.pallas_call(
        make_whiten_kernel(rows, count),
        in_specs=[smem()] + [vmem()] * (2 + len(sums)),
        out_specs=[vmem(), vmem()],
        out_shape=[
            jax.ShapeDtypeStruct(square, BF16),
            jax.ShapeDtypeStruct((1, embed), F32),
        ],
        scratch_shapes=[pltpu.VMEM(square, F32)] * 2 + [pltpu.VMEM(square, BF16)] * 3,
        compiler_params=params(24),
        cost_estimate=pl.CostEstimate(
            flops=5 * 2 * embed**3, bytes_accessed=2 * embed**2, transcendentals=0
        ),
        name="whiten",
    )(place, near, far, *sums)


def contrast_kernel(order, group_ref, mean_ref, whitener_ref, *refs):
    loss_ref, grad_ref, white, others, tables, numbers, offsets_ref, sem = refs[-8:]
    block_refs = [ref.at[i] for ref in refs[:-8] for i in range(ref.shape[0])]
    block_refs = [block_refs[order.index(k)] for k in range(len(order))]
    groups, rows, embed = white.shape
    group = group_ref[0]

    for k in range(0, groups, 2):
        pair = block_refs[k : k + 2]
        centered = [(ref[0:rows, :].astype(F32) - mean_ref[...]).astype(BF16) for ref in pair]
        value = dot(jnp.concatenate(centered, axis=0), whitener_ref[...]).astype(BF16)
        for side, ref in enumerate(pair):
            white[group ^ (k + side)] = value[side * rows : (side + 1) * rows]
            table = ref[rows:, :].astype(F32)[0:8]
            tables[group ^ (k + side)] = table
            numbers[group ^ (k + side)] = table[:, 0:LANES].astype(jnp.int32)
    copy = pltpu.make_async_copy(numbers, offsets_ref, sem)
    copy.start()
    copy.wait()

    places = lax.broadcasted_iota(jnp.int32, (rows, rows), 0).astype(F32)

    @pl.loop(0, groups)
    def _(g):
        for k in range(PARTNERS):
            others[k * rows : (k + 1) * rows, :] = white[(g + offsets_ref[g, 1, k]) % groups]
        logits = dot(others[...], white[g], (1, 1)) * LOGIT_SCALE
        loss = jnp.zeros((1, rows), F32)
        weights = []
        for k in range(PARTNERS):
            own = logits[k * rows : (k + 1) * rows]
            peak = jnp.max(own, axis=0, keepdims=True)
            powers = jnp.exp(own - peak)
            sums = jnp.sum(powers, axis=0, keepdims=True)
            hit = places == tables[g, 0:1, k * rows : (k + 1) * rows]
            picked = jnp.sum(jnp.where(hit, own, 0.0), axis=0, keepdims=True)
            loss = loss + (peak + jnp.log(sums) - picked)
            share = powers * (1.0 / (PARTNERS * sums))
            weights.append(jnp.where(hit, share - 1.0 / PARTNERS, share).astype(BF16))
        grad = dot(jnp.concatenate(weights, axis=0), others[...], (0, 0))
        grad_ref[g] = (grad * LOGIT_SCALE).astype(BF16)

        @pl.when(g == group)
        def _():
            loss_ref[...] = loss * (1.0 / PARTNERS)


def contrast(group, blocks, order, mean, whitener):
    groups = len(order)
    rows, embed = blocks[0].shape[1:]
    rows -= TAIL
    return pl.pallas_call(
        functools.partial(contrast_kernel, order),
        in_specs=[smem()] + [vmem()] * (2 + len(blocks)),
        out_specs=[vmem()] * 2,
        out_shape=[
            jax.ShapeDtypeStruct((1, rows), F32),
            jax.ShapeDtypeStruct((groups, rows, embed), BF16),
        ],
        scratch_shapes=[
            pltpu.VMEM((groups, rows, embed), BF16),
            pltpu.VMEM((PARTNERS * rows, embed), BF16),
            pltpu.VMEM((groups, 8, embed), F32),
            pltpu.VMEM((groups, 8, LANES), jnp.int32),
            pltpu.SMEM((groups, 8, LANES), jnp.int32),
            pltpu.SemaphoreType.DMA,
        ],
        compiler_params=params(min(58, 12 + 6 * groups * rows * embed // 2**20)),
        cost_estimate=pl.CostEstimate(
            flops=groups * rows * 2 * embed * (embed + 2 * PARTNERS * rows),
            bytes_accessed=4 * groups * rows * embed,
            transcendentals=groups * PARTNERS * rows * rows,
        ),
        name="contrast",
    )(group, mean, whitener, *blocks)


def pieces_kernel(shares, group_ref, window_ref, grad_ref, *refs):
    groups, _, embed = grad_ref.shape
    outs, total = refs[-1 - shares : -1], refs[-1]
    features = [ref.at[i] for ref in refs[: -1 - shares] for i in range(ref.shape[0])]
    share = outs[0].shape[0]

    def columns(at):
        value = dot(features[0][:, at], grad_ref[group_ref[0]], (0, 0))
        for k in range(1, groups):
            value = value + dot(features[k][:, at], grad_ref[group_ref[0] ^ k], (0, 0))
        return value

    if share % LANES:
        total[...] = columns(slice(None))
    for r, out in enumerate(outs):
        at = pl.ds(pl.multiple_of((window_ref[0] ^ r) * share, share), share)
        value = total[at, :] if share % LANES else columns(at)
        out[...] = value.astype(out.dtype)


def weight_pieces(group, window, grad, slices, shares):
    groups, rows, embed = grad.shape
    columns = slices[0].shape[2]
    share = columns // shares
    return pl.pallas_call(
        functools.partial(pieces_kernel, shares),
        in_specs=[smem(), smem()] + [vmem()] * (1 + len(slices)),
        out_specs=[vmem()] * shares,
        out_shape=[
            jax.ShapeDtypeStruct((share, embed), BF16 if r else F32) for r in range(shares)
        ],
        scratch_shapes=[pltpu.VMEM((columns if share % LANES else 8, embed), F32)],
        compiler_params=params(24),
        cost_estimate=pl.CostEstimate(
            flops=groups * rows * 2 * embed * columns,
            bytes_accessed=2 * groups * rows * (embed + columns),
            transcendentals=0,
        ),
        name="weight_pieces",
    )(group, window, grad, *slices)


def finish_kernel(*refs):
    keep_ref, whitener_ref, out_ref = refs[0], refs[-2], refs[-1]
    value = keep_ref[...]
    for ref in refs[1:-2]:
        value = value + ref[...].astype(F32)
    high, low = split(value)
    out_ref[...] = dot(high, whitener_ref[...], (1, 1)) + dot(low, whitener_ref[...], (1, 1))


def finish(pieces, whitener):
    return pl.pallas_call(
        finish_kernel,
        in_specs=[vmem()] * (len(pieces) + 1),
        out_specs=vmem(),
        out_shape=jax.ShapeDtypeStruct(pieces[0].shape, F32),
        compiler_params=params(12),
        name="finish",
    )(*pieces, whitener)


def shards(features, proj_weight, partner_offsets, ortholog_index):
    rows, depth = features.shape
    embed = proj_weight.shape[1]
    groups = lax.axis_size("sp")
    shares = lax.axis_size("win")
    devices = groups * shares
    group = lax.axis_index("sp").astype(jnp.int32)
    window = lax.axis_index("win").astype(jnp.int32)
    me = group * shares + window

    direct = groups == 8
    by_x, by_near, by_far = shares, 2 * shares, 4 * shares
    me_scalar = me.reshape(1)
    if direct:
        own_slices, x_slices = cut(group.reshape(1), features, groups)
        own_slices, x_slices, me_scalar = lax.optimization_barrier((own_slices, x_slices, me_scalar))
        x_slices = xor_permute(x_slices, by_x)
    else:
        slices = features.reshape(rows, groups, depth // groups).transpose(1, 0, 2)
        slices = lax.all_to_all(slices, "sp", 0, 0)
        slices = [
            lax.dynamic_index_in_dim(slices, group ^ k, 0, keepdims=True) for k in range(groups)
        ]

    block, send, keep = project(
        me_scalar, partner_offsets, features, proj_weight, ortholog_index.T
    )
    block = block[None]
    if direct:
        block_far = xor_permute(block, by_far)
        block_near = xor_permute(block, by_near)
    else:
        gathered = lax.all_gather(block, "sp", tiled=True)

    arrived = [xor_permute(send, 1)]
    if direct:
        arrived[0], x_slices = lax.optimization_barrier((arrived[0], x_slices))
    sent = send
    seen = 1
    stages = []
    low = 1
    place = me & 1
    while keep.shape[0] > 32:
        count = 4
        own = (me >> low) & (count - 1)
        keep, sends, seen = stage(own, keep, sent, arrived, seen, count, embed)
        if direct and stages:
            *sends, block_far, block_near = lax.optimization_barrier(
                (*sends, block_far, block_near)
            )
            pair_x = xor_permute(jnp.concatenate([block, block_near]), by_x)
        arrived = [xor_permute(piece, (r + 1) << low) for r, piece in enumerate(sends)]
        sent = sends[0]
        stages.append((low, count))
        place = place * count + own
        low += 2
    size = keep.shape[0]
    part = keep
    for piece in arrived:
        part = part + piece[:size].astype(F32)
    sums = [sent, *arrived]
    extra = devices >> low
    if extra > 1:
        mine = jnp.concatenate([part.astype(BF16)] + [piece[size:] for piece in sums])
        others = [xor_permute(mine, r << low) for r in range(1, extra)]
        for piece in others:
            part = part + piece[:size].astype(F32)
        sums = [mine, *others]
    part = part.astype(BF16)
    for number, (low, count) in enumerate(reversed(stages)):
        if direct and number == 1:
            part, pair_x, block_far = lax.optimization_barrier((part, pair_x, block_far))
            block_far_near = xor_permute(block_far, by_near)
        part = jnp.concatenate(
            [part] + [xor_permute(part, r << low) for r in range(1, count)], axis=0
        )
    part = part.reshape(-1, size, part.shape[1])
    if direct:
        part, block_far_near, own_slices, x_slices = lax.optimization_barrier(
            (part, block_far_near, own_slices, x_slices)
        )
        far_x = xor_permute(jnp.concatenate([block_far, block_far_near]), by_x)
        blocks = [block, block_near, pair_x, block_far, block_far_near, far_x]
        order = [0, 2, 1, 3, 4, 6, 5, 7]
        slices = [own_slices[:1], x_slices[:1]]
        for r in range(1, groups // 2):
            pair = jnp.stack([own_slices[r], x_slices[r]])
            slices.append(xor_permute(pair, 2 * r * shares))
    else:
        order = list(range(groups))
        blocks = [
            lax.dynamic_index_in_dim(gathered, group ^ k, 0, keepdims=True) for k in order
        ]
    other = xor_permute(part, 1)

    whitener, mean = whiten(place.reshape(1), part, other, sums, seen, rows, embed)
    loss, grad = contrast(group.reshape(1), blocks, order, mean, whitener)
    pieces = weight_pieces(group.reshape(1), window.reshape(1), grad, slices, shares)
    pieces = [pieces[0]] + [xor_permute(pieces[r], r) for r in range(1, shares)]
    return loss[0], finish(pieces, whitener)


def solution(mesh):
    return jax.shard_map(
        shards,
        mesh=mesh,
        in_specs=(P(("sp", "win"), None), P(), P("sp", None), P(("sp", "win"), None)),
        out_specs=(P(("sp", "win")), P(("sp", "win"), None)),
        check_vma=False,
    )
```

```python
import functools

import jax
import jax.numpy as jnp
from jax import lax
from jax.experimental import pallas as pl
from jax.experimental.pallas import tpu as pltpu
from jax.sharding import PartitionSpec as P

PARTNERS = 4
LOGIT_SCALE = 0.125
AXES = ("sp", "win")
LANES = 128
TAIL = 16
CHUNKS = 8
F32 = jnp.float32
BF16 = jnp.bfloat16
HIGHEST = lax.Precision.HIGHEST


def dot(a, b, contract=(1, 0), precision=None):
    return lax.dot_general(
        a,
        b,
        (((contract[0],), (contract[1],)), ((), ())),
        precision=precision,
        preferred_element_type=F32,
    )


def params(mebibytes, semantics=None):
    return pltpu.CompilerParams(
        vmem_limit_bytes=mebibytes * 2**20, dimension_semantics=semantics
    )


def vmem():
    return pl.BlockSpec(memory_space=pltpu.VMEM)


def smem():
    return pl.BlockSpec(memory_space=pltpu.SMEM)


def xor_permute(piece, mask):
    devices = lax.axis_size(AXES)
    return lax.ppermute(piece, AXES, [(i, i ^ mask) for i in range(devices)])


def split(value):
    high = value.astype(BF16)
    return high, (value - high.astype(F32)).astype(BF16)


def cut_kernel(group_ref, features_hbm, *refs):
    outs, sems = refs[:-1], refs[-1]
    columns = outs[0].shape[1]
    copies = []
    for k, out in enumerate(outs):
        start = pl.multiple_of((group_ref[0] ^ k) * columns, columns)
        copies.append(
            pltpu.make_async_copy(features_hbm.at[:, pl.ds(start, columns)], out, sems.at[k])
        )
        copies[k].start()
    for copy in copies:
        copy.wait()


def cut(group, features, groups):
    rows, depth = features.shape
    return pl.pallas_call(
        cut_kernel,
        in_specs=[smem(), pl.BlockSpec(memory_space=pltpu.HBM)],
        out_specs=[vmem()] * groups,
        out_shape=[jax.ShapeDtypeStruct((rows, depth // groups), BF16)] * groups,
        scratch_shapes=[pltpu.SemaphoreType.DMA((groups,))],
        compiler_params=params(8),
        name="cut",
    )(group, features)


def pack_sums(sums, packed, rows):
    high = sums.astype(BF16).astype(F32)
    pad = jnp.zeros((sums.shape[0], 2 * packed - sums.shape[1]), F32)
    lines = []
    for half in (high, sums - high):
        lines += [half[:, :packed], jnp.concatenate([half[:, packed:], pad], axis=1)]
    if rows > 4 * sums.shape[0]:
        lines.append(jnp.zeros((rows - 4 * sums.shape[0], packed), F32))
    return jnp.concatenate(lines, axis=0).astype(BF16)


def unpack_sums(block, count, embed):
    wide = block.astype(F32)
    packed = wide.shape[1]
    low = 2 * count
    left = wide[0:count] + wide[low : low + count]
    right = wide[count:low] + wide[low + count : low + 2 * count]
    return jnp.concatenate([left, right[:, : embed - packed]], axis=1)


def project_kernel(
    me_ref,
    offsets_ref,
    features_hbm,
    weight_hbm,
    ortholog_hbm,
    block_ref,
    send_ref,
    keep_ref,
    features_ref,
    weight_ref,
    ortholog_ref,
    means,
    wide,
    sems,
):
    rows = features_ref.shape[0]
    depth, embed = weight_ref.shape
    half, packed = keep_ref.shape
    blocks = embed // LANES
    tile = depth // CHUNKS

    copies = []
    for n in range(CHUNKS):
        at = pl.ds(n * tile, tile)
        copies.append(
            (
                pltpu.make_async_copy(features_hbm.at[:, at], features_ref.at[:, at], sems.at[0, n]),
                pltpu.make_async_copy(weight_hbm.at[at, :], weight_ref.at[at, :], sems.at[1, n]),
            )
        )
        for copy in copies[-1]:
            copy.start()
    table_copy = pltpu.make_async_copy(ortholog_hbm, ortholog_ref, sems.at[0, CHUNKS])
    table_copy.start()

    total = jnp.zeros((rows, embed), F32)
    for n in range(CHUNKS):
        for copy in copies[n]:
            copy.wait()
        at = slice(n * tile, (n + 1) * tile)
        total = total + dot(features_ref[:, at], weight_ref[at, :])
    projected = total.astype(BF16)
    block_ref[0:rows, :] = projected

    table_copy.wait()
    line = lax.broadcasted_iota(jnp.int32, (TAIL, embed), 0)
    lane = lax.broadcasted_iota(jnp.int32, (TAIL, embed), 1)
    table = jnp.zeros((TAIL, embed), F32)
    for k in range(PARTNERS):
        table = jnp.where((line == 1) & (lane == k), offsets_ref[0, k].astype(F32), table)
    hits = jnp.concatenate(
        [ortholog_ref[k : k + 1, :].astype(F32) for k in range(PARTNERS)]
        + ([jnp.zeros((1, embed - PARTNERS * rows), F32)] if embed > PARTNERS * rows else []),
        axis=1,
    )
    block_ref[rows:, :] = jnp.where(line == 0, hits, table).astype(BF16)

    sums = jnp.sum(projected.astype(F32), axis=0, keepdims=True)
    send_ref[half:, :] = pack_sums(sums, packed, TAIL)
    wide[:, :embed] = projected
    wide[:, embed:] = projected[:, : packed - LANES]
    ones = jnp.ones((rows, LANES), BF16)
    means[...] = jnp.broadcast_to(sums * (1.0 / rows), means.shape)
    core = me_ref[0] & 1
    for side, out in ((1, send_ref), (0, keep_ref)):
        for r in range(blocks // 2):
            block = (core ^ side) * (blocks // 2) + r
            start = pl.multiple_of(block * LANES, LANES)
            own = wide[:, pl.ds(start, LANES)]
            gram = dot(own, wide[:, pl.ds(start, packed)], (0, 0))
            sums = dot(own, ones, (0, 0))
            for k in range(packed // LANES):
                other = pl.multiple_of((block + k) % blocks * LANES, LANES)
                at = slice(k * LANES, (k + 1) * LANES)
                value = gram[:, at] - sums * means[0:1, pl.ds(other, LANES)]
                out[r * LANES : (r + 1) * LANES, at] = value.astype(out.dtype)


def project(me, offsets, features, weight, ortholog):
    rows, depth = features.shape
    embed = weight.shape[1]
    packed = embed // 2 + LANES
    hbm = pl.BlockSpec(memory_space=pltpu.HBM)
    return pl.pallas_call(
        project_kernel,
        in_specs=[smem(), smem(), hbm, hbm, hbm],
        out_specs=[vmem()] * 3,
        out_shape=[
            jax.ShapeDtypeStruct((rows + TAIL, embed), BF16),
            jax.ShapeDtypeStruct((embed // 2 + TAIL, packed), BF16),
            jax.ShapeDtypeStruct((embed // 2, packed), F32),
        ],
        scratch_shapes=[
            pltpu.VMEM((rows, depth), BF16),
            pltpu.VMEM((depth, embed), BF16),
            pltpu.VMEM((PARTNERS, rows), jnp.int32),
            pltpu.VMEM((8, embed), F32),
            pltpu.VMEM((rows, embed + packed - LANES), BF16),
            pltpu.SemaphoreType.DMA((2, CHUNKS + 1)),
        ],
        compiler_params=params(49),
        cost_estimate=pl.CostEstimate(
            flops=2 * rows * depth * embed, bytes_accessed=2 * depth * embed, transcendentals=0
        ),
        name="project",
    )(me, offsets, features, weight, ortholog)


def make_stage_kernel(seen, arrivals, count, embed):
    def kernel(own_ref, keep_ref, sent_ref, *refs):
        arrived, next_keep, outs = refs[:arrivals], refs[arrivals], refs[arrivals + 1 :]
        full, packed = keep_ref.shape
        share = full // count
        own = own_ref[0]
        sums = [unpack_sums(ref[full:, :], seen, embed) for ref in (sent_ref, *arrived)]
        block = pack_sums(jnp.concatenate(sums, axis=0), packed, outs[0].shape[0] - share)
        for r in range(count):
            at = pl.ds(pl.multiple_of((own ^ r) * share, share), share)
            value = keep_ref[at, :]
            for ref in arrived:
                value = value + ref[at, :].astype(F32)
            if r == 0:
                next_keep[...] = value
            else:
                outs[r - 1][:share, :] = value.astype(BF16)
                outs[r - 1][share:, :] = block

    return kernel


def stage(own, keep, sent, arrived, seen, count, embed):
    full, packed = keep.shape
    share = full // count
    held = seen * (1 + len(arrived))
    tail = -(-4 * held // TAIL) * TAIL
    out = pl.pallas_call(
        make_stage_kernel(seen, len(arrived), count, embed),
        in_specs=[smem()] + [vmem()] * (2 + len(arrived)),
        out_specs=[vmem()] * count,
        out_shape=[jax.ShapeDtypeStruct((share, packed), F32)]
        + [jax.ShapeDtypeStruct((share + tail, packed), BF16)] * (count - 1),
        compiler_params=params(16),
        cost_estimate=pl.CostEstimate(
            flops=full * packed, bytes_accessed=4 * full * packed, transcendentals=0
        ),
        name="stage",
    )(own.reshape(1), keep, sent, *arrived)
    return out[0], out[1:], held


def make_whiten_kernel(rows, count):
    def kernel(
        place_ref,
        near_ref,
        far_ref,
        *refs,
    ):
        sums_refs = refs[:-7]
        whitener_ref, mean_ref, scaled, rest, first, left, right = refs[-7:]
        place = place_ref[0]
        embed = scaled.shape[0]
        blocks = embed // LANES
        half = blocks // 2
        pieces, depth = near_ref.shape[:2]
        per_block = LANES // depth
        totals = jnp.concatenate(
            [
                unpack_sums(ref[start : start + 4 * count, :], count, embed)
                for ref in sums_refs
                for start in range(depth, ref.shape[0], 4 * count)
            ],
            axis=0,
        )
        total_rows = rows * totals.shape[0]
        tile = 512
        tiles = embed // tile

        mean = jnp.sum(totals, axis=0, keepdims=True) * (1.0 / total_rows)
        mean_ref[...] = mean
        shift_high, shift_low = split(totals * (1.0 / rows) - mean)
        shift_left = jnp.concatenate([shift_high, shift_high, shift_low], axis=0)
        shift_right = jnp.concatenate([shift_high, shift_low, shift_high], axis=0)

        def unpack(source_ref, side):
            for i in range(side * half, (side + 1) * half):
                for part in range(per_block):
                    piece = ((i - side * half) * per_block + part) ^ (place % pieces)
                    wide = source_ref[piece].astype(F32)
                    lines = pl.ds(i * LANES + part * depth, depth)
                    for k in range(half + 1):
                        if k == half and side:
                            continue
                        j = (i + k) % blocks
                        scaled[lines, j * LANES : (j + 1) * LANES] = wide[
                            :, k * LANES : (k + 1) * LANES
                        ]

        for core in range(2):

            @pl.when(place // pieces == core)
            def _():
                unpack(near_ref, core)
                unpack(far_ref, 1 - core)

        for i in range(blocks):
            for k in range(1, half + 1):
                if k == half and i >= half:
                    continue
                j = (i + k) % blocks
                scaled[j * LANES : (j + 1) * LANES, i * LANES : (i + 1) * LANES] = scaled[
                    i * LANES : (i + 1) * LANES, j * LANES : (j + 1) * LANES
                ].T
        squares = jnp.zeros((1, embed), F32)
        for t in range(tiles):
            lines = slice(t * tile, (t + 1) * tile)
            between = dot(shift_left[:, lines], shift_right, (0, 0))
            covariance = (scaled[lines, :] + rows * between) * (1.0 / total_rows)
            scaled[lines, :] = covariance
            first[lines, :] = covariance.astype(BF16)
            squares = squares + jnp.sum(covariance * covariance, axis=0, keepdims=True)
        frobenius = jnp.sqrt(jnp.sum(squares, axis=1, keepdims=True))
        inverse = 1.0 / frobenius
        root = lax.rsqrt(frobenius)

        def product(one, two, finish):
            @pl.loop(0, tiles)
            def _(t):
                lines = pl.ds(pl.multiple_of(t * tile, tile), tile)
                finish(lines, dot(one[lines, :], two[...]))

        def second(lines, value):
            value = value * (inverse * inverse)
            own = scaled[lines, :] * inverse
            scaled[lines, :] = own
            rest[lines, :] = 27.0 * value - 39.0 * own
            left[lines, :] = value.astype(BF16)
            right[lines, :] = (value - 9.0 * own).astype(BF16)

        product(first, first, second)

        def fourth(lines, value):
            value = (value + rest[lines, :]) * (1.0 / 16.0)
            rest[lines, :] = value
            whitener_ref[lines, :] = value.astype(BF16)

        product(left, right, fourth)

        def moved(lines, value):
            value = value * inverse
            scaled[lines, :] = 2.25 * 2.25 * scaled[lines, :] + 4.5 * value
            right[lines, :] = value.astype(BF16)

        product(first, whitener_ref, moved)

        def quad(lines, value):
            value = value + scaled[lines, :]
            rest[lines, :] = 3.0 * rest[lines, :] - 2.25 * value
            left[lines, :] = value.astype(BF16)

        product(whitener_ref, right, quad)
        first[...] = whitener_ref[...]

        def last(lines, value):
            at = lax.broadcasted_iota(jnp.int32, value.shape, 0) + lines.start
            eye = at == lax.broadcasted_iota(jnp.int32, value.shape, 1)
            value = 0.5 * (rest[lines, :] - value)
            value = value + jnp.where(eye, 0.5 * 3.0 * 2.25, 0.0)
            whitener_ref[lines, :] = (value * root).astype(BF16)

        product(first, left, last)

    return kernel


def whiten(place, near, far, sums, count, rows, embed):
    square = (embed, embed)
    return pl.pallas_call(
        make_whiten_kernel(rows, count),
        in_specs=[smem()] + [vmem()] * (2 + len(sums)),
        out_specs=[vmem(), vmem()],
        out_shape=[
            jax.ShapeDtypeStruct(square, BF16),
            jax.ShapeDtypeStruct((1, embed), F32),
        ],
        scratch_shapes=[pltpu.VMEM(square, F32)] * 2 + [pltpu.VMEM(square, BF16)] * 3,
        compiler_params=params(24),
        cost_estimate=pl.CostEstimate(
            flops=5 * 2 * embed**3, bytes_accessed=2 * embed**2, transcendentals=0
        ),
        name="whiten",
    )(place, near, far, *sums)


def contrast_kernel(order, group_ref, mean_ref, whitener_ref, *refs):
    loss_ref, grad_ref, white, tables, numbers, offsets_ref, sem = refs[-11:-4]
    even, odd = (refs[-4], refs[-3]), (refs[-2], refs[-1])
    block_refs = [ref.at[i] for ref in refs[:-11] for i in range(ref.shape[0])]
    block_refs = [block_refs[order.index(k)] for k in range(len(order))]
    groups, rows, embed = white.shape
    group = group_ref[0]

    for k in range(0, groups, 2):
        pair = block_refs[k : k + 2]
        centered = [(ref[0:rows, :].astype(F32) - mean_ref[...]).astype(BF16) for ref in pair]
        value = dot(jnp.concatenate(centered, axis=0), whitener_ref[...]).astype(BF16)
        for side, ref in enumerate(pair):
            white[group ^ (k + side)] = value[side * rows : (side + 1) * rows]
            table = ref[rows:, :].astype(F32)[0:8]
            tables[group ^ (k + side)] = table
            numbers[group ^ (k + side)] = table[:, 0:LANES].astype(jnp.int32)
    copy = pltpu.make_async_copy(numbers, offsets_ref, sem)
    copy.start()
    copy.wait()

    places = lax.broadcasted_iota(jnp.int32, (rows, rows), 0).astype(F32)
    log2e = 1.4426950408889634

    def partner(g, k):
        return white[(g + offsets_ref[g, 1, k]) % groups]

    def scores(g, buffers):
        own = white[g]
        for k in range(PARTNERS):
            buffers[0][k * rows : (k + 1) * rows, :] = dot(partner(g, k), own, (1, 1))

    def softmax(g, buffers):
        loss = jnp.zeros((1, rows), F32)
        for k in range(PARTNERS):
            at = slice(k * rows, (k + 1) * rows)
            own = buffers[0][at, :]
            peak = jnp.max(own, axis=0, keepdims=True)
            powers = jnp.exp2((own - peak) * (LOGIT_SCALE * log2e))
            sums = jnp.sum(powers, axis=0, keepdims=True)
            hit = places == tables[g, 0:1, at]
            picked = jnp.sum(jnp.where(hit, own, 0.0), axis=0, keepdims=True)
            loss = loss + ((peak - picked) * LOGIT_SCALE + jnp.log(sums))
            share = powers * (1.0 / (PARTNERS * sums))
            weights = share - jnp.where(hit, 1.0 / PARTNERS, 0.0)
            buffers[1][at, :] = weights.astype(BF16)
        return loss * (1.0 / PARTNERS)

    def gradient(g, buffers):
        grad = dot(buffers[1][0:rows, :], partner(g, 0), (0, 0))
        for k in range(1, PARTNERS):
            grad = grad + dot(buffers[1][k * rows : (k + 1) * rows, :], partner(g, k), (0, 0))
        grad_ref[g] = (grad * LOGIT_SCALE).astype(BF16)

    scores(0, even)

    @pl.loop(0, groups // 2)
    def _(pair):
        g = 2 * pair
        scores(g + 1, odd)
        first = softmax(g, even)
        gradient(g, even)
        second = softmax(g + 1, odd)
        scores(lax.rem(g + 2, groups), even)
        gradient(g + 1, odd)

        @pl.when(pair == group // 2)
        def _():
            loss_ref[...] = jnp.where(group % 2 == 0, first, second)


def contrast(group, blocks, order, mean, whitener):
    groups = len(order)
    rows, embed = blocks[0].shape[1:]
    rows -= TAIL
    return pl.pallas_call(
        functools.partial(contrast_kernel, order),
        in_specs=[smem()] + [vmem()] * (2 + len(blocks)),
        out_specs=[vmem()] * 2,
        out_shape=[
            jax.ShapeDtypeStruct((1, rows), F32),
            jax.ShapeDtypeStruct((groups, rows, embed), BF16),
        ],
        scratch_shapes=[
            pltpu.VMEM((groups, rows, embed), BF16),
            pltpu.VMEM((groups, 8, embed), F32),
            pltpu.VMEM((groups, 8, LANES), jnp.int32),
            pltpu.SMEM((groups, 8, LANES), jnp.int32),
            pltpu.SemaphoreType.DMA,
        ]
        + [pltpu.VMEM((PARTNERS * rows, rows), F32), pltpu.VMEM((PARTNERS * rows, rows), BF16)] * 2,
        compiler_params=params(min(58, 12 + 6 * groups * rows * embed // 2**20)),
        cost_estimate=pl.CostEstimate(
            flops=groups * rows * 2 * embed * (embed + 2 * PARTNERS * rows),
            bytes_accessed=4 * groups * rows * embed,
            transcendentals=groups * PARTNERS * rows * rows,
        ),
        name="contrast",
    )(group, mean, whitener, *blocks)


def pieces_kernel(share, masks, group_ref, window_ref, grad_ref, *refs):
    groups = grad_ref.shape[0]
    features, (keep_ref, send_ref, total) = refs[:groups], refs[groups:]

    def columns(at):
        value = dot(features[0][:, at], grad_ref[group_ref[0]], (0, 0))
        for k in range(1, groups):
            value = value + dot(features[k][:, at], grad_ref[group_ref[0] ^ k], (0, 0))
        return value

    if share % LANES:
        total[...] = columns(slice(None))
    for n, mask in enumerate(masks):
        at = pl.ds(pl.multiple_of((window_ref[0] ^ mask) * share, share), share)
        value = total[at, :] if share % LANES else columns(at)
        out, n = (send_ref, n - len(masks) // 2) if n >= len(masks) // 2 else (keep_ref, n)
        out[n * share : (n + 1) * share, :] = value.astype(out.dtype)


def weight_pieces(group, window, grad, slices, shares, masks):
    groups, rows, embed = grad.shape
    columns = slices[0].shape[1]
    share = columns // shares
    half = len(masks) // 2 * share
    return pl.pallas_call(
        functools.partial(pieces_kernel, share, masks),
        in_specs=[smem(), smem()] + [vmem()] * (1 + len(slices)),
        out_specs=[vmem()] * 2,
        out_shape=[
            jax.ShapeDtypeStruct((half, embed), F32),
            jax.ShapeDtypeStruct((half, embed), BF16),
        ],
        scratch_shapes=[pltpu.VMEM((columns if share % LANES else 8, embed), F32)],
        compiler_params=params(24),
        cost_estimate=pl.CostEstimate(
            flops=groups * rows * 2 * embed * share * len(masks),
            bytes_accessed=2 * groups * rows * (embed + columns),
            transcendentals=0,
        ),
        name="weight_pieces",
    )(group, window, grad, *slices)


def join_kernel(keep_ref, arrived_ref, out_ref):
    out_ref[...] = (keep_ref[...] + arrived_ref[...].astype(F32)).astype(BF16)


def join(keep, arrived):
    return pl.pallas_call(
        join_kernel,
        in_specs=[vmem()] * 2,
        out_specs=vmem(),
        out_shape=jax.ShapeDtypeStruct(keep.shape, BF16),
        compiler_params=params(8),
        name="join",
    )(keep, arrived)


def finish_kernel(*refs):
    keep_ref, whitener_ref, out_ref = refs[0], refs[-2], refs[-1]
    value = keep_ref[...]
    for ref in refs[1:-2]:
        value = value + ref[...].astype(F32)
    high, low = split(value)
    both = dot(jnp.concatenate([high, low], axis=0), whitener_ref[...], (1, 1))
    out_ref[...] = both[: value.shape[0]] + both[value.shape[0] :]


def finish(pieces, whitener):
    return pl.pallas_call(
        finish_kernel,
        in_specs=[vmem()] * (len(pieces) + 1),
        out_specs=vmem(),
        out_shape=jax.ShapeDtypeStruct(pieces[0].shape, F32),
        compiler_params=params(12),
        name="finish",
    )(*pieces, whitener)


def shards(features, proj_weight, partner_offsets, ortholog_index):
    rows, depth = features.shape
    embed = proj_weight.shape[1]
    groups = lax.axis_size("sp")
    shares = lax.axis_size("win")
    devices = groups * shares
    group = lax.axis_index("sp").astype(jnp.int32)
    window = lax.axis_index("win").astype(jnp.int32)
    me = group * shares + window

    direct = groups == 8
    by_x, by_near, by_far = shares, 2 * shares, 4 * shares
    if not direct:
        slices = features.reshape(rows, groups, depth // groups).transpose(1, 0, 2)
        slices = lax.all_to_all(slices, "sp", 0, 0)
        slices = [
            lax.dynamic_index_in_dim(slices, group ^ k, 0, keepdims=False) for k in range(groups)
        ]

    block, send, keep = project(
        me.reshape(1), partner_offsets, features, proj_weight, ortholog_index.T
    )
    block = block[None]
    if direct:
        block_far = xor_permute(block, by_far)
        block_near = xor_permute(block, by_near)
    else:
        gathered = lax.all_gather(block, "sp", tiled=True)

    arrived = [xor_permute(send, 1)]
    sent = send
    seen = 1
    stages = []
    low = 1
    place = me & 1
    while keep.shape[0] > 32:
        count = 4
        own = (me >> low) & (count - 1)
        keep, sends, seen = stage(own, keep, sent, arrived, seen, count, embed)
        if direct and stages:
            group_scalar = group.reshape(1)
            *sends, block_far, block_near, group_scalar = lax.optimization_barrier(
                (*sends, block_far, block_near, group_scalar)
            )
            slices = cut(group_scalar, features, groups)
            pair_x = xor_permute(jnp.concatenate([block, block_near]), by_x)
        arrived = [xor_permute(piece, (r + 1) << low) for r, piece in enumerate(sends)]
        sent = sends[0]
        stages.append((low, count))
        place = place * count + own
        low += 2
    size = keep.shape[0]
    part = keep
    for piece in arrived:
        part = part + piece[:size].astype(F32)
    sums = [sent, *arrived]
    extra = devices >> low
    if extra > 1:
        mine = jnp.concatenate([part.astype(BF16)] + [piece[size:] for piece in sums])
        others = [xor_permute(mine, r << low) for r in range(1, extra)]
        for piece in others:
            part = part + piece[:size].astype(F32)
        sums = [mine, *others]
    part = part.astype(BF16)
    for number, (low, count) in enumerate(reversed(stages)):
        if direct and number == 1:
            part, pair_x, block_far = lax.optimization_barrier((part, pair_x, block_far))
            block_far_near = xor_permute(block_far, by_near)
        part = jnp.concatenate(
            [part] + [xor_permute(part, r << low) for r in range(1, count)], axis=0
        )
    part = part.reshape(-1, size, part.shape[1])
    if direct:
        part, block_far_near, *slices = lax.optimization_barrier((part, block_far_near, *slices))
        far_x = xor_permute(jnp.concatenate([block_far, block_far_near]), by_x)
        blocks = [block, block_near, pair_x, block_far, block_far_near, far_x]
        order = [0, 2, 1, 3, 4, 6, 5, 7]
        slices = list(slices)
        for k in (2, 4, 6, 1, 3, 5, 7):
            slices[k] = xor_permute(slices[k], k * shares)
    else:
        order = list(range(groups))
        blocks = [
            lax.dynamic_index_in_dim(gathered, group ^ k, 0, keepdims=True) for k in order
        ]
    other = xor_permute(part, 1)

    whitener, mean = whiten(place.reshape(1), part, other, sums, seen, rows, embed)
    loss, grad = contrast(group.reshape(1), blocks, order, mean, whitener)
    group, window = group.reshape(1), window.reshape(1)
    pieces = []
    for mask in reversed(range(0, shares, 2)):
        keep, send = weight_pieces(group, window, grad, slices, shares, (mask, mask + 1))
        arrived = xor_permute(send, 1)
        if mask:
            pieces.append(xor_permute(join(keep, arrived), mask))
        else:
            pieces = [keep, arrived] + pieces
    return loss[0], finish(pieces, whitener)


def solution(mesh):
    return jax.shard_map(
        shards,
        mesh=mesh,
        in_specs=(P(("sp", "win"), None), P(), P("sp", None), P(("sp", "win"), None)),
        out_specs=(P(("sp", "win")), P(("sp", "win"), None)),
        check_vma=False,
    )
```

```python
import functools

import jax
import jax.numpy as jnp
from jax import lax
from jax.experimental import pallas as pl
from jax.experimental.pallas import tpu as pltpu
from jax.sharding import PartitionSpec as P

PARTNERS = 4
LOGIT_SCALE = 0.125
AXES = ("sp", "win")
LANES = 128
TAIL = 16
CHUNKS = 8
F32 = jnp.float32
BF16 = jnp.bfloat16
HIGHEST = lax.Precision.HIGHEST


def dot(a, b, contract=(1, 0), precision=None):
    return lax.dot_general(
        a,
        b,
        (((contract[0],), (contract[1],)), ((), ())),
        precision=precision,
        preferred_element_type=F32,
    )


def params(mebibytes, semantics=None):
    return pltpu.CompilerParams(
        vmem_limit_bytes=mebibytes * 2**20, dimension_semantics=semantics
    )


def vmem():
    return pl.BlockSpec(memory_space=pltpu.VMEM)


def smem():
    return pl.BlockSpec(memory_space=pltpu.SMEM)


def xor_permute(piece, mask):
    devices = lax.axis_size(AXES)
    return lax.ppermute(piece, AXES, [(i, i ^ mask) for i in range(devices)])


def split(value):
    high = value.astype(BF16)
    return high, (value - high.astype(F32)).astype(BF16)


def cut_kernel(group_ref, features_hbm, *refs):
    outs, sems = refs[:-1], refs[-1]
    columns = outs[0].shape[1]
    copies = []
    for k, out in enumerate(outs):
        start = pl.multiple_of((group_ref[0] ^ k) * columns, columns)
        copies.append(
            pltpu.make_async_copy(features_hbm.at[:, pl.ds(start, columns)], out, sems.at[k])
        )
        copies[k].start()
    for copy in copies:
        copy.wait()


def cut(group, features, groups):
    rows, depth = features.shape
    return pl.pallas_call(
        cut_kernel,
        in_specs=[smem(), pl.BlockSpec(memory_space=pltpu.HBM)],
        out_specs=[pl.BlockSpec(memory_space=pltpu.HBM)] * groups,
        out_shape=[jax.ShapeDtypeStruct((rows, depth // groups), BF16)] * groups,
        scratch_shapes=[pltpu.SemaphoreType.DMA((groups,))],
        compiler_params=params(8),
        name="cut",
    )(group, features)


def pack_sums(sums, packed, rows):
    high = sums.astype(BF16).astype(F32)
    pad = jnp.zeros((sums.shape[0], 2 * packed - sums.shape[1]), F32)
    lines = []
    for half in (high, sums - high):
        lines += [half[:, :packed], jnp.concatenate([half[:, packed:], pad], axis=1)]
    if rows > 4 * sums.shape[0]:
        lines.append(jnp.zeros((rows - 4 * sums.shape[0], packed), F32))
    return jnp.concatenate(lines, axis=0).astype(BF16)


def unpack_sums(block, count, embed):
    wide = block.astype(F32)
    packed = wide.shape[1]
    low = 2 * count
    left = wide[0:count] + wide[low : low + count]
    right = wide[count:low] + wide[low + count : low + 2 * count]
    return jnp.concatenate([left, right[:, : embed - packed]], axis=1)


def project_kernel(
    me_ref,
    offsets_ref,
    features_hbm,
    weight_hbm,
    ortholog_hbm,
    block_ref,
    send_ref,
    keep_ref,
    features_ref,
    weight_ref,
    ortholog_ref,
    means,
    wide,
    sems,
):
    rows = features_ref.shape[0]
    depth, embed = weight_ref.shape
    half, packed = keep_ref.shape
    blocks = embed // LANES
    tile = depth // CHUNKS

    copies = []
    for n in range(CHUNKS):
        at = pl.ds(n * tile, tile)
        copies.append(
            (
                pltpu.make_async_copy(features_hbm.at[:, at], features_ref.at[:, at], sems.at[0, n]),
                pltpu.make_async_copy(weight_hbm.at[at, :], weight_ref.at[at, :], sems.at[1, n]),
            )
        )
        for copy in copies[-1]:
            copy.start()
    table_copy = pltpu.make_async_copy(ortholog_hbm, ortholog_ref, sems.at[0, CHUNKS])
    table_copy.start()

    total = jnp.zeros((rows, embed), F32)
    for n in range(CHUNKS):
        for copy in copies[n]:
            copy.wait()
        at = slice(n * tile, (n + 1) * tile)
        total = total + dot(features_ref[:, at], weight_ref[at, :])
    projected = total.astype(BF16)
    block_ref[0:rows, :] = projected

    table_copy.wait()
    line = lax.broadcasted_iota(jnp.int32, (TAIL, embed), 0)
    lane = lax.broadcasted_iota(jnp.int32, (TAIL, embed), 1)
    table = jnp.zeros((TAIL, embed), F32)
    for k in range(PARTNERS):
        table = jnp.where((line == 1) & (lane == k), offsets_ref[0, k].astype(F32), table)
    hits = jnp.concatenate(
        [ortholog_ref[k : k + 1, :].astype(F32) for k in range(PARTNERS)]
        + ([jnp.zeros((1, embed - PARTNERS * rows), F32)] if embed > PARTNERS * rows else []),
        axis=1,
    )
    block_ref[rows:, :] = jnp.where(line == 0, hits, table).astype(BF16)

    sums = jnp.sum(projected.astype(F32), axis=0, keepdims=True)
    send_ref[half:, :] = pack_sums(sums, packed, TAIL)
    wide[:, :embed] = projected
    wide[:, embed:] = projected[:, : packed - LANES]
    ones = jnp.ones((rows, LANES), BF16)
    means[...] = jnp.broadcast_to(sums * (1.0 / rows), means.shape)
    core = me_ref[0] & 1
    for side, out in ((1, send_ref), (0, keep_ref)):
        for r in range(blocks // 2):
            block = (core ^ side) * (blocks // 2) + r
            start = pl.multiple_of(block * LANES, LANES)
            own = wide[:, pl.ds(start, LANES)]
            gram = dot(own, wide[:, pl.ds(start, packed)], (0, 0))
            sums = dot(own, ones, (0, 0))
            for k in range(packed // LANES):
                other = pl.multiple_of((block + k) % blocks * LANES, LANES)
                at = slice(k * LANES, (k + 1) * LANES)
                value = gram[:, at] - sums * means[0:1, pl.ds(other, LANES)]
                out[r * LANES : (r + 1) * LANES, at] = value.astype(out.dtype)


def project(me, offsets, features, weight, ortholog):
    rows, depth = features.shape
    embed = weight.shape[1]
    packed = embed // 2 + LANES
    hbm = pl.BlockSpec(memory_space=pltpu.HBM)
    return pl.pallas_call(
        project_kernel,
        in_specs=[smem(), smem(), hbm, hbm, hbm],
        out_specs=[vmem()] * 3,
        out_shape=[
            jax.ShapeDtypeStruct((rows + TAIL, embed), BF16),
            jax.ShapeDtypeStruct((embed // 2 + TAIL, packed), BF16),
            jax.ShapeDtypeStruct((embed // 2, packed), F32),
        ],
        scratch_shapes=[
            pltpu.VMEM((rows, depth), BF16),
            pltpu.VMEM((depth, embed), BF16),
            pltpu.VMEM((PARTNERS, rows), jnp.int32),
            pltpu.VMEM((8, embed), F32),
            pltpu.VMEM((rows, embed + packed - LANES), BF16),
            pltpu.SemaphoreType.DMA((2, CHUNKS + 1)),
        ],
        compiler_params=params(51),
        cost_estimate=pl.CostEstimate(
            flops=2 * rows * depth * embed, bytes_accessed=2 * depth * embed, transcendentals=0
        ),
        name="project",
    )(me, offsets, features, weight, ortholog)


def make_stage_kernel(seen, arrivals, count, embed):
    def kernel(own_ref, keep_ref, sent_ref, *refs):
        arrived, next_keep, outs = refs[:arrivals], refs[arrivals], refs[arrivals + 1 :]
        full, packed = keep_ref.shape
        share = full // count
        own = own_ref[0]
        sums = [unpack_sums(ref[full:, :], seen, embed) for ref in (sent_ref, *arrived)]
        block = pack_sums(jnp.concatenate(sums, axis=0), packed, outs[0].shape[0] - share)
        for r in range(count):
            at = pl.ds(pl.multiple_of((own ^ r) * share, share), share)
            value = keep_ref[at, :]
            for ref in arrived:
                value = value + ref[at, :].astype(F32)
            if r == 0:
                next_keep[...] = value
            else:
                outs[r - 1][:share, :] = value.astype(BF16)
                outs[r - 1][share:, :] = block

    return kernel


def stage(own, keep, sent, arrived, seen, count, embed):
    full, packed = keep.shape
    share = full // count
    held = seen * (1 + len(arrived))
    tail = -(-4 * held // TAIL) * TAIL
    out = pl.pallas_call(
        make_stage_kernel(seen, len(arrived), count, embed),
        in_specs=[smem()] + [vmem()] * (2 + len(arrived)),
        out_specs=[vmem()] * count,
        out_shape=[jax.ShapeDtypeStruct((share, packed), F32)]
        + [jax.ShapeDtypeStruct((share + tail, packed), BF16)] * (count - 1),
        compiler_params=params(16),
        cost_estimate=pl.CostEstimate(
            flops=full * packed, bytes_accessed=4 * full * packed, transcendentals=0
        ),
        name="stage",
    )(own.reshape(1), keep, sent, *arrived)
    return out[0], out[1:], held


def make_whiten_kernel(rows, count):
    def kernel(
        place_ref,
        near_ref,
        far_ref,
        *refs,
    ):
        sums_refs = refs[:-7]
        whitener_ref, mean_ref, scaled, rest, first, left, right = refs[-7:]
        place = place_ref[0]
        embed = scaled.shape[0]
        blocks = embed // LANES
        half = blocks // 2
        pieces, depth = near_ref.shape[:2]
        per_block = LANES // depth
        totals = jnp.concatenate(
            [
                unpack_sums(ref[start : start + 4 * count, :], count, embed)
                for ref in sums_refs
                for start in range(depth, ref.shape[0], 4 * count)
            ],
            axis=0,
        )
        total_rows = rows * totals.shape[0]
        tile = 256

        mean = jnp.sum(totals, axis=0, keepdims=True) * (1.0 / total_rows)
        mean_ref[...] = mean
        shift_high, shift_low = split(totals * (1.0 / rows) - mean)
        shift_left = jnp.concatenate([shift_high, shift_high, shift_low], axis=0)
        shift_right = jnp.concatenate([shift_high, shift_low, shift_high], axis=0)

        def block_at(i, j):
            return slice(i * LANES, (i + 1) * LANES), slice(j * LANES, (j + 1) * LANES)

        def unpack(source_ref, side):
            for i in range(side * half, (side + 1) * half):
                for part in range(per_block):
                    piece = ((i - side * half) * per_block + part) ^ (place % pieces)
                    wide = source_ref[piece].astype(F32)
                    lines = pl.ds(i * LANES + part * depth, depth)
                    for k in range(half + 1):
                        if k == half and side:
                            continue
                        j = (i + k) % blocks
                        scaled[lines, j * LANES : (j + 1) * LANES] = wide[
                            :, k * LANES : (k + 1) * LANES
                        ]

        for core in range(2):

            @pl.when(place // pieces == core)
            def _():
                unpack(near_ref, core)
                unpack(far_ref, 1 - core)

        for i in range(blocks):
            for j in range(blocks):
                held = (j - i) % blocks < half or ((j - i) % blocks == half and i < half)
                if not held and i * LANES // tile <= j * LANES // tile:
                    scaled[block_at(i, j)] = scaled[block_at(j, i)].T

        panels = []
        for t in range(embed // tile):
            panels.append((slice(0, (t + 1) * tile), slice(t * tile, (t + 1) * tile)))

        def mirror(out, panel, value):
            rows_at, columns_at = panel
            value = value.astype(BF16)
            out[panel] = value
            above = columns_at.start
            if above:
                out[columns_at, 0:above] = value[0:above].T

        squares = jnp.zeros((1, tile), F32)
        for panel in panels:
            rows_at, columns_at = panel
            between = dot(shift_left[:, rows_at], shift_right[:, columns_at], (0, 0))
            covariance = (scaled[panel] + rows * between) * (1.0 / total_rows)
            scaled[panel] = covariance
            mirror(first, panel, covariance)
            above = columns_at.start
            square = covariance * covariance
            squares = squares + jnp.sum(square[above:], axis=0, keepdims=True)
            if above:
                squares = squares + 2.0 * jnp.sum(square[:above], axis=0, keepdims=True)
        frobenius = jnp.sqrt(jnp.sum(squares, axis=1, keepdims=True))
        inverse = 1.0 / frobenius
        root = lax.rsqrt(frobenius)

        def product(one, two, finish):
            for panel in panels:
                finish(panel, dot(one[panel[0], :], two[:, panel[1]]))

        def second(panel, value):
            value = value * (inverse * inverse)
            own = scaled[panel] * inverse
            scaled[panel] = own
            rest[panel] = 27.0 * value - 39.0 * own
            mirror(left, panel, value)
            mirror(right, panel, value - 9.0 * own)

        product(first, first, second)

        def fourth(panel, value):
            value = (value + rest[panel]) * (1.0 / 16.0)
            rest[panel] = value
            mirror(whitener_ref, panel, value)

        product(left, right, fourth)

        def moved(panel, value):
            value = value * inverse
            scaled[panel] = 2.25 * 2.25 * scaled[panel] + 4.5 * value
            mirror(right, panel, value)

        product(first, whitener_ref, moved)

        def quad(panel, value):
            value = value + scaled[panel]
            rest[panel] = 3.0 * rest[panel] - 2.25 * value
            mirror(left, panel, value)

        product(whitener_ref, right, quad)
        first[...] = whitener_ref[...]

        def last(panel, value):
            at = lax.broadcasted_iota(jnp.int32, value.shape, 0)
            eye = at == lax.broadcasted_iota(jnp.int32, value.shape, 1) + panel[1].start
            value = 0.5 * (rest[panel] - value)
            value = value + jnp.where(eye, 0.5 * 3.0 * 2.25, 0.0)
            mirror(whitener_ref, panel, value * root)

        product(first, left, last)

    return kernel


def whiten(place, near, far, sums, count, rows, embed):
    square = (embed, embed)
    return pl.pallas_call(
        make_whiten_kernel(rows, count),
        in_specs=[smem()] + [vmem()] * (2 + len(sums)),
        out_specs=[vmem(), vmem()],
        out_shape=[
            jax.ShapeDtypeStruct(square, BF16),
            jax.ShapeDtypeStruct((1, embed), F32),
        ],
        scratch_shapes=[pltpu.VMEM(square, F32)] * 2 + [pltpu.VMEM(square, BF16)] * 3,
        compiler_params=params(24),
        cost_estimate=pl.CostEstimate(
            flops=5 * 2 * embed**3, bytes_accessed=2 * embed**2, transcendentals=0
        ),
        name="whiten",
    )(place, near, far, *sums)


def contrast_kernel(order, group_ref, mean_ref, whitener_ref, *refs):
    loss_ref, grad_ref, white, tables, numbers, offsets_ref, sem = refs[-11:-4]
    even, odd = (refs[-4], refs[-3]), (refs[-2], refs[-1])
    block_refs = [ref.at[i] for ref in refs[:-11] for i in range(ref.shape[0])]
    block_refs = [block_refs[order.index(k)] for k in range(len(order))]
    groups, rows, embed = white.shape
    group = group_ref[0]

    for k in range(0, groups, 2):
        pair = block_refs[k : k + 2]
        centered = [(ref[0:rows, :].astype(F32) - mean_ref[...]).astype(BF16) for ref in pair]
        value = dot(jnp.concatenate(centered, axis=0), whitener_ref[...]).astype(BF16)
        for side, ref in enumerate(pair):
            white[group ^ (k + side)] = value[side * rows : (side + 1) * rows]
            table = ref[rows:, :].astype(F32)[0:8]
            tables[group ^ (k + side)] = table
            numbers[group ^ (k + side)] = table[:, 0:LANES].astype(jnp.int32)
    copy = pltpu.make_async_copy(numbers, offsets_ref, sem)
    copy.start()
    copy.wait()

    places = lax.broadcasted_iota(jnp.int32, (rows, rows), 0).astype(F32)
    log2e = 1.4426950408889634

    def partner(g, k):
        return white[(g + offsets_ref[g, 1, k]) % groups]

    def scores(g, buffers):
        own = white[g]
        for k in range(PARTNERS):
            buffers[0][k * rows : (k + 1) * rows, :] = dot(partner(g, k), own, (1, 1))

    def softmax(g, buffers):
        loss = jnp.zeros((1, rows), F32)
        for k in range(PARTNERS):
            at = slice(k * rows, (k + 1) * rows)
            own = buffers[0][at, :]
            peak = jnp.max(own, axis=0, keepdims=True)
            powers = jnp.exp2((own - peak) * (LOGIT_SCALE * log2e))
            sums = jnp.sum(powers, axis=0, keepdims=True)
            hit = places == tables[g, 0:1, at]
            picked = jnp.sum(jnp.where(hit, own, 0.0), axis=0, keepdims=True)
            loss = loss + ((peak - picked) * LOGIT_SCALE + jnp.log(sums))
            share = powers * (1.0 / (PARTNERS * sums))
            weights = share - jnp.where(hit, 1.0 / PARTNERS, 0.0)
            buffers[1][at, :] = weights.astype(BF16)
        return loss * (1.0 / PARTNERS)

    def gradient(g, buffers):
        grad = dot(buffers[1][0:rows, :], partner(g, 0), (0, 0))
        for k in range(1, PARTNERS):
            grad = grad + dot(buffers[1][k * rows : (k + 1) * rows, :], partner(g, k), (0, 0))
        grad_ref[g] = (grad * LOGIT_SCALE).astype(BF16)

    scores(0, even)

    @pl.loop(0, groups // 2)
    def _(pair):
        g = 2 * pair
        scores(g + 1, odd)
        first = softmax(g, even)
        gradient(g, even)
        second = softmax(g + 1, odd)
        scores(lax.rem(g + 2, groups), even)
        gradient(g + 1, odd)

        @pl.when(pair == group // 2)
        def _():
            loss_ref[...] = jnp.where(group % 2 == 0, first, second)


def contrast(group, blocks, order, mean, whitener):
    groups = len(order)
    rows, embed = blocks[0].shape[1:]
    rows -= TAIL
    return pl.pallas_call(
        functools.partial(contrast_kernel, order),
        in_specs=[smem()] + [vmem()] * (2 + len(blocks)),
        out_specs=[vmem()] * 2,
        out_shape=[
            jax.ShapeDtypeStruct((1, rows), F32),
            jax.ShapeDtypeStruct((groups, rows, embed), BF16),
        ],
        scratch_shapes=[
            pltpu.VMEM((groups, rows, embed), BF16),
            pltpu.VMEM((groups, 8, embed), F32),
            pltpu.VMEM((groups, 8, LANES), jnp.int32),
            pltpu.SMEM((groups, 8, LANES), jnp.int32),
            pltpu.SemaphoreType.DMA,
        ]
        + [pltpu.VMEM((PARTNERS * rows, rows), F32), pltpu.VMEM((PARTNERS * rows, rows), BF16)] * 2,
        compiler_params=params(min(58, 12 + 6 * groups * rows * embed // 2**20)),
        cost_estimate=pl.CostEstimate(
            flops=groups * rows * 2 * embed * (embed + 2 * PARTNERS * rows),
            bytes_accessed=4 * groups * rows * embed,
            transcendentals=groups * PARTNERS * rows * rows,
        ),
        name="contrast",
    )(group, mean, whitener, *blocks)


def pieces_kernel(share, masks, order, group_ref, window_ref, grad_ref, *refs):
    groups = grad_ref.shape[0]
    features, (keep_ref, send_ref, total) = refs[:groups], refs[groups:]

    def columns(at):
        value = None
        for k, feature_ref in zip(order, features):
            term = dot(feature_ref[:, at], grad_ref[group_ref[0] ^ k], (0, 0))
            value = term if value is None else value + term
        return value

    if share % LANES:
        total[...] = columns(slice(None))
    for n, mask in enumerate(masks):
        at = pl.ds(pl.multiple_of((window_ref[0] ^ mask) * share, share), share)
        value = total[at, :] if share % LANES else columns(at)
        out, n = (send_ref, n - len(masks) // 2) if n >= len(masks) // 2 else (keep_ref, n)
        out[n * share : (n + 1) * share, :] = value.astype(out.dtype)


def weight_pieces(group, window, grad, slices, order, shares, masks):
    groups, rows, embed = grad.shape
    columns = slices[0].shape[1]
    share = columns // shares
    half = len(masks) // 2 * share
    return pl.pallas_call(
        functools.partial(pieces_kernel, share, masks, order),
        in_specs=[smem(), smem()] + [vmem()] * (1 + len(slices)),
        out_specs=[vmem()] * 2,
        out_shape=[
            jax.ShapeDtypeStruct((half, embed), F32),
            jax.ShapeDtypeStruct((half, embed), BF16),
        ],
        scratch_shapes=[pltpu.VMEM((columns if share % LANES else 8, embed), F32)],
        compiler_params=params(24),
        cost_estimate=pl.CostEstimate(
            flops=groups * rows * 2 * embed * share * len(masks),
            bytes_accessed=2 * groups * rows * (embed + columns),
            transcendentals=0,
        ),
        name="weight_pieces",
    )(group, window, grad, *slices)


def join_kernel(keep_ref, arrived_ref, out_ref):
    out_ref[...] = (keep_ref[...] + arrived_ref[...].astype(F32)).astype(BF16)


def join(keep, arrived):
    return pl.pallas_call(
        join_kernel,
        in_specs=[vmem()] * 2,
        out_specs=vmem(),
        out_shape=jax.ShapeDtypeStruct(keep.shape, BF16),
        compiler_params=params(8),
        name="join",
    )(keep, arrived)


def finish_kernel(*refs):
    keep_ref, whitener_ref, out_ref = refs[0], refs[-2], refs[-1]
    value = keep_ref[...]
    for ref in refs[1:-2]:
        value = value + ref[...].astype(F32)
    high, low = split(value)
    both = dot(jnp.concatenate([high, low], axis=0), whitener_ref[...], (1, 1))
    out_ref[...] = both[: value.shape[0]] + both[value.shape[0] :]


def finish(pieces, whitener):
    return pl.pallas_call(
        finish_kernel,
        in_specs=[vmem()] * (len(pieces) + 1),
        out_specs=vmem(),
        out_shape=jax.ShapeDtypeStruct(pieces[0].shape, F32),
        compiler_params=params(12),
        name="finish",
    )(*pieces, whitener)


def shards(features, proj_weight, partner_offsets, ortholog_index):
    rows, depth = features.shape
    embed = proj_weight.shape[1]
    groups = lax.axis_size("sp")
    shares = lax.axis_size("win")
    devices = groups * shares
    group = lax.axis_index("sp").astype(jnp.int32)
    window = lax.axis_index("win").astype(jnp.int32)
    me = group * shares + window

    direct = groups == 8
    by_x, by_near, by_far = shares, 2 * shares, 4 * shares
    if not direct:
        slices = features.reshape(rows, groups, depth // groups).transpose(1, 0, 2)
        slices = lax.all_to_all(slices, "sp", 0, 0)
        slices = [
            lax.dynamic_index_in_dim(slices, group ^ k, 0, keepdims=False) for k in range(groups)
        ]

    block, send, keep = project(
        me.reshape(1), partner_offsets, features, proj_weight, ortholog_index.T
    )
    block = block[None]
    if direct:
        block_x = xor_permute(block, by_x)
        block_far = xor_permute(block, by_far)
        block_near = xor_permute(block, by_near)
    else:
        gathered = lax.all_gather(block, "sp", tiled=True)

    arrived = [xor_permute(send, 1)]
    if direct:
        arrived[0], block_x = lax.optimization_barrier((arrived[0], block_x))
    sent = send
    seen = 1
    stages = []
    low = 1
    place = me & 1
    while keep.shape[0] > 32:
        count = 4
        own = (me >> low) & (count - 1)
        keep, sends, seen = stage(own, keep, sent, arrived, seen, count, embed)
        if direct and stages:
            group_scalar = group.reshape(1)
            *sends, block_far, block_near, group_scalar = lax.optimization_barrier(
                (*sends, block_far, block_near, group_scalar)
            )
            slices = cut(group_scalar, features, groups)
            pair_x = xor_permute(jnp.concatenate([block_far, block_near]), by_x)
        arrived = [xor_permute(piece, (r + 1) << low) for r, piece in enumerate(sends)]
        sent = sends[0]
        stages.append((low, count))
        place = place * count + own
        low += 2
    size = keep.shape[0]
    part = keep
    for piece in arrived:
        part = part + piece[:size].astype(F32)
    sums = [sent, *arrived]
    extra = devices >> low
    if extra > 1:
        mine = jnp.concatenate([part.astype(BF16)] + [piece[size:] for piece in sums])
        others = [xor_permute(mine, r << low) for r in range(1, extra)]
        for piece in others:
            part = part + piece[:size].astype(F32)
        sums = [mine, *others]
    part = part.astype(BF16)
    for number, (low, count) in enumerate(reversed(stages)):
        if direct and number == 1:
            part, block_far = lax.optimization_barrier((part, block_far))
            block_far_near = xor_permute(block_far, by_near)
            part, pair_x = lax.optimization_barrier((part, pair_x))
        part = jnp.concatenate(
            [part] + [xor_permute(part, r << low) for r in range(1, count)], axis=0
        )
    part = part.reshape(-1, size, part.shape[1])
    if direct:
        part, block_far_near = lax.optimization_barrier((part, block_far_near))
        far_near_x = xor_permute(block_far_near, by_x)
        blocks = [block, block_x, block_near, block_far, pair_x, block_far_near, far_near_x]
        order = [0, 1, 2, 4, 5, 3, 6, 7]
    else:
        order = slice_order = list(range(groups))
        blocks = [
            lax.dynamic_index_in_dim(gathered, group ^ k, 0, keepdims=True) for k in order
        ]
    other = xor_permute(part, 1)
    if direct:
        other, *slices = lax.optimization_barrier((other, *slices))
        slice_order = [0, 2, 4, 6, 1, 3, 5, 7]
        slices = [xor_permute(slices[k], k * shares) if k else slices[k] for k in slice_order]

    whitener, mean = whiten(place.reshape(1), part, other, sums, seen, rows, embed)
    loss, grad = contrast(group.reshape(1), blocks, order, mean, whitener)
    group, window = group.reshape(1), window.reshape(1)
    pieces = []
    for mask in reversed(range(0, shares, 2)):
        keep, send = weight_pieces(
            group, window, grad, slices, slice_order, shares, (mask, mask + 1)
        )
        arrived = xor_permute(send, 1)
        if mask:
            pieces.append(xor_permute(join(keep, arrived), mask))
        else:
            pieces = [keep, arrived] + pieces
    return loss[0], finish(pieces, whitener)


def solution(mesh):
    return jax.shard_map(
        shards,
        mesh=mesh,
        in_specs=(P(("sp", "win"), None), P(), P("sp", None), P(("sp", "win"), None)),
        out_specs=(P(("sp", "win")), P(("sp", "win"), None)),
        check_vma=False,
    )
```

```python
import functools

import jax
import jax.numpy as jnp
from jax import lax
from jax.experimental import pallas as pl
from jax.experimental.pallas import tpu as pltpu
from jax.sharding import PartitionSpec as P

PARTNERS = 4
LOGIT_SCALE = 0.125
AXES = ("sp", "win")
LANES = 128
TAIL = 16
CHUNKS = 8
F32 = jnp.float32
BF16 = jnp.bfloat16
HIGHEST = lax.Precision.HIGHEST


def dot(a, b, contract=(1, 0), precision=None):
    return lax.dot_general(
        a,
        b,
        (((contract[0],), (contract[1],)), ((), ())),
        precision=precision,
        preferred_element_type=F32,
    )


def params(mebibytes, semantics=None):
    return pltpu.CompilerParams(
        vmem_limit_bytes=mebibytes * 2**20, dimension_semantics=semantics
    )


def vmem():
    return pl.BlockSpec(memory_space=pltpu.VMEM)


def smem():
    return pl.BlockSpec(memory_space=pltpu.SMEM)


def xor_permute(piece, mask):
    devices = lax.axis_size(AXES)
    return lax.ppermute(piece, AXES, [(i, i ^ mask) for i in range(devices)])


def split(value):
    high = value.astype(BF16)
    return high, (value - high.astype(F32)).astype(BF16)


def cut_kernel(group_ref, features_hbm, *refs):
    outs, sems = refs[:-1], refs[-1]
    columns = outs[0].shape[1]
    copies = []
    for k, out in enumerate(outs):
        start = pl.multiple_of((group_ref[0] ^ k) * columns, columns)
        copies.append(
            pltpu.make_async_copy(features_hbm.at[:, pl.ds(start, columns)], out, sems.at[k])
        )
        copies[k].start()
    for copy in copies:
        copy.wait()


def cut(group, features, groups):
    rows, depth = features.shape
    return pl.pallas_call(
        cut_kernel,
        in_specs=[smem(), pl.BlockSpec(memory_space=pltpu.HBM)],
        out_specs=[pl.BlockSpec(memory_space=pltpu.HBM)] * groups,
        out_shape=[jax.ShapeDtypeStruct((rows, depth // groups), BF16)] * groups,
        scratch_shapes=[pltpu.SemaphoreType.DMA((groups,))],
        compiler_params=params(8),
        name="cut",
    )(group, features)


def pack_sums(sums, packed, rows):
    high = sums.astype(BF16).astype(F32)
    pad = jnp.zeros((sums.shape[0], 2 * packed - sums.shape[1]), F32)
    lines = []
    for half in (high, sums - high):
        lines += [half[:, :packed], jnp.concatenate([half[:, packed:], pad], axis=1)]
    if rows > 4 * sums.shape[0]:
        lines.append(jnp.zeros((rows - 4 * sums.shape[0], packed), F32))
    return jnp.concatenate(lines, axis=0).astype(BF16)


def unpack_sums(block, count, embed):
    wide = block.astype(F32)
    packed = wide.shape[1]
    low = 2 * count
    left = wide[0:count] + wide[low : low + count]
    right = wide[count:low] + wide[low + count : low + 2 * count]
    return jnp.concatenate([left, right[:, : embed - packed]], axis=1)


def project_kernel(
    me_ref,
    offsets_ref,
    features_hbm,
    weight_hbm,
    ortholog_hbm,
    block_ref,
    send_ref,
    keep_ref,
    features_ref,
    weight_ref,
    ortholog_ref,
    means,
    wide,
    sems,
):
    rows = features_ref.shape[0]
    depth, embed = weight_ref.shape
    half, packed = keep_ref.shape
    blocks = embed // LANES
    tile = depth // CHUNKS

    copies = []
    for n in range(CHUNKS):
        at = pl.ds(n * tile, tile)
        copies.append(
            (
                pltpu.make_async_copy(features_hbm.at[:, at], features_ref.at[:, at], sems.at[0, n]),
                pltpu.make_async_copy(weight_hbm.at[at, :], weight_ref.at[at, :], sems.at[1, n]),
            )
        )
        for copy in copies[-1]:
            copy.start()
    table_copy = pltpu.make_async_copy(ortholog_hbm, ortholog_ref, sems.at[0, CHUNKS])
    table_copy.start()

    total = jnp.zeros((rows, embed), F32)
    for n in range(CHUNKS):
        for copy in copies[n]:
            copy.wait()
        at = slice(n * tile, (n + 1) * tile)
        total = total + dot(features_ref[:, at], weight_ref[at, :])
    projected = total.astype(BF16)
    block_ref[0:rows, :] = projected

    table_copy.wait()
    line = lax.broadcasted_iota(jnp.int32, (TAIL, embed), 0)
    lane = lax.broadcasted_iota(jnp.int32, (TAIL, embed), 1)
    table = jnp.zeros((TAIL, embed), F32)
    for k in range(PARTNERS):
        table = jnp.where((line == 1) & (lane == k), offsets_ref[0, k].astype(F32), table)
    hits = jnp.concatenate(
        [ortholog_ref[k : k + 1, :].astype(F32) for k in range(PARTNERS)]
        + ([jnp.zeros((1, embed - PARTNERS * rows), F32)] if embed > PARTNERS * rows else []),
        axis=1,
    )
    block_ref[rows:, :] = jnp.where(line == 0, hits, table).astype(BF16)

    sums = jnp.sum(projected.astype(F32), axis=0, keepdims=True)
    send_ref[half:, :] = pack_sums(sums, packed, TAIL)
    wide[:, :embed] = projected
    wide[:, embed:] = projected[:, : packed - LANES]
    ones = jnp.ones((rows, LANES), BF16)
    means[...] = jnp.broadcast_to(sums * (1.0 / rows), means.shape)
    core = me_ref[0] & 1
    for side, out in ((1, send_ref), (0, keep_ref)):
        for r in range(blocks // 2):
            block = (core ^ side) * (blocks // 2) + r
            start = pl.multiple_of(block * LANES, LANES)
            own = wide[:, pl.ds(start, LANES)]
            gram = dot(own, wide[:, pl.ds(start, packed)], (0, 0))
            sums = dot(own, ones, (0, 0))
            for k in range(packed // LANES):
                other = pl.multiple_of((block + k) % blocks * LANES, LANES)
                at = slice(k * LANES, (k + 1) * LANES)
                value = gram[:, at] - sums * means[0:1, pl.ds(other, LANES)]
                out[r * LANES : (r + 1) * LANES, at] = value.astype(out.dtype)


def project(me, offsets, features, weight, ortholog):
    rows, depth = features.shape
    embed = weight.shape[1]
    packed = embed // 2 + LANES
    hbm = pl.BlockSpec(memory_space=pltpu.HBM)
    return pl.pallas_call(
        project_kernel,
        in_specs=[smem(), smem(), hbm, hbm, hbm],
        out_specs=[vmem()] * 3,
        out_shape=[
            jax.ShapeDtypeStruct((rows + TAIL, embed), BF16),
            jax.ShapeDtypeStruct((embed // 2 + TAIL, packed), BF16),
            jax.ShapeDtypeStruct((embed // 2, packed), F32),
        ],
        scratch_shapes=[
            pltpu.VMEM((rows, depth), BF16),
            pltpu.VMEM((depth, embed), BF16),
            pltpu.VMEM((PARTNERS, rows), jnp.int32),
            pltpu.VMEM((8, embed), F32),
            pltpu.VMEM((rows, embed + packed - LANES), BF16),
            pltpu.SemaphoreType.DMA((2, CHUNKS + 1)),
        ],
        compiler_params=params(51),
        cost_estimate=pl.CostEstimate(
            flops=2 * rows * depth * embed, bytes_accessed=2 * depth * embed, transcendentals=0
        ),
        name="project",
    )(me, offsets, features, weight, ortholog)


def make_stage_kernel(seen, arrivals, count, embed):
    def kernel(own_ref, keep_ref, sent_ref, *refs):
        arrived, next_keep, outs = refs[:arrivals], refs[arrivals], refs[arrivals + 1 :]
        full, packed = keep_ref.shape
        share = full // count
        own = own_ref[0]
        sums = [unpack_sums(ref[full:, :], seen, embed) for ref in (sent_ref, *arrived)]
        block = pack_sums(jnp.concatenate(sums, axis=0), packed, outs[0].shape[0] - share)
        for r in range(count):
            at = pl.ds(pl.multiple_of((own ^ r) * share, share), share)
            value = keep_ref[at, :]
            for ref in arrived:
                value = value + ref[at, :].astype(F32)
            if r == 0:
                next_keep[...] = value
            else:
                outs[r - 1][:share, :] = value.astype(BF16)
                outs[r - 1][share:, :] = block

    return kernel


def stage(own, keep, sent, arrived, seen, count, embed):
    full, packed = keep.shape
    share = full // count
    held = seen * (1 + len(arrived))
    tail = -(-4 * held // TAIL) * TAIL
    out = pl.pallas_call(
        make_stage_kernel(seen, len(arrived), count, embed),
        in_specs=[smem()] + [vmem()] * (2 + len(arrived)),
        out_specs=[vmem()] * count,
        out_shape=[jax.ShapeDtypeStruct((share, packed), F32)]
        + [jax.ShapeDtypeStruct((share + tail, packed), BF16)] * (count - 1),
        compiler_params=params(16),
        cost_estimate=pl.CostEstimate(
            flops=full * packed, bytes_accessed=4 * full * packed, transcendentals=0
        ),
        name="stage",
    )(own.reshape(1), keep, sent, *arrived)
    return out[0], out[1:], held


def make_whiten_kernel(rows, count):
    def kernel(
        place_ref,
        near_ref,
        far_ref,
        *refs,
    ):
        sums_refs = refs[:-7]
        whitener_ref, mean_ref, scaled, rest, first, left, right = refs[-7:]
        place = place_ref[0]
        embed = scaled.shape[0]
        blocks = embed // LANES
        half = blocks // 2
        pieces, depth = near_ref.shape[:2]
        per_block = LANES // depth
        totals = jnp.concatenate(
            [
                unpack_sums(ref[start : start + 4 * count, :], count, embed)
                for ref in sums_refs
                for start in range(depth, ref.shape[0], 4 * count)
            ],
            axis=0,
        )
        total_rows = rows * totals.shape[0]
        tile = 256

        mean = jnp.sum(totals, axis=0, keepdims=True) * (1.0 / total_rows)
        mean_ref[...] = mean
        shift_high, shift_low = split(totals * (1.0 / rows) - mean)
        shift_left = jnp.concatenate([shift_high, shift_high, shift_low], axis=0)
        shift_right = jnp.concatenate([shift_high, shift_low, shift_high], axis=0)

        def block_at(i, j):
            return slice(i * LANES, (i + 1) * LANES), slice(j * LANES, (j + 1) * LANES)

        def unpack(source_ref, side):
            for i in range(side * half, (side + 1) * half):
                for part in range(per_block):
                    piece = ((i - side * half) * per_block + part) ^ (place % pieces)
                    wide = source_ref[piece].astype(F32)
                    lines = pl.ds(i * LANES + part * depth, depth)
                    for k in range(half + 1):
                        if k == half and side:
                            continue
                        j = (i + k) % blocks
                        scaled[lines, j * LANES : (j + 1) * LANES] = wide[
                            :, k * LANES : (k + 1) * LANES
                        ]

        for core in range(2):

            @pl.when(place // pieces == core)
            def _():
                unpack(near_ref, core)
                unpack(far_ref, 1 - core)

        for i in range(blocks):
            for j in range(blocks):
                held = (j - i) % blocks < half or ((j - i) % blocks == half and i < half)
                if not held and i * LANES // tile <= j * LANES // tile:
                    scaled[block_at(i, j)] = scaled[block_at(j, i)].T

        panels = []
        for t in range(embed // tile):
            panels.append((slice(0, (t + 1) * tile), slice(t * tile, (t + 1) * tile)))

        def mirror(out, panel, value):
            rows_at, columns_at = panel
            value = value.astype(BF16)
            out[panel] = value
            above = columns_at.start
            if above:
                out[columns_at, 0:above] = value[0:above].T

        squares = jnp.zeros((1, tile), F32)
        for panel in panels:
            rows_at, columns_at = panel
            between = dot(shift_left[:, rows_at], shift_right[:, columns_at], (0, 0))
            covariance = (scaled[panel] + rows * between) * (1.0 / total_rows)
            scaled[panel] = covariance
            mirror(first, panel, covariance)
            above = columns_at.start
            square = covariance * covariance
            squares = squares + jnp.sum(square[above:], axis=0, keepdims=True)
            if above:
                squares = squares + 2.0 * jnp.sum(square[:above], axis=0, keepdims=True)
        frobenius = jnp.sqrt(jnp.sum(squares, axis=1, keepdims=True))
        inverse = 1.0 / frobenius
        root = lax.rsqrt(frobenius)

        def product(one, two, finish):
            for panel in panels:
                finish(panel, dot(one[panel[0], :], two[:, panel[1]]))

        def second(panel, value):
            value = value * (inverse * inverse)
            own = scaled[panel] * inverse
            scaled[panel] = own
            rest[panel] = 27.0 * value - 39.0 * own
            mirror(left, panel, value)
            mirror(right, panel, value - 9.0 * own)

        product(first, first, second)

        def fourth(panel, value):
            value = (value + rest[panel]) * (1.0 / 16.0)
            rest[panel] = value
            mirror(whitener_ref, panel, value)

        product(left, right, fourth)

        def moved(panel, value):
            value = value * inverse
            scaled[panel] = 2.25 * 2.25 * scaled[panel] + 4.5 * value
            mirror(right, panel, value)

        product(first, whitener_ref, moved)

        def quad(panel, value):
            value = value + scaled[panel]
            rest[panel] = 3.0 * rest[panel] - 2.25 * value
            mirror(left, panel, value)

        product(whitener_ref, right, quad)
        first[...] = whitener_ref[...]

        def last(panel, value):
            at = lax.broadcasted_iota(jnp.int32, value.shape, 0)
            eye = at == lax.broadcasted_iota(jnp.int32, value.shape, 1) + panel[1].start
            value = 0.5 * (rest[panel] - value)
            value = value + jnp.where(eye, 0.5 * 3.0 * 2.25, 0.0)
            mirror(whitener_ref, panel, value * root)

        product(first, left, last)

    return kernel


def whiten(place, near, far, sums, count, rows, embed):
    square = (embed, embed)
    return pl.pallas_call(
        make_whiten_kernel(rows, count),
        in_specs=[smem()] + [vmem()] * (2 + len(sums)),
        out_specs=[vmem(), vmem()],
        out_shape=[
            jax.ShapeDtypeStruct(square, BF16),
            jax.ShapeDtypeStruct((1, embed), F32),
        ],
        scratch_shapes=[pltpu.VMEM(square, F32)] * 2 + [pltpu.VMEM(square, BF16)] * 3,
        compiler_params=params(24),
        cost_estimate=pl.CostEstimate(
            flops=5 * 2 * embed**3, bytes_accessed=2 * embed**2, transcendentals=0
        ),
        name="whiten",
    )(place, near, far, *sums)


def contrast_kernel(order, group_ref, mean_ref, whitener_ref, *refs):
    loss_ref, grad_ref, white, tables, numbers, offsets_ref, sem = refs[-11:-4]
    even, odd = (refs[-4], refs[-3]), (refs[-2], refs[-1])
    block_refs = [ref.at[i] for ref in refs[:-11] for i in range(ref.shape[0])]
    block_refs = [block_refs[order.index(k)] for k in range(len(order))]
    groups, rows, embed = white.shape
    group = group_ref[0]

    for k in range(0, groups, 2):
        pair = block_refs[k : k + 2]
        centered = [(ref[0:rows, :].astype(F32) - mean_ref[...]).astype(BF16) for ref in pair]
        value = dot(jnp.concatenate(centered, axis=0), whitener_ref[...]).astype(BF16)
        for side, ref in enumerate(pair):
            white[group ^ (k + side)] = value[side * rows : (side + 1) * rows]
            table = ref[rows:, :].astype(F32)[0:8]
            tables[group ^ (k + side)] = table
            numbers[group ^ (k + side)] = table[:, 0:LANES].astype(jnp.int32)
    copy = pltpu.make_async_copy(numbers, offsets_ref, sem)
    copy.start()
    copy.wait()

    places = lax.broadcasted_iota(jnp.int32, (rows, rows), 0).astype(F32)
    log2e = 1.4426950408889634

    def partner(g, k):
        return white[(g + offsets_ref[g, 1, k]) % groups]

    def scores(g, buffers):
        own = white[g]
        for k in range(PARTNERS):
            buffers[0][k * rows : (k + 1) * rows, :] = dot(partner(g, k), own, (1, 1))

    def softmax(g, buffers):
        loss = jnp.zeros((1, rows), F32)
        for k in range(PARTNERS):
            at = slice(k * rows, (k + 1) * rows)
            own = buffers[0][at, :]
            peak = jnp.max(own, axis=0, keepdims=True)
            powers = jnp.exp2((own - peak) * (LOGIT_SCALE * log2e))
            sums = jnp.sum(powers, axis=0, keepdims=True)
            hit = places == tables[g, 0:1, at]
            picked = jnp.sum(jnp.where(hit, own, 0.0), axis=0, keepdims=True)
            loss = loss + ((peak - picked) * LOGIT_SCALE + jnp.log(sums))
            share = powers * (1.0 / (PARTNERS * sums))
            weights = share - jnp.where(hit, 1.0 / PARTNERS, 0.0)
            buffers[1][at, :] = weights.astype(BF16)
        return loss * (1.0 / PARTNERS)

    def gradient(g, buffers):
        grad = dot(buffers[1][0:rows, :], partner(g, 0), (0, 0))
        for k in range(1, PARTNERS):
            grad = grad + dot(buffers[1][k * rows : (k + 1) * rows, :], partner(g, k), (0, 0))
        grad_ref[g] = (grad * LOGIT_SCALE).astype(BF16)

    scores(0, even)

    @pl.loop(0, groups // 2)
    def _(pair):
        g = 2 * pair
        scores(g + 1, odd)
        first = softmax(g, even)
        gradient(g, even)
        second = softmax(g + 1, odd)
        scores(lax.rem(g + 2, groups), even)
        gradient(g + 1, odd)

        @pl.when(pair == group // 2)
        def _():
            loss_ref[...] = jnp.where(group % 2 == 0, first, second)


def contrast(group, blocks, order, mean, whitener):
    groups = len(order)
    rows, embed = blocks[0].shape[1:]
    rows -= TAIL
    return pl.pallas_call(
        functools.partial(contrast_kernel, order),
        in_specs=[smem()] + [vmem()] * (2 + len(blocks)),
        out_specs=[vmem()] * 2,
        out_shape=[
            jax.ShapeDtypeStruct((1, rows), F32),
            jax.ShapeDtypeStruct((groups, rows, embed), BF16),
        ],
        scratch_shapes=[
            pltpu.VMEM((groups, rows, embed), BF16),
            pltpu.VMEM((groups, 8, embed), F32),
            pltpu.VMEM((groups, 8, LANES), jnp.int32),
            pltpu.SMEM((groups, 8, LANES), jnp.int32),
            pltpu.SemaphoreType.DMA,
        ]
        + [pltpu.VMEM((PARTNERS * rows, rows), F32), pltpu.VMEM((PARTNERS * rows, rows), BF16)] * 2,
        compiler_params=params(min(58, 12 + 6 * groups * rows * embed // 2**20)),
        cost_estimate=pl.CostEstimate(
            flops=groups * rows * 2 * embed * (embed + 2 * PARTNERS * rows),
            bytes_accessed=4 * groups * rows * embed,
            transcendentals=groups * PARTNERS * rows * rows,
        ),
        name="contrast",
    )(group, mean, whitener, *blocks)


def pieces_kernel(share, masks, order, group_ref, window_ref, grad_ref, *refs):
    groups = grad_ref.shape[0]
    features, (keep_ref, send_ref, total) = refs[:groups], refs[groups:]

    def columns(at):
        value = None
        for k, feature_ref in zip(order, features):
            term = dot(feature_ref[:, at], grad_ref[group_ref[0] ^ k], (0, 0))
            value = term if value is None else value + term
        return value

    if share % LANES:
        total[...] = columns(slice(None))
    for n, mask in enumerate(masks):
        at = pl.ds(pl.multiple_of((window_ref[0] ^ mask) * share, share), share)
        value = total[at, :] if share % LANES else columns(at)
        out, n = (send_ref, n - len(masks) // 2) if n >= len(masks) // 2 else (keep_ref, n)
        out[n * share : (n + 1) * share, :] = value.astype(out.dtype)


def weight_pieces(group, window, grad, slices, order, shares, masks):
    groups, rows, embed = grad.shape
    columns = slices[0].shape[1]
    share = columns // shares
    half = len(masks) // 2 * share
    return pl.pallas_call(
        functools.partial(pieces_kernel, share, masks, order),
        in_specs=[smem(), smem()] + [vmem()] * (1 + len(slices)),
        out_specs=[vmem()] * 2,
        out_shape=[
            jax.ShapeDtypeStruct((half, embed), F32),
            jax.ShapeDtypeStruct((half, embed), BF16),
        ],
        scratch_shapes=[pltpu.VMEM((columns if share % LANES else 8, embed), F32)],
        compiler_params=params(24),
        cost_estimate=pl.CostEstimate(
            flops=groups * rows * 2 * embed * share * len(masks),
            bytes_accessed=2 * groups * rows * (embed + columns),
            transcendentals=0,
        ),
        name="weight_pieces",
    )(group, window, grad, *slices)


def join_kernel(keep_ref, arrived_ref, out_ref):
    out_ref[...] = (keep_ref[...] + arrived_ref[...].astype(F32)).astype(BF16)


def join(keep, arrived):
    return pl.pallas_call(
        join_kernel,
        in_specs=[vmem()] * 2,
        out_specs=vmem(),
        out_shape=jax.ShapeDtypeStruct(keep.shape, BF16),
        compiler_params=params(8),
        name="join",
    )(keep, arrived)


def finish_kernel(*refs):
    keep_ref, whitener_ref, out_ref = refs[0], refs[-2], refs[-1]
    value = keep_ref[...]
    for ref in refs[1:-2]:
        value = value + ref[...].astype(F32)
    high, low = split(value)
    both = dot(jnp.concatenate([high, low], axis=0), whitener_ref[...], (1, 1))
    out_ref[...] = both[: value.shape[0]] + both[value.shape[0] :]


def finish(pieces, whitener):
    return pl.pallas_call(
        finish_kernel,
        in_specs=[vmem()] * (len(pieces) + 1),
        out_specs=vmem(),
        out_shape=jax.ShapeDtypeStruct(pieces[0].shape, F32),
        compiler_params=params(12),
        name="finish",
    )(*pieces, whitener)


def shards(features, proj_weight, partner_offsets, ortholog_index):
    rows, depth = features.shape
    embed = proj_weight.shape[1]
    groups = lax.axis_size("sp")
    shares = lax.axis_size("win")
    devices = groups * shares
    group = lax.axis_index("sp").astype(jnp.int32)
    window = lax.axis_index("win").astype(jnp.int32)
    me = group * shares + window

    direct = groups == 8
    by_x, by_near, by_far = shares, 2 * shares, 4 * shares
    if not direct:
        slices = features.reshape(rows, groups, depth // groups).transpose(1, 0, 2)
        slices = lax.all_to_all(slices, "sp", 0, 0)
        slices = [
            lax.dynamic_index_in_dim(slices, group ^ k, 0, keepdims=False) for k in range(groups)
        ]

    block, send, keep = project(
        me.reshape(1), partner_offsets, features, proj_weight, ortholog_index.T
    )
    block = block[None]
    if direct:
        block_x = xor_permute(block, by_x)
        block_far = xor_permute(block, by_far)
        block_near = xor_permute(block, by_near)
    else:
        gathered = lax.all_gather(block, "sp", tiled=True)

    arrived = [xor_permute(send, 1)]
    sent = send
    seen = 1
    stages = []
    low = 1
    place = me & 1
    while keep.shape[0] > 32:
        count = 4
        own = (me >> low) & (count - 1)
        keep, sends, seen = stage(own, keep, sent, arrived, seen, count, embed)
        if direct and stages:
            group_scalar = group.reshape(1)
            *sends, block_x, block_near, block_far, group_scalar = lax.optimization_barrier(
                (*sends, block_x, block_near, block_far, group_scalar)
            )
            slices = list(cut(group_scalar, features, groups))
            pair_x = xor_permute(jnp.concatenate([block_far, block_near]), by_x)
        arrived = [xor_permute(piece, (r + 1) << low) for r, piece in enumerate(sends)]
        sent = sends[0]
        stages.append((low, count))
        place = place * count + own
        low += 2
    size = keep.shape[0]
    part = keep
    for piece in arrived:
        part = part + piece[:size].astype(F32)
    sums = [sent, *arrived]
    extra = devices >> low
    if extra > 1:
        mine = jnp.concatenate([part.astype(BF16)] + [piece[size:] for piece in sums])
        others = [xor_permute(mine, r << low) for r in range(1, extra)]
        for piece in others:
            part = part + piece[:size].astype(F32)
        sums = [mine, *others]
    part = part.astype(BF16)
    for number, (low, count) in enumerate(reversed(stages)):
        if direct and number == 1:
            part, block_far, slices[4] = lax.optimization_barrier((part, block_far, slices[4]))
            block_far_near = xor_permute(block_far, by_near)
            slices[4] = xor_permute(slices[4], by_far)
            part, pair_x = lax.optimization_barrier((part, pair_x))
        part = jnp.concatenate(
            [part] + [xor_permute(part, r << low) for r in range(1, count)], axis=0
        )
    part = part.reshape(-1, size, part.shape[1])
    if direct:
        part, block_far_near = lax.optimization_barrier((part, block_far_near))
        far_near_x = xor_permute(block_far_near, by_x)
        blocks = [block, block_x, block_near, block_far, pair_x, block_far_near, far_near_x]
        order = [0, 1, 2, 4, 5, 3, 6, 7]
    else:
        order = slice_order = list(range(groups))
        blocks = [
            lax.dynamic_index_in_dim(gathered, group ^ k, 0, keepdims=True) for k in order
        ]
    other = xor_permute(part, 1)
    if direct:
        slice_order = [0, 4, 6, 2, 1, 3, 5, 7]
        later = slice_order[2:]
        other, *held = lax.optimization_barrier((other, *(slices[k] for k in later)))
        for k, piece in zip(later, held):
            slices[k] = xor_permute(piece, k * shares)
        slices = [slices[k] for k in slice_order]

    whitener, mean = whiten(place.reshape(1), part, other, sums, seen, rows, embed)
    loss, grad = contrast(group.reshape(1), blocks, order, mean, whitener)
    group, window = group.reshape(1), window.reshape(1)
    pieces = []
    for mask in reversed(range(0, shares, 2)):
        keep, send = weight_pieces(
            group, window, grad, slices, slice_order, shares, (mask, mask + 1)
        )
        arrived = xor_permute(send, 1)
        if mask:
            pieces.append(xor_permute(join(keep, arrived), mask))
        else:
            pieces = [keep, arrived] + pieces
    return loss[0], finish(pieces, whitener)


def solution(mesh):
    return jax.shard_map(
        shards,
        mesh=mesh,
        in_specs=(P(("sp", "win"), None), P(), P("sp", None), P(("sp", "win"), None)),
        out_specs=(P(("sp", "win")), P(("sp", "win"), None)),
        check_vma=False,
    )
```

```python
import functools

import jax
import jax.numpy as jnp
from jax import lax
from jax.experimental import pallas as pl
from jax.experimental.pallas import tpu as pltpu
from jax.sharding import PartitionSpec as P

PARTNERS = 4
LOGIT_SCALE = 0.125
AXES = ("sp", "win")
LANES = 128
TAIL = 16
CHUNKS = 8
F32 = jnp.float32
BF16 = jnp.bfloat16
HIGHEST = lax.Precision.HIGHEST


def dot(a, b, contract=(1, 0), precision=None):
    return lax.dot_general(
        a,
        b,
        (((contract[0],), (contract[1],)), ((), ())),
        precision=precision,
        preferred_element_type=F32,
    )


def params(mebibytes, semantics=None):
    return pltpu.CompilerParams(
        vmem_limit_bytes=mebibytes * 2**20, dimension_semantics=semantics
    )


def vmem():
    return pl.BlockSpec(memory_space=pltpu.VMEM)


def smem():
    return pl.BlockSpec(memory_space=pltpu.SMEM)


def xor_permute(piece, mask):
    devices = lax.axis_size(AXES)
    return lax.ppermute(piece, AXES, [(i, i ^ mask) for i in range(devices)])


def split(value):
    high = value.astype(BF16)
    return high, (value - high.astype(F32)).astype(BF16)


def cut_kernel(group_ref, features_hbm, *refs):
    outs, sems = refs[:-1], refs[-1]
    columns = outs[0].shape[1]
    copies = []
    for k, out in enumerate(outs):
        start = pl.multiple_of((group_ref[0] ^ k) * columns, columns)
        copies.append(
            pltpu.make_async_copy(features_hbm.at[:, pl.ds(start, columns)], out, sems.at[k])
        )
        copies[k].start()
    for copy in copies:
        copy.wait()


def cut(group, features, groups):
    rows, depth = features.shape
    return pl.pallas_call(
        cut_kernel,
        in_specs=[smem(), pl.BlockSpec(memory_space=pltpu.HBM)],
        out_specs=[pl.BlockSpec(memory_space=pltpu.HBM)] * groups,
        out_shape=[jax.ShapeDtypeStruct((rows, depth // groups), BF16)] * groups,
        scratch_shapes=[pltpu.SemaphoreType.DMA((groups,))],
        compiler_params=params(8),
        name="cut",
    )(group, features)


def pack_sums(sums, packed, rows):
    high = sums.astype(BF16).astype(F32)
    pad = jnp.zeros((sums.shape[0], 2 * packed - sums.shape[1]), F32)
    lines = []
    for half in (high, sums - high):
        lines += [half[:, :packed], jnp.concatenate([half[:, packed:], pad], axis=1)]
    if rows > 4 * sums.shape[0]:
        lines.append(jnp.zeros((rows - 4 * sums.shape[0], packed), F32))
    return jnp.concatenate(lines, axis=0).astype(BF16)


def unpack_sums(block, count, embed):
    wide = block.astype(F32)
    packed = wide.shape[1]
    low = 2 * count
    left = wide[0:count] + wide[low : low + count]
    right = wide[count:low] + wide[low + count : low + 2 * count]
    return jnp.concatenate([left, right[:, : embed - packed]], axis=1)


def project_kernel(
    me_ref,
    offsets_ref,
    features_hbm,
    weight_hbm,
    ortholog_hbm,
    block_ref,
    send_ref,
    keep_ref,
    features_ref,
    weight_ref,
    ortholog_ref,
    means,
    wide,
    sems,
):
    rows = features_ref.shape[0]
    depth, embed = weight_ref.shape
    half, packed = keep_ref.shape
    blocks = embed // LANES
    tile = depth // CHUNKS

    copies = []
    for n in range(CHUNKS):
        at = pl.ds(n * tile, tile)
        copies.append(
            (
                pltpu.make_async_copy(features_hbm.at[:, at], features_ref.at[:, at], sems.at[0, n]),
                pltpu.make_async_copy(weight_hbm.at[at, :], weight_ref.at[at, :], sems.at[1, n]),
            )
        )
        for copy in copies[-1]:
            copy.start()
    table_copy = pltpu.make_async_copy(ortholog_hbm, ortholog_ref, sems.at[0, CHUNKS])
    table_copy.start()

    total = jnp.zeros((rows, embed), F32)
    for n in range(CHUNKS):
        for copy in copies[n]:
            copy.wait()
        at = slice(n * tile, (n + 1) * tile)
        total = total + dot(features_ref[:, at], weight_ref[at, :])
    projected = total.astype(BF16)
    block_ref[0:rows, :] = projected

    table_copy.wait()
    line = lax.broadcasted_iota(jnp.int32, (TAIL, embed), 0)
    lane = lax.broadcasted_iota(jnp.int32, (TAIL, embed), 1)
    table = jnp.zeros((TAIL, embed), F32)
    for k in range(PARTNERS):
        table = jnp.where((line == 1) & (lane == k), offsets_ref[0, k].astype(F32), table)
    hits = jnp.concatenate(
        [ortholog_ref[k : k + 1, :].astype(F32) for k in range(PARTNERS)]
        + ([jnp.zeros((1, embed - PARTNERS * rows), F32)] if embed > PARTNERS * rows else []),
        axis=1,
    )
    block_ref[rows:, :] = jnp.where(line == 0, hits, table).astype(BF16)

    sums = jnp.sum(projected.astype(F32), axis=0, keepdims=True)
    send_ref[half:, :] = pack_sums(sums, packed, TAIL)
    wide[:, :embed] = projected
    wide[:, embed:] = projected[:, : packed - LANES]
    ones = jnp.ones((rows, LANES), BF16)
    means[...] = jnp.broadcast_to(sums * (1.0 / rows), means.shape)
    core = me_ref[0] & 1
    for side, out in ((1, send_ref), (0, keep_ref)):
        for r in range(blocks // 2):
            block = (core ^ side) * (blocks // 2) + r
            start = pl.multiple_of(block * LANES, LANES)
            own = wide[:, pl.ds(start, LANES)]
            gram = dot(own, wide[:, pl.ds(start, packed)], (0, 0))
            sums = dot(own, ones, (0, 0))
            for k in range(packed // LANES):
                other = pl.multiple_of((block + k) % blocks * LANES, LANES)
                at = slice(k * LANES, (k + 1) * LANES)
                value = gram[:, at] - sums * means[0:1, pl.ds(other, LANES)]
                out[r * LANES : (r + 1) * LANES, at] = value.astype(out.dtype)


def project(me, offsets, features, weight, ortholog):
    rows, depth = features.shape
    embed = weight.shape[1]
    packed = embed // 2 + LANES
    hbm = pl.BlockSpec(memory_space=pltpu.HBM)
    return pl.pallas_call(
        project_kernel,
        in_specs=[smem(), smem(), hbm, hbm, hbm],
        out_specs=[vmem()] * 3,
        out_shape=[
            jax.ShapeDtypeStruct((rows + TAIL, embed), BF16),
            jax.ShapeDtypeStruct((embed // 2 + TAIL, packed), BF16),
            jax.ShapeDtypeStruct((embed // 2, packed), F32),
        ],
        scratch_shapes=[
            pltpu.VMEM((rows, depth), BF16),
            pltpu.VMEM((depth, embed), BF16),
            pltpu.VMEM((PARTNERS, rows), jnp.int32),
            pltpu.VMEM((8, embed), F32),
            pltpu.VMEM((rows, embed + packed - LANES), BF16),
            pltpu.SemaphoreType.DMA((2, CHUNKS + 1)),
        ],
        compiler_params=params(51),
        cost_estimate=pl.CostEstimate(
            flops=2 * rows * depth * embed, bytes_accessed=2 * depth * embed, transcendentals=0
        ),
        name="project",
    )(me, offsets, features, weight, ortholog)


def make_stage_kernel(seen, arrivals, count, embed):
    def kernel(own_ref, keep_ref, sent_ref, *refs):
        arrived, next_keep, outs = refs[:arrivals], refs[arrivals], refs[arrivals + 1 :]
        full, packed = keep_ref.shape
        share = full // count
        own = own_ref[0]
        sums = [unpack_sums(ref[full:, :], seen, embed) for ref in (sent_ref, *arrived)]
        block = pack_sums(jnp.concatenate(sums, axis=0), packed, outs[0].shape[0] - share)
        for r in range(count):
            at = pl.ds(pl.multiple_of((own ^ r) * share, share), share)
            value = keep_ref[at, :]
            for ref in arrived:
                value = value + ref[at, :].astype(F32)
            if r == 0:
                next_keep[...] = value
            else:
                outs[r - 1][:share, :] = value.astype(BF16)
                outs[r - 1][share:, :] = block

    return kernel


def stage(own, keep, sent, arrived, seen, count, embed):
    full, packed = keep.shape
    share = full // count
    held = seen * (1 + len(arrived))
    tail = -(-4 * held // TAIL) * TAIL
    out = pl.pallas_call(
        make_stage_kernel(seen, len(arrived), count, embed),
        in_specs=[smem()] + [vmem()] * (2 + len(arrived)),
        out_specs=[vmem()] * count,
        out_shape=[jax.ShapeDtypeStruct((share, packed), F32)]
        + [jax.ShapeDtypeStruct((share + tail, packed), BF16)] * (count - 1),
        compiler_params=params(16),
        cost_estimate=pl.CostEstimate(
            flops=full * packed, bytes_accessed=4 * full * packed, transcendentals=0
        ),
        name="stage",
    )(own.reshape(1), keep, sent, *arrived)
    return out[0], out[1:], held


def make_whiten_kernel(rows, count):
    def kernel(
        place_ref,
        near_ref,
        far_ref,
        *refs,
    ):
        sums_refs = refs[:-7]
        whitener_ref, mean_ref, scaled, rest, first, left, right = refs[-7:]
        place = place_ref[0]
        embed = scaled.shape[0]
        blocks = embed // LANES
        half = blocks // 2
        pieces, depth = near_ref.shape[:2]
        per_block = LANES // depth
        totals = jnp.concatenate(
            [
                unpack_sums(ref[start : start + 4 * count, :], count, embed)
                for ref in sums_refs
                for start in range(depth, ref.shape[0], 4 * count)
            ],
            axis=0,
        )
        total_rows = rows * totals.shape[0]
        tile = 256

        mean = jnp.sum(totals, axis=0, keepdims=True) * (1.0 / total_rows)
        mean_ref[...] = mean
        shift_high, shift_low = split(totals * (1.0 / rows) - mean)
        shift_left = jnp.concatenate([shift_high, shift_high, shift_low], axis=0)
        shift_right = jnp.concatenate([shift_high, shift_low, shift_high], axis=0)

        def block_at(i, j):
            return slice(i * LANES, (i + 1) * LANES), slice(j * LANES, (j + 1) * LANES)

        def unpack(source_ref, side):
            for i in range(side * half, (side + 1) * half):
                for part in range(per_block):
                    piece = ((i - side * half) * per_block + part) ^ (place % pieces)
                    wide = source_ref[piece].astype(F32)
                    lines = pl.ds(i * LANES + part * depth, depth)
                    for k in range(half + 1):
                        if k == half and side:
                            continue
                        j = (i + k) % blocks
                        scaled[lines, j * LANES : (j + 1) * LANES] = wide[
                            :, k * LANES : (k + 1) * LANES
                        ]

        for core in range(2):

            @pl.when(place // pieces == core)
            def _():
                unpack(near_ref, core)
                unpack(far_ref, 1 - core)

        for i in range(blocks):
            for j in range(blocks):
                held = (j - i) % blocks < half or ((j - i) % blocks == half and i < half)
                if not held and i * LANES // tile <= j * LANES // tile:
                    scaled[block_at(i, j)] = scaled[block_at(j, i)].T

        panels = []
        for t in range(embed // tile):
            panels.append((slice(0, (t + 1) * tile), slice(t * tile, (t + 1) * tile)))

        def mirror(out, panel, value):
            rows_at, columns_at = panel
            value = value.astype(BF16)
            out[panel] = value
            above = columns_at.start
            if above:
                out[columns_at, 0:above] = value[0:above].T

        squares = jnp.zeros((1, tile), F32)
        for panel in panels:
            rows_at, columns_at = panel
            between = dot(shift_left[:, rows_at], shift_right[:, columns_at], (0, 0))
            covariance = (scaled[panel] + rows * between) * (1.0 / total_rows)
            scaled[panel] = covariance
            mirror(first, panel, covariance)
            above = columns_at.start
            square = covariance * covariance
            squares = squares + jnp.sum(square[above:], axis=0, keepdims=True)
            if above:
                squares = squares + 2.0 * jnp.sum(square[:above], axis=0, keepdims=True)
        frobenius = jnp.sqrt(jnp.sum(squares, axis=1, keepdims=True))
        inverse = 1.0 / frobenius
        root = lax.rsqrt(frobenius)

        def product(one, two, finish):
            for panel in panels:
                finish(panel, dot(one[panel[0], :], two[:, panel[1]]))

        def second(panel, value):
            value = value * (inverse * inverse)
            own = scaled[panel] * inverse
            scaled[panel] = own
            rest[panel] = 27.0 * value - 39.0 * own
            mirror(left, panel, value)
            mirror(right, panel, value - 9.0 * own)

        product(first, first, second)

        def fourth(panel, value):
            value = (value + rest[panel]) * (1.0 / 16.0)
            rest[panel] = value
            mirror(whitener_ref, panel, value)

        product(left, right, fourth)

        def moved(panel, value):
            value = value * inverse
            scaled[panel] = 2.25 * 2.25 * scaled[panel] + 4.5 * value
            mirror(right, panel, value)

        product(first, whitener_ref, moved)

        def quad(panel, value):
            value = value + scaled[panel]
            rest[panel] = 3.0 * rest[panel] - 2.25 * value
            mirror(left, panel, value)

        product(whitener_ref, right, quad)
        first[...] = whitener_ref[...]

        def last(panel, value):
            at = lax.broadcasted_iota(jnp.int32, value.shape, 0)
            eye = at == lax.broadcasted_iota(jnp.int32, value.shape, 1) + panel[1].start
            value = 0.5 * (rest[panel] - value)
            value = value + jnp.where(eye, 0.5 * 3.0 * 2.25, 0.0)
            mirror(whitener_ref, panel, value * root)

        product(first, left, last)

    return kernel


def whiten(place, near, far, sums, count, rows, embed):
    square = (embed, embed)
    return pl.pallas_call(
        make_whiten_kernel(rows, count),
        in_specs=[smem()] + [vmem()] * (2 + len(sums)),
        out_specs=[vmem(), vmem()],
        out_shape=[
            jax.ShapeDtypeStruct(square, BF16),
            jax.ShapeDtypeStruct((1, embed), F32),
        ],
        scratch_shapes=[pltpu.VMEM(square, F32)] * 2 + [pltpu.VMEM(square, BF16)] * 3,
        compiler_params=params(24),
        cost_estimate=pl.CostEstimate(
            flops=5 * 2 * embed**3, bytes_accessed=2 * embed**2, transcendentals=0
        ),
        name="whiten",
    )(place, near, far, *sums)


def contrast_kernel(order, group_ref, mean_ref, whitener_ref, *refs):
    loss_ref, grad_ref, white, tables, numbers, offsets_ref, sem = refs[-11:-4]
    even, odd = (refs[-4], refs[-3]), (refs[-2], refs[-1])
    block_refs = [ref.at[i] for ref in refs[:-11] for i in range(ref.shape[0])]
    block_refs = [block_refs[order.index(k)] for k in range(len(order))]
    groups, rows, embed = white.shape
    group = group_ref[0]

    for k in range(0, groups, 2):
        pair = block_refs[k : k + 2]
        centered = [(ref[0:rows, :].astype(F32) - mean_ref[...]).astype(BF16) for ref in pair]
        value = dot(jnp.concatenate(centered, axis=0), whitener_ref[...]).astype(BF16)
        for side, ref in enumerate(pair):
            white[group ^ (k + side)] = value[side * rows : (side + 1) * rows]
            table = ref[rows:, :].astype(F32)[0:8]
            tables[group ^ (k + side)] = table
            numbers[group ^ (k + side)] = table[:, 0:LANES].astype(jnp.int32)
    copy = pltpu.make_async_copy(numbers, offsets_ref, sem)
    copy.start()
    copy.wait()

    places = lax.broadcasted_iota(jnp.int32, (rows, rows), 0).astype(F32)
    log2e = 1.4426950408889634

    def partner(g, k):
        return white[(g + offsets_ref[g, 1, k]) % groups]

    def scores(g, buffers):
        own = white[g]
        for k in range(PARTNERS):
            buffers[0][k * rows : (k + 1) * rows, :] = dot(partner(g, k), own, (1, 1))

    def softmax(g, buffers):
        loss = jnp.zeros((1, rows), F32)
        for k in range(PARTNERS):
            at = slice(k * rows, (k + 1) * rows)
            own = buffers[0][at, :]
            peak = jnp.max(own, axis=0, keepdims=True)
            powers = jnp.exp2((own - peak) * (LOGIT_SCALE * log2e))
            sums = jnp.sum(powers, axis=0, keepdims=True)
            hit = places == tables[g, 0:1, at]
            picked = jnp.sum(jnp.where(hit, own, 0.0), axis=0, keepdims=True)
            loss = loss + ((peak - picked) * LOGIT_SCALE + jnp.log(sums))
            share = powers * (1.0 / (PARTNERS * sums))
            weights = share - jnp.where(hit, 1.0 / PARTNERS, 0.0)
            buffers[1][at, :] = weights.astype(BF16)
        return loss * (1.0 / PARTNERS)

    def gradient(g, buffers):
        grad = dot(buffers[1][0:rows, :], partner(g, 0), (0, 0))
        for k in range(1, PARTNERS):
            grad = grad + dot(buffers[1][k * rows : (k + 1) * rows, :], partner(g, k), (0, 0))
        grad_ref[g] = (grad * LOGIT_SCALE).astype(BF16)

    scores(0, even)

    @pl.loop(0, groups // 2)
    def _(pair):
        g = 2 * pair
        scores(g + 1, odd)
        first = softmax(g, even)
        gradient(g, even)
        second = softmax(g + 1, odd)
        scores(lax.rem(g + 2, groups), even)
        gradient(g + 1, odd)

        @pl.when(pair == group // 2)
        def _():
            loss_ref[...] = jnp.where(group % 2 == 0, first, second)


def contrast(group, blocks, order, mean, whitener):
    groups = len(order)
    rows, embed = blocks[0].shape[1:]
    rows -= TAIL
    return pl.pallas_call(
        functools.partial(contrast_kernel, order),
        in_specs=[smem()] + [vmem()] * (2 + len(blocks)),
        out_specs=[vmem()] * 2,
        out_shape=[
            jax.ShapeDtypeStruct((1, rows), F32),
            jax.ShapeDtypeStruct((groups, rows, embed), BF16),
        ],
        scratch_shapes=[
            pltpu.VMEM((groups, rows, embed), BF16),
            pltpu.VMEM((groups, 8, embed), F32),
            pltpu.VMEM((groups, 8, LANES), jnp.int32),
            pltpu.SMEM((groups, 8, LANES), jnp.int32),
            pltpu.SemaphoreType.DMA,
        ]
        + [pltpu.VMEM((PARTNERS * rows, rows), F32), pltpu.VMEM((PARTNERS * rows, rows), BF16)] * 2,
        compiler_params=params(min(58, 12 + 6 * groups * rows * embed // 2**20)),
        cost_estimate=pl.CostEstimate(
            flops=groups * rows * 2 * embed * (embed + 2 * PARTNERS * rows),
            bytes_accessed=4 * groups * rows * embed,
            transcendentals=groups * PARTNERS * rows * rows,
        ),
        name="contrast",
    )(group, mean, whitener, *blocks)


def pieces_kernel(share, masks, order, group_ref, window_ref, grad_ref, *refs):
    groups = grad_ref.shape[0]
    features, (keep_ref, send_ref, total) = refs[:groups], refs[groups:]

    def columns(at):
        value = None
        for k, feature_ref in zip(order, features):
            term = dot(feature_ref[:, at], grad_ref[group_ref[0] ^ k], (0, 0))
            value = term if value is None else value + term
        return value

    if share % LANES:
        total[...] = columns(slice(None))
    for n, mask in enumerate(masks):
        at = pl.ds(pl.multiple_of((window_ref[0] ^ mask) * share, share), share)
        value = total[at, :] if share % LANES else columns(at)
        out, n = (send_ref, n - len(masks) // 2) if n >= len(masks) // 2 else (keep_ref, n)
        out[n * share : (n + 1) * share, :] = value.astype(out.dtype)


def weight_pieces(group, window, grad, slices, order, shares, masks):
    groups, rows, embed = grad.shape
    columns = slices[0].shape[1]
    share = columns // shares
    half = len(masks) // 2 * share
    return pl.pallas_call(
        functools.partial(pieces_kernel, share, masks, order),
        in_specs=[smem(), smem()] + [vmem()] * (1 + len(slices)),
        out_specs=[vmem()] * 2,
        out_shape=[
            jax.ShapeDtypeStruct((half, embed), F32),
            jax.ShapeDtypeStruct((half, embed), BF16),
        ],
        scratch_shapes=[pltpu.VMEM((columns if share % LANES else 8, embed), F32)],
        compiler_params=params(24),
        cost_estimate=pl.CostEstimate(
            flops=groups * rows * 2 * embed * share * len(masks),
            bytes_accessed=2 * groups * rows * (embed + columns),
            transcendentals=0,
        ),
        name="weight_pieces",
    )(group, window, grad, *slices)


def join_kernel(keep_ref, arrived_ref, out_ref):
    out_ref[...] = (keep_ref[...] + arrived_ref[...].astype(F32)).astype(BF16)


def join(keep, arrived):
    return pl.pallas_call(
        join_kernel,
        in_specs=[vmem()] * 2,
        out_specs=vmem(),
        out_shape=jax.ShapeDtypeStruct(keep.shape, BF16),
        compiler_params=params(8),
        name="join",
    )(keep, arrived)


def finish_kernel(*refs):
    keep_ref, whitener_ref, out_ref = refs[0], refs[-2], refs[-1]
    value = keep_ref[...]
    for ref in refs[1:-2]:
        value = value + ref[...].astype(F32)
    high, low = split(value)
    both = dot(jnp.concatenate([high, low], axis=0), whitener_ref[...], (1, 1))
    out_ref[...] = both[: value.shape[0]] + both[value.shape[0] :]


def finish(pieces, whitener):
    return pl.pallas_call(
        finish_kernel,
        in_specs=[vmem()] * (len(pieces) + 1),
        out_specs=vmem(),
        out_shape=jax.ShapeDtypeStruct(pieces[0].shape, F32),
        compiler_params=params(12),
        name="finish",
    )(*pieces, whitener)


def shards(features, proj_weight, partner_offsets, ortholog_index):
    rows, depth = features.shape
    embed = proj_weight.shape[1]
    groups = lax.axis_size("sp")
    shares = lax.axis_size("win")
    devices = groups * shares
    group = lax.axis_index("sp").astype(jnp.int32)
    window = lax.axis_index("win").astype(jnp.int32)
    me = group * shares + window

    direct = groups == 8
    by_x, by_near, by_far = shares, 2 * shares, 4 * shares
    if not direct:
        slices = features.reshape(rows, groups, depth // groups).transpose(1, 0, 2)
        slices = lax.all_to_all(slices, "sp", 0, 0)
        slices = [
            lax.dynamic_index_in_dim(slices, group ^ k, 0, keepdims=False) for k in range(groups)
        ]

    block, send, keep = project(
        me.reshape(1), partner_offsets, features, proj_weight, ortholog_index.T
    )
    block = block[None]
    if direct:
        block_x = xor_permute(block, by_x)
        block_far = xor_permute(block, by_far)
    else:
        gathered = lax.all_gather(block, "sp", tiled=True)

    arrived = [xor_permute(send, 1)]
    sent = send
    seen = 1
    stages = []
    low = 1
    place = me & 1
    while keep.shape[0] > 32:
        count = 4
        own = (me >> low) & (count - 1)
        keep, sends, seen = stage(own, keep, sent, arrived, seen, count, embed)
        if direct and stages:
            *sends, block_far, block_x = lax.optimization_barrier((*sends, block_far, block_x))
            far_x = xor_permute(block_far, by_x)
        arrived = [xor_permute(piece, (r + 1) << low) for r, piece in enumerate(sends)]
        sent = sends[0]
        stages.append((low, count))
        place = place * count + own
        low += 2
    size = keep.shape[0]
    part = keep
    for piece in arrived:
        part = part + piece[:size].astype(F32)
    sums = [sent, *arrived]
    extra = devices >> low
    if extra > 1:
        mine = jnp.concatenate([part.astype(BF16)] + [piece[size:] for piece in sums])
        others = [xor_permute(mine, r << low) for r in range(1, extra)]
        for piece in others:
            part = part + piece[:size].astype(F32)
        sums = [mine, *others]
    part = part.astype(BF16)
    for number, (low, count) in enumerate(reversed(stages)):
        if direct and number == 1:
            part, block_far, block = lax.optimization_barrier((part, block_far, block))
            far_near = xor_permute(block_far, by_near)
            block_near = xor_permute(block, by_near)
            part, far_x = lax.optimization_barrier((part, far_x))
        part = jnp.concatenate(
            [part] + [xor_permute(part, r << low) for r in range(1, count)], axis=0
        )
    part = part.reshape(-1, size, part.shape[1])
    if direct:
        group_scalar = group.reshape(1)
        part, far_near, group_scalar = lax.optimization_barrier((part, far_near, group_scalar))
        far_near_x = xor_permute(far_near, by_x)
        slices = list(cut(group_scalar, features, groups))
        slices[4] = xor_permute(slices[4], by_far)
    else:
        order = slice_order = list(range(groups))
        blocks = [
            lax.dynamic_index_in_dim(gathered, group ^ k, 0, keepdims=True) for k in order
        ]
    other = xor_permute(part, 1)
    whitener, mean = whiten(place.reshape(1), part, other, sums, seen, rows, embed)
    if direct:
        later = (2, 6, 5, 7, 1, 3)
        mean, block_near, far_near_x, slices[4], *held = lax.optimization_barrier(
            (mean, block_near, far_near_x, slices[4], *(slices[k] for k in later))
        )
        near_x = xor_permute(block_near, by_x)
        for k, piece in zip(later, held):
            slices[k] = xor_permute(piece, k * shares)
        slice_order = [0, 4, *later]
        slices = [slices[k] for k in slice_order]
        blocks = [block, block_x, block_near, near_x, block_far, far_x, far_near, far_near_x]
        order = list(range(groups))
    loss, grad = contrast(group.reshape(1), blocks, order, mean, whitener)
    group, window = group.reshape(1), window.reshape(1)
    pieces = []
    for mask in reversed(range(0, shares, 2)):
        keep, send = weight_pieces(
            group, window, grad, slices, slice_order, shares, (mask, mask + 1)
        )
        arrived = xor_permute(send, 1)
        if mask:
            pieces.append(xor_permute(join(keep, arrived), mask))
        else:
            pieces = [keep, arrived] + pieces
    return loss[0], finish(pieces, whitener)


def solution(mesh):
    return jax.shard_map(
        shards,
        mesh=mesh,
        in_specs=(P(("sp", "win"), None), P(), P("sp", None), P(("sp", "win"), None)),
        out_specs=(P(("sp", "win")), P(("sp", "win"), None)),
        check_vma=False,
    )
```

```python
import functools

import jax
import jax.numpy as jnp
from jax import lax
from jax.experimental import pallas as pl
from jax.experimental.pallas import tpu as pltpu
from jax.sharding import PartitionSpec as P

PARTNERS = 4
LOGIT_SCALE = 0.125
AXES = ("sp", "win")
LANES = 128
TAIL = 16
CHUNKS = 8
F32 = jnp.float32
BF16 = jnp.bfloat16
HIGHEST = lax.Precision.HIGHEST


def dot(a, b, contract=(1, 0), precision=None):
    return lax.dot_general(
        a,
        b,
        (((contract[0],), (contract[1],)), ((), ())),
        precision=precision,
        preferred_element_type=F32,
    )


def params(mebibytes, semantics=None):
    return pltpu.CompilerParams(
        vmem_limit_bytes=mebibytes * 2**20, dimension_semantics=semantics
    )


def vmem():
    return pl.BlockSpec(memory_space=pltpu.VMEM)


def smem():
    return pl.BlockSpec(memory_space=pltpu.SMEM)


def xor_permute(piece, mask):
    devices = lax.axis_size(AXES)
    return lax.ppermute(piece, AXES, [(i, i ^ mask) for i in range(devices)])


def split(value):
    high = value.astype(BF16)
    return high, (value - high.astype(F32)).astype(BF16)


def cut_kernel(group_ref, features_hbm, *refs):
    outs, sems = refs[:-1], refs[-1]
    columns = outs[0].shape[1]
    copies = []
    for k, out in enumerate(outs):
        start = pl.multiple_of((group_ref[0] ^ k) * columns, columns)
        copies.append(
            pltpu.make_async_copy(features_hbm.at[:, pl.ds(start, columns)], out, sems.at[k])
        )
        copies[k].start()
    for copy in copies:
        copy.wait()


def cut(group, features, groups):
    rows, depth = features.shape
    return pl.pallas_call(
        cut_kernel,
        in_specs=[smem(), pl.BlockSpec(memory_space=pltpu.HBM)],
        out_specs=[pl.BlockSpec(memory_space=pltpu.HBM)] * groups,
        out_shape=[jax.ShapeDtypeStruct((rows, depth // groups), BF16)] * groups,
        scratch_shapes=[pltpu.SemaphoreType.DMA((groups,))],
        compiler_params=params(8),
        name="cut",
    )(group, features)


def pack_sums(sums, packed, rows):
    high = sums.astype(BF16).astype(F32)
    pad = jnp.zeros((sums.shape[0], 2 * packed - sums.shape[1]), F32)
    lines = []
    for half in (high, sums - high):
        lines += [half[:, :packed], jnp.concatenate([half[:, packed:], pad], axis=1)]
    if rows > 4 * sums.shape[0]:
        lines.append(jnp.zeros((rows - 4 * sums.shape[0], packed), F32))
    return jnp.concatenate(lines, axis=0).astype(BF16)


def unpack_sums(block, count, embed):
    wide = block.astype(F32)
    packed = wide.shape[1]
    low = 2 * count
    left = wide[0:count] + wide[low : low + count]
    right = wide[count:low] + wide[low + count : low + 2 * count]
    return jnp.concatenate([left, right[:, : embed - packed]], axis=1)


def project_kernel(
    me_ref,
    offsets_ref,
    features_hbm,
    weight_hbm,
    ortholog_hbm,
    block_ref,
    send_ref,
    keep_ref,
    features_ref,
    weight_ref,
    ortholog_ref,
    means,
    wide,
    sems,
):
    rows = features_ref.shape[0]
    depth, embed = weight_ref.shape
    half, packed = keep_ref.shape
    blocks = embed // LANES
    tile = depth // CHUNKS

    copies = []
    for n in range(CHUNKS):
        at = pl.ds(n * tile, tile)
        copies.append(
            (
                pltpu.make_async_copy(features_hbm.at[:, at], features_ref.at[:, at], sems.at[0, n]),
                pltpu.make_async_copy(weight_hbm.at[at, :], weight_ref.at[at, :], sems.at[1, n]),
            )
        )
        for copy in copies[-1]:
            copy.start()
    table_copy = pltpu.make_async_copy(ortholog_hbm, ortholog_ref, sems.at[0, CHUNKS])
    table_copy.start()

    total = jnp.zeros((rows, embed), F32)
    for n in range(CHUNKS):
        for copy in copies[n]:
            copy.wait()
        at = slice(n * tile, (n + 1) * tile)
        total = total + dot(features_ref[:, at], weight_ref[at, :])
    projected = total.astype(BF16)
    block_ref[0:rows, :] = projected

    table_copy.wait()
    line = lax.broadcasted_iota(jnp.int32, (TAIL, embed), 0)
    lane = lax.broadcasted_iota(jnp.int32, (TAIL, embed), 1)
    table = jnp.zeros((TAIL, embed), F32)
    for k in range(PARTNERS):
        table = jnp.where((line == 1) & (lane == k), offsets_ref[0, k].astype(F32), table)
    hits = jnp.concatenate(
        [ortholog_ref[k : k + 1, :].astype(F32) for k in range(PARTNERS)]
        + ([jnp.zeros((1, embed - PARTNERS * rows), F32)] if embed > PARTNERS * rows else []),
        axis=1,
    )
    block_ref[rows:, :] = jnp.where(line == 0, hits, table).astype(BF16)

    sums = jnp.sum(projected.astype(F32), axis=0, keepdims=True)
    send_ref[half:, :] = pack_sums(sums, packed, TAIL)
    wide[:, :embed] = projected
    wide[:, embed:] = projected[:, : packed - LANES]
    ones = jnp.ones((rows, LANES), BF16)
    means[...] = jnp.broadcast_to(sums * (1.0 / rows), means.shape)
    core = me_ref[0] & 1
    for side, out in ((1, send_ref), (0, keep_ref)):
        for r in range(blocks // 2):
            block = (core ^ side) * (blocks // 2) + r
            start = pl.multiple_of(block * LANES, LANES)
            own = wide[:, pl.ds(start, LANES)]
            gram = dot(own, wide[:, pl.ds(start, packed)], (0, 0))
            sums = dot(own, ones, (0, 0))
            for k in range(packed // LANES):
                other = pl.multiple_of((block + k) % blocks * LANES, LANES)
                at = slice(k * LANES, (k + 1) * LANES)
                value = gram[:, at] - sums * means[0:1, pl.ds(other, LANES)]
                out[r * LANES : (r + 1) * LANES, at] = value.astype(out.dtype)


def project(me, offsets, features, weight, ortholog):
    rows, depth = features.shape
    embed = weight.shape[1]
    packed = embed // 2 + LANES
    hbm = pl.BlockSpec(memory_space=pltpu.HBM)
    return pl.pallas_call(
        project_kernel,
        in_specs=[smem(), smem(), hbm, hbm, hbm],
        out_specs=[vmem()] * 3,
        out_shape=[
            jax.ShapeDtypeStruct((rows + TAIL, embed), BF16),
            jax.ShapeDtypeStruct((embed // 2 + TAIL, packed), BF16),
            jax.ShapeDtypeStruct((embed // 2, packed), F32),
        ],
        scratch_shapes=[
            pltpu.VMEM((rows, depth), BF16),
            pltpu.VMEM((depth, embed), BF16),
            pltpu.VMEM((PARTNERS, rows), jnp.int32),
            pltpu.VMEM((8, embed), F32),
            pltpu.VMEM((rows, embed + packed - LANES), BF16),
            pltpu.SemaphoreType.DMA((2, CHUNKS + 1)),
        ],
        compiler_params=params(51),
        cost_estimate=pl.CostEstimate(
            flops=2 * rows * depth * embed, bytes_accessed=2 * depth * embed, transcendentals=0
        ),
        name="project",
    )(me, offsets, features, weight, ortholog)


def make_stage_kernel(seen, arrivals, count, embed):
    def kernel(own_ref, keep_ref, sent_ref, *refs):
        arrived, next_keep, outs = refs[:arrivals], refs[arrivals], refs[arrivals + 1 :]
        full, packed = keep_ref.shape
        share = full // count
        own = own_ref[0]
        sums = [unpack_sums(ref[full:, :], seen, embed) for ref in (sent_ref, *arrived)]
        block = pack_sums(jnp.concatenate(sums, axis=0), packed, outs[0].shape[0] - share)
        for r in range(count):
            at = pl.ds(pl.multiple_of((own ^ r) * share, share), share)
            value = keep_ref[at, :]
            for ref in arrived:
                value = value + ref[at, :].astype(F32)
            if r == 0:
                next_keep[...] = value
            else:
                outs[r - 1][:share, :] = value.astype(BF16)
                outs[r - 1][share:, :] = block

    return kernel


def stage(own, keep, sent, arrived, seen, count, embed):
    full, packed = keep.shape
    share = full // count
    held = seen * (1 + len(arrived))
    tail = -(-4 * held // TAIL) * TAIL
    out = pl.pallas_call(
        make_stage_kernel(seen, len(arrived), count, embed),
        in_specs=[smem()] + [vmem()] * (2 + len(arrived)),
        out_specs=[vmem()] * count,
        out_shape=[jax.ShapeDtypeStruct((share, packed), F32)]
        + [jax.ShapeDtypeStruct((share + tail, packed), BF16)] * (count - 1),
        compiler_params=params(16),
        cost_estimate=pl.CostEstimate(
            flops=full * packed, bytes_accessed=4 * full * packed, transcendentals=0
        ),
        name="stage",
    )(own.reshape(1), keep, sent, *arrived)
    return out[0], out[1:], held


def make_whiten_kernel(rows, count):
    def kernel(
        place_ref,
        near_ref,
        far_ref,
        *refs,
    ):
        sums_refs = refs[:-7]
        whitener_ref, mean_ref, scaled, rest, first, left, right = refs[-7:]
        place = place_ref[0]
        embed = scaled.shape[0]
        blocks = embed // LANES
        half = blocks // 2
        pieces, depth = near_ref.shape[:2]
        per_block = LANES // depth
        totals = jnp.concatenate(
            [
                unpack_sums(ref[start : start + 4 * count, :], count, embed)
                for ref in sums_refs
                for start in range(depth, ref.shape[0], 4 * count)
            ],
            axis=0,
        )
        total_rows = rows * totals.shape[0]
        tile = 256

        mean = jnp.sum(totals, axis=0, keepdims=True) * (1.0 / total_rows)
        mean_ref[...] = mean
        shift_high, shift_low = split(totals * (1.0 / rows) - mean)
        shift_left = jnp.concatenate([shift_high, shift_high, shift_low], axis=0)
        shift_right = jnp.concatenate([shift_high, shift_low, shift_high], axis=0)

        def block_at(i, j):
            return slice(i * LANES, (i + 1) * LANES), slice(j * LANES, (j + 1) * LANES)

        def unpack(source_ref, side):
            for i in range(side * half, (side + 1) * half):
                for part in range(per_block):
                    piece = ((i - side * half) * per_block + part) ^ (place % pieces)
                    wide = source_ref[piece].astype(F32)
                    lines = pl.ds(i * LANES + part * depth, depth)
                    for k in range(half + 1):
                        if k == half and side:
                            continue
                        j = (i + k) % blocks
                        scaled[lines, j * LANES : (j + 1) * LANES] = wide[
                            :, k * LANES : (k + 1) * LANES
                        ]

        for core in range(2):

            @pl.when(place // pieces == core)
            def _():
                unpack(near_ref, core)
                unpack(far_ref, 1 - core)

        for i in range(blocks):
            for j in range(blocks):
                held = (j - i) % blocks < half or ((j - i) % blocks == half and i < half)
                if not held and i * LANES // tile <= j * LANES // tile:
                    scaled[block_at(i, j)] = scaled[block_at(j, i)].T

        panels = []
        for t in range(embed // tile):
            panels.append((slice(0, (t + 1) * tile), slice(t * tile, (t + 1) * tile)))

        def mirror(out, panel, value):
            rows_at, columns_at = panel
            value = value.astype(BF16)
            out[panel] = value
            above = columns_at.start
            if above:
                out[columns_at, 0:above] = value[0:above].T

        squares = jnp.zeros((1, tile), F32)
        for panel in panels:
            rows_at, columns_at = panel
            between = dot(shift_left[:, rows_at], shift_right[:, columns_at], (0, 0))
            covariance = (scaled[panel] + rows * between) * (1.0 / total_rows)
            scaled[panel] = covariance
            mirror(first, panel, covariance)
            above = columns_at.start
            square = covariance * covariance
            squares = squares + jnp.sum(square[above:], axis=0, keepdims=True)
            if above:
                squares = squares + 2.0 * jnp.sum(square[:above], axis=0, keepdims=True)
        frobenius = jnp.sqrt(jnp.sum(squares, axis=1, keepdims=True))
        inverse = 1.0 / frobenius
        root = lax.rsqrt(frobenius)

        def product(one, two, finish):
            for panel in panels:
                finish(panel, dot(one[panel[0], :], two[:, panel[1]]))

        def second(panel, value):
            value = value * (inverse * inverse)
            own = scaled[panel] * inverse
            scaled[panel] = own
            rest[panel] = 27.0 * value - 39.0 * own
            mirror(left, panel, value)
            mirror(right, panel, value - 9.0 * own)

        product(first, first, second)

        def fourth(panel, value):
            value = (value + rest[panel]) * (1.0 / 16.0)
            rest[panel] = value
            mirror(whitener_ref, panel, value)

        product(left, right, fourth)

        def moved(panel, value):
            value = value * inverse
            scaled[panel] = 2.25 * 2.25 * scaled[panel] + 4.5 * value
            mirror(right, panel, value)

        product(first, whitener_ref, moved)

        def quad(panel, value):
            value = value + scaled[panel]
            rest[panel] = 3.0 * rest[panel] - 2.25 * value
            mirror(left, panel, value)

        product(whitener_ref, right, quad)
        first[...] = whitener_ref[...]

        def last(panel, value):
            at = lax.broadcasted_iota(jnp.int32, value.shape, 0)
            eye = at == lax.broadcasted_iota(jnp.int32, value.shape, 1) + panel[1].start
            value = 0.5 * (rest[panel] - value)
            value = value + jnp.where(eye, 0.5 * 3.0 * 2.25, 0.0)
            mirror(whitener_ref, panel, value * root)

        product(first, left, last)

    return kernel


def whiten(place, near, far, sums, count, rows, embed):
    square = (embed, embed)
    return pl.pallas_call(
        make_whiten_kernel(rows, count),
        in_specs=[smem()] + [vmem()] * (2 + len(sums)),
        out_specs=[vmem(), vmem()],
        out_shape=[
            jax.ShapeDtypeStruct(square, BF16),
            jax.ShapeDtypeStruct((1, embed), F32),
        ],
        scratch_shapes=[pltpu.VMEM(square, F32)] * 2 + [pltpu.VMEM(square, BF16)] * 3,
        compiler_params=params(24),
        cost_estimate=pl.CostEstimate(
            flops=5 * 2 * embed**3, bytes_accessed=2 * embed**2, transcendentals=0
        ),
        name="whiten",
    )(place, near, far, *sums)


def contrast_kernel(order, group_ref, mean_ref, whitener_ref, *refs):
    loss_ref, grad_ref, white, tables, numbers, offsets_ref, sem = refs[-11:-4]
    even, odd = (refs[-4], refs[-3]), (refs[-2], refs[-1])
    block_refs = [ref.at[i] for ref in refs[:-11] for i in range(ref.shape[0])]
    block_refs = [block_refs[order.index(k)] for k in range(len(order))]
    groups, rows, embed = white.shape
    group = group_ref[0]

    for k in range(0, groups, 2):
        pair = block_refs[k : k + 2]
        centered = [(ref[0:rows, :].astype(F32) - mean_ref[...]).astype(BF16) for ref in pair]
        value = dot(jnp.concatenate(centered, axis=0), whitener_ref[...]).astype(BF16)
        for side, ref in enumerate(pair):
            white[group ^ (k + side)] = value[side * rows : (side + 1) * rows]
            table = ref[rows:, :].astype(F32)[0:8]
            tables[group ^ (k + side)] = table
            numbers[group ^ (k + side)] = table[:, 0:LANES].astype(jnp.int32)
    copy = pltpu.make_async_copy(numbers, offsets_ref, sem)
    copy.start()
    copy.wait()

    places = lax.broadcasted_iota(jnp.int32, (rows, rows), 0).astype(F32)
    log2e = 1.4426950408889634

    def partner(g, k):
        return white[(g + offsets_ref[g, 1, k]) % groups]

    def scores(g, buffers):
        own = white[g]
        for k in range(PARTNERS):
            buffers[0][k * rows : (k + 1) * rows, :] = dot(partner(g, k), own, (1, 1))

    def softmax(g, buffers):
        loss = jnp.zeros((1, rows), F32)
        for k in range(PARTNERS):
            at = slice(k * rows, (k + 1) * rows)
            own = buffers[0][at, :]
            peak = jnp.max(own, axis=0, keepdims=True)
            powers = jnp.exp2((own - peak) * (LOGIT_SCALE * log2e))
            sums = jnp.sum(powers, axis=0, keepdims=True)
            hit = places == tables[g, 0:1, at]
            picked = jnp.sum(jnp.where(hit, own, 0.0), axis=0, keepdims=True)
            loss = loss + ((peak - picked) * LOGIT_SCALE + jnp.log(sums))
            share = powers * (1.0 / (PARTNERS * sums))
            weights = share - jnp.where(hit, 1.0 / PARTNERS, 0.0)
            buffers[1][at, :] = weights.astype(BF16)
        return loss * (1.0 / PARTNERS)

    def gradient(g, buffers):
        grad = dot(buffers[1][0:rows, :], partner(g, 0), (0, 0))
        for k in range(1, PARTNERS):
            grad = grad + dot(buffers[1][k * rows : (k + 1) * rows, :], partner(g, k), (0, 0))
        grad_ref[g] = (grad * LOGIT_SCALE).astype(BF16)

    scores(0, even)

    @pl.loop(0, groups // 2)
    def _(pair):
        g = 2 * pair
        scores(g + 1, odd)
        first = softmax(g, even)
        gradient(g, even)
        second = softmax(g + 1, odd)
        scores(lax.rem(g + 2, groups), even)
        gradient(g + 1, odd)

        @pl.when(pair == group // 2)
        def _():
            loss_ref[...] = jnp.where(group % 2 == 0, first, second)


def contrast(group, blocks, order, mean, whitener):
    groups = len(order)
    rows, embed = blocks[0].shape[1:]
    rows -= TAIL
    return pl.pallas_call(
        functools.partial(contrast_kernel, order),
        in_specs=[smem()] + [vmem()] * (2 + len(blocks)),
        out_specs=[vmem()] * 2,
        out_shape=[
            jax.ShapeDtypeStruct((1, rows), F32),
            jax.ShapeDtypeStruct((groups, rows, embed), BF16),
        ],
        scratch_shapes=[
            pltpu.VMEM((groups, rows, embed), BF16),
            pltpu.VMEM((groups, 8, embed), F32),
            pltpu.VMEM((groups, 8, LANES), jnp.int32),
            pltpu.SMEM((groups, 8, LANES), jnp.int32),
            pltpu.SemaphoreType.DMA,
        ]
        + [pltpu.VMEM((PARTNERS * rows, rows), F32), pltpu.VMEM((PARTNERS * rows, rows), BF16)] * 2,
        compiler_params=params(min(58, 12 + 6 * groups * rows * embed // 2**20)),
        cost_estimate=pl.CostEstimate(
            flops=groups * rows * 2 * embed * (embed + 2 * PARTNERS * rows),
            bytes_accessed=4 * groups * rows * embed,
            transcendentals=groups * PARTNERS * rows * rows,
        ),
        name="contrast",
    )(group, mean, whitener, *blocks)


def pieces_kernel(share, masks, order, group_ref, window_ref, grad_ref, *refs):
    groups = grad_ref.shape[0]
    features, (keep_ref, send_ref, total) = refs[:groups], refs[groups:]

    def columns(at):
        value = None
        for k, feature_ref in zip(order, features):
            term = dot(feature_ref[:, at], grad_ref[group_ref[0] ^ k], (0, 0))
            value = term if value is None else value + term
        return value

    if share % LANES:
        total[...] = columns(slice(None))
    for n, mask in enumerate(masks):
        at = pl.ds(pl.multiple_of((window_ref[0] ^ mask) * share, share), share)
        value = total[at, :] if share % LANES else columns(at)
        out, n = (send_ref, n - len(masks) // 2) if n >= len(masks) // 2 else (keep_ref, n)
        out[n * share : (n + 1) * share, :] = value.astype(out.dtype)


def weight_pieces(group, window, grad, slices, order, shares, masks):
    groups, rows, embed = grad.shape
    columns = slices[0].shape[1]
    share = columns // shares
    half = len(masks) // 2 * share
    return pl.pallas_call(
        functools.partial(pieces_kernel, share, masks, order),
        in_specs=[smem(), smem()] + [vmem()] * (1 + len(slices)),
        out_specs=[vmem()] * 2,
        out_shape=[
            jax.ShapeDtypeStruct((half, embed), F32),
            jax.ShapeDtypeStruct((half, embed), BF16),
        ],
        scratch_shapes=[pltpu.VMEM((columns if share % LANES else 8, embed), F32)],
        compiler_params=params(24),
        cost_estimate=pl.CostEstimate(
            flops=groups * rows * 2 * embed * share * len(masks),
            bytes_accessed=2 * groups * rows * (embed + columns),
            transcendentals=0,
        ),
        name="weight_pieces",
    )(group, window, grad, *slices)


def join_kernel(keep_ref, arrived_ref, out_ref):
    out_ref[...] = (keep_ref[...] + arrived_ref[...].astype(F32)).astype(BF16)


def join(keep, arrived):
    return pl.pallas_call(
        join_kernel,
        in_specs=[vmem()] * 2,
        out_specs=vmem(),
        out_shape=jax.ShapeDtypeStruct(keep.shape, BF16),
        compiler_params=params(8),
        name="join",
    )(keep, arrived)


def finish_kernel(*refs):
    keep_ref, whitener_ref, out_ref = refs[0], refs[-2], refs[-1]
    value = keep_ref[...]
    for ref in refs[1:-2]:
        value = value + ref[...].astype(F32)
    high, low = split(value)
    both = dot(jnp.concatenate([high, low], axis=0), whitener_ref[...], (1, 1))
    out_ref[...] = both[: value.shape[0]] + both[value.shape[0] :]


def finish(pieces, whitener):
    return pl.pallas_call(
        finish_kernel,
        in_specs=[vmem()] * (len(pieces) + 1),
        out_specs=vmem(),
        out_shape=jax.ShapeDtypeStruct(pieces[0].shape, F32),
        compiler_params=params(12),
        name="finish",
    )(*pieces, whitener)


def shards(features, proj_weight, partner_offsets, ortholog_index):
    rows, depth = features.shape
    embed = proj_weight.shape[1]
    groups = lax.axis_size("sp")
    shares = lax.axis_size("win")
    devices = groups * shares
    group = lax.axis_index("sp").astype(jnp.int32)
    window = lax.axis_index("win").astype(jnp.int32)
    me = group * shares + window

    direct = groups == 8
    by_x, by_near, by_far = shares, 2 * shares, 4 * shares
    if not direct:
        slices = features.reshape(rows, groups, depth // groups).transpose(1, 0, 2)
        slices = lax.all_to_all(slices, "sp", 0, 0)
        slices = [
            lax.dynamic_index_in_dim(slices, group ^ k, 0, keepdims=False) for k in range(groups)
        ]

    block, send, keep = project(
        me.reshape(1), partner_offsets, features, proj_weight, ortholog_index.T
    )
    block = block[None]
    if direct:
        block_x = xor_permute(block, by_x)
        block_far = xor_permute(block, by_far)
        block_near = xor_permute(block, by_near)
    else:
        gathered = lax.all_gather(block, "sp", tiled=True)

    arrived = [xor_permute(send, 1)]
    if direct:
        arrived[0], block_x = lax.optimization_barrier((arrived[0], block_x))
    sent = send
    seen = 1
    stages = []
    low = 1
    place = me & 1
    while keep.shape[0] > 32:
        count = 4
        own = (me >> low) & (count - 1)
        keep, sends, seen = stage(own, keep, sent, arrived, seen, count, embed)
        if direct and stages:
            group_scalar = group.reshape(1)
            *sends, block_near, block_far, group_scalar = lax.optimization_barrier(
                (*sends, block_near, block_far, group_scalar)
            )
            slices = cut(group_scalar, features, groups)
            far_x = xor_permute(block_far, by_x)
        arrived = [xor_permute(piece, (r + 1) << low) for r, piece in enumerate(sends)]
        sent = sends[0]
        stages.append((low, count))
        place = place * count + own
        low += 2
    size = keep.shape[0]
    part = keep
    for piece in arrived:
        part = part + piece[:size].astype(F32)
    sums = [sent, *arrived]
    extra = devices >> low
    if extra > 1:
        mine = jnp.concatenate([part.astype(BF16)] + [piece[size:] for piece in sums])
        others = [xor_permute(mine, r << low) for r in range(1, extra)]
        for piece in others:
            part = part + piece[:size].astype(F32)
        sums = [mine, *others]
    part = part.astype(BF16)
    for number, (low, count) in enumerate(reversed(stages)):
        if direct and number == 1:
            part, block_far = lax.optimization_barrier((part, block_far))
            block_far_near = xor_permute(block_far, by_near)
            part, far_x = lax.optimization_barrier((part, far_x))
        part = jnp.concatenate(
            [part] + [xor_permute(part, r << low) for r in range(1, count)], axis=0
        )
    part = part.reshape(-1, size, part.shape[1])
    if direct:
        part, block_far_near = lax.optimization_barrier((part, block_far_near))
        pair_x = xor_permute(jnp.concatenate([block_near, block_far_near]), by_x)
        blocks = [block, block_x, block_near, block_far, far_x, block_far_near, pair_x]
        order = [0, 1, 2, 4, 5, 6, 3, 7]
    else:
        order = slice_order = list(range(groups))
        blocks = [
            lax.dynamic_index_in_dim(gathered, group ^ k, 0, keepdims=True) for k in order
        ]
    other = xor_permute(part, 1)
    if direct:
        other, *slices = lax.optimization_barrier((other, *slices))
        slice_order = [0, 2, 4, 6, 1, 3, 5, 7]
        slices = [xor_permute(slices[k], k * shares) if k else slices[k] for k in slice_order]

    whitener, mean = whiten(place.reshape(1), part, other, sums, seen, rows, embed)
    loss, grad = contrast(group.reshape(1), blocks, order, mean, whitener)
    group, window = group.reshape(1), window.reshape(1)
    pieces = []
    for mask in reversed(range(0, shares, 2)):
        keep, send = weight_pieces(
            group, window, grad, slices, slice_order, shares, (mask, mask + 1)
        )
        arrived = xor_permute(send, 1)
        if mask:
            pieces.append(xor_permute(join(keep, arrived), mask))
        else:
            pieces = [keep, arrived] + pieces
    return loss[0], finish(pieces, whitener)


def solution(mesh):
    return jax.shard_map(
        shards,
        mesh=mesh,
        in_specs=(P(("sp", "win"), None), P(), P("sp", None), P(("sp", "win"), None)),
        out_specs=(P(("sp", "win")), P(("sp", "win"), None)),
        check_vma=False,
    )
```

```python
import functools

import jax
import jax.numpy as jnp
from jax import lax
from jax.experimental import pallas as pl
from jax.experimental.pallas import tpu as pltpu
from jax.sharding import PartitionSpec as P

PARTNERS = 4
LOGIT_SCALE = 0.125
AXES = ("sp", "win")
LANES = 128
TAIL = 16
CHUNKS = 8
F32 = jnp.float32
BF16 = jnp.bfloat16
HIGHEST = lax.Precision.HIGHEST


def dot(a, b, contract=(1, 0), precision=None):
    return lax.dot_general(
        a,
        b,
        (((contract[0],), (contract[1],)), ((), ())),
        precision=precision,
        preferred_element_type=F32,
    )


def params(mebibytes, semantics=None):
    return pltpu.CompilerParams(
        vmem_limit_bytes=mebibytes * 2**20, dimension_semantics=semantics
    )


def vmem():
    return pl.BlockSpec(memory_space=pltpu.VMEM)


def smem():
    return pl.BlockSpec(memory_space=pltpu.SMEM)


def xor_permute(piece, mask):
    devices = lax.axis_size(AXES)
    return lax.ppermute(piece, AXES, [(i, i ^ mask) for i in range(devices)])


def split(value):
    high = value.astype(BF16)
    return high, (value - high.astype(F32)).astype(BF16)


def cut_kernel(ids_ref, features_hbm, *refs):
    outs, sems = refs[:-1], refs[-1]
    columns = outs[0].shape[1]
    copies = []
    for k, out in enumerate(outs):
        start = pl.multiple_of((ids_ref[0] ^ k) * columns, columns)
        copies.append(
            pltpu.make_async_copy(features_hbm.at[:, pl.ds(start, columns)], out, sems.at[k])
        )
        copies[k].start()
    for copy in copies:
        copy.wait()


def cut(ids, features, groups):
    rows, depth = features.shape
    return pl.pallas_call(
        cut_kernel,
        in_specs=[smem(), pl.BlockSpec(memory_space=pltpu.HBM)],
        out_specs=[pl.BlockSpec(memory_space=pltpu.HBM)] * groups,
        out_shape=[jax.ShapeDtypeStruct((rows, depth // groups), BF16)] * groups,
        scratch_shapes=[pltpu.SemaphoreType.DMA((groups,))],
        compiler_params=params(8),
        name="cut",
    )(ids, features)


def pack_sums(sums, packed, rows):
    high = sums.astype(BF16).astype(F32)
    pad = jnp.zeros((sums.shape[0], 2 * packed - sums.shape[1]), F32)
    lines = []
    for half in (high, sums - high):
        lines += [half[:, :packed], jnp.concatenate([half[:, packed:], pad], axis=1)]
    if rows > 4 * sums.shape[0]:
        lines.append(jnp.zeros((rows - 4 * sums.shape[0], packed), F32))
    return jnp.concatenate(lines, axis=0).astype(BF16)


def unpack_sums(block, count, embed):
    wide = block.astype(F32)
    packed = wide.shape[1]
    low = 2 * count
    left = wide[0:count] + wide[low : low + count]
    right = wide[count:low] + wide[low + count : low + 2 * count]
    return jnp.concatenate([left, right[:, : embed - packed]], axis=1)


def project_kernel(
    ids_ref,
    offsets_ref,
    features_hbm,
    weight_hbm,
    ortholog_hbm,
    block_ref,
    send_ref,
    keep_ref,
    features_ref,
    weight_ref,
    ortholog_ref,
    means,
    wide,
    sems,
):
    rows = features_ref.shape[0]
    depth, embed = weight_ref.shape
    half, packed = keep_ref.shape
    blocks = embed // LANES
    tile = depth // CHUNKS

    copies = []
    for n in range(CHUNKS):
        at = pl.ds(n * tile, tile)
        copies.append(
            (
                pltpu.make_async_copy(features_hbm.at[:, at], features_ref.at[:, at], sems.at[0, n]),
                pltpu.make_async_copy(weight_hbm.at[at, :], weight_ref.at[at, :], sems.at[1, n]),
            )
        )
        for copy in copies[-1]:
            copy.start()
    table_copy = pltpu.make_async_copy(ortholog_hbm, ortholog_ref, sems.at[0, CHUNKS])
    table_copy.start()

    total = jnp.zeros((rows, embed), F32)
    for n in range(CHUNKS):
        for copy in copies[n]:
            copy.wait()
        at = slice(n * tile, (n + 1) * tile)
        total = total + dot(features_ref[:, at], weight_ref[at, :])
    projected = total.astype(BF16)
    block_ref[0:rows, :] = projected

    table_copy.wait()
    line = lax.broadcasted_iota(jnp.int32, (TAIL, embed), 0)
    lane = lax.broadcasted_iota(jnp.int32, (TAIL, embed), 1)
    table = jnp.zeros((TAIL, embed), F32)
    for k in range(PARTNERS):
        table = jnp.where((line == 1) & (lane == k), offsets_ref[0, k].astype(F32), table)
    hits = jnp.concatenate(
        [ortholog_ref[k : k + 1, :].astype(F32) for k in range(PARTNERS)]
        + ([jnp.zeros((1, embed - PARTNERS * rows), F32)] if embed > PARTNERS * rows else []),
        axis=1,
    )
    block_ref[rows:, :] = jnp.where(line == 0, hits, table).astype(BF16)

    sums = jnp.sum(projected.astype(F32), axis=0, keepdims=True)
    send_ref[half:, :] = pack_sums(sums, packed, TAIL)
    wide[:, :embed] = projected
    wide[:, embed:] = projected[:, : packed - LANES]
    ones = jnp.ones((rows, LANES), BF16)
    means[...] = jnp.broadcast_to(sums * (1.0 / rows), means.shape)
    core = ids_ref[2] & 1
    for side, out in ((1, send_ref), (0, keep_ref)):
        for r in range(blocks // 2):
            block = (core ^ side) * (blocks // 2) + r
            start = pl.multiple_of(block * LANES, LANES)
            own = wide[:, pl.ds(start, LANES)]
            gram = dot(own, wide[:, pl.ds(start, packed)], (0, 0))
            sums = dot(own, ones, (0, 0))
            for k in range(packed // LANES):
                other = pl.multiple_of((block + k) % blocks * LANES, LANES)
                at = slice(k * LANES, (k + 1) * LANES)
                value = gram[:, at] - sums * means[0:1, pl.ds(other, LANES)]
                out[r * LANES : (r + 1) * LANES, at] = value.astype(out.dtype)


def project(ids, offsets, features, weight, ortholog):
    rows, depth = features.shape
    embed = weight.shape[1]
    packed = embed // 2 + LANES
    hbm = pl.BlockSpec(memory_space=pltpu.HBM)
    return pl.pallas_call(
        project_kernel,
        in_specs=[smem(), smem(), hbm, hbm, hbm],
        out_specs=[vmem()] * 3,
        out_shape=[
            jax.ShapeDtypeStruct((rows + TAIL, embed), BF16),
            jax.ShapeDtypeStruct((embed // 2 + TAIL, packed), BF16),
            jax.ShapeDtypeStruct((embed // 2, packed), F32),
        ],
        scratch_shapes=[
            pltpu.VMEM((rows, depth), BF16),
            pltpu.VMEM((depth, embed), BF16),
            pltpu.VMEM((PARTNERS, rows), jnp.int32),
            pltpu.VMEM((8, embed), F32),
            pltpu.VMEM((rows, embed + packed - LANES), BF16),
            pltpu.SemaphoreType.DMA((2, CHUNKS + 1)),
        ],
        compiler_params=params(51),
        cost_estimate=pl.CostEstimate(
            flops=2 * rows * depth * embed, bytes_accessed=2 * depth * embed, transcendentals=0
        ),
        name="project",
    )(ids, offsets, features, weight, ortholog)


def make_stage_kernel(seen, arrivals, low, count, embed):
    def kernel(ids_ref, keep_ref, sent_ref, *refs):
        arrived, next_keep, outs = refs[:arrivals], refs[arrivals], refs[arrivals + 1 :]
        full, packed = keep_ref.shape
        share = full // count
        own = (ids_ref[2] >> low) & (count - 1)
        sums = [unpack_sums(ref[full:, :], seen, embed) for ref in (sent_ref, *arrived)]
        block = pack_sums(jnp.concatenate(sums, axis=0), packed, outs[0].shape[0] - share)
        for r in range(count):
            at = pl.ds(pl.multiple_of((own ^ r) * share, share), share)
            value = keep_ref[at, :]
            for ref in arrived:
                value = value + ref[at, :].astype(F32)
            if r == 0:
                next_keep[...] = value
            else:
                outs[r - 1][:share, :] = value.astype(BF16)
                outs[r - 1][share:, :] = block

    return kernel


def stage(ids, keep, sent, arrived, seen, low, count, embed):
    full, packed = keep.shape
    share = full // count
    held = seen * (1 + len(arrived))
    tail = -(-4 * held // TAIL) * TAIL
    out = pl.pallas_call(
        make_stage_kernel(seen, len(arrived), low, count, embed),
        in_specs=[smem()] + [vmem()] * (2 + len(arrived)),
        out_specs=[vmem()] * count,
        out_shape=[jax.ShapeDtypeStruct((share, packed), F32)]
        + [jax.ShapeDtypeStruct((share + tail, packed), BF16)] * (count - 1),
        compiler_params=params(16),
        cost_estimate=pl.CostEstimate(
            flops=full * packed, bytes_accessed=4 * full * packed, transcendentals=0
        ),
        name="stage",
    )(ids, keep, sent, *arrived)
    return out[0], out[1:], held


def make_whiten_kernel(rows, count, stages):
    def kernel(
        ids_ref,
        near_ref,
        far_ref,
        *refs,
    ):
        sums_refs = refs[:-7]
        whitener_ref, mean_ref, scaled, rest, first, left, right = refs[-7:]
        me = ids_ref[2]
        place = me & 1
        for low, size in stages:
            place = place * size + ((me >> low) & (size - 1))
        embed = scaled.shape[0]
        blocks = embed // LANES
        half = blocks // 2
        pieces, depth = near_ref.shape[:2]
        per_block = LANES // depth
        totals = jnp.concatenate(
            [
                unpack_sums(ref[start : start + 4 * count, :], count, embed)
                for ref in sums_refs
                for start in range(depth, ref.shape[0], 4 * count)
            ],
            axis=0,
        )
        total_rows = rows * totals.shape[0]
        tile = 256

        mean = jnp.sum(totals, axis=0, keepdims=True) * (1.0 / total_rows)
        mean_ref[...] = mean
        shift_high, shift_low = split(totals * (1.0 / rows) - mean)
        shift_left = jnp.concatenate([shift_high, shift_high, shift_low], axis=0)
        shift_right = jnp.concatenate([shift_high, shift_low, shift_high], axis=0)

        def block_at(i, j):
            return slice(i * LANES, (i + 1) * LANES), slice(j * LANES, (j + 1) * LANES)

        def unpack(source_ref, side):
            for i in range(side * half, (side + 1) * half):
                for part in range(per_block):
                    piece = ((i - side * half) * per_block + part) ^ (place % pieces)
                    wide = source_ref[piece].astype(F32)
                    lines = pl.ds(i * LANES + part * depth, depth)
                    for k in range(half + 1):
                        if k == half and side:
                            continue
                        j = (i + k) % blocks
                        scaled[lines, j * LANES : (j + 1) * LANES] = wide[
                            :, k * LANES : (k + 1) * LANES
                        ]

        for core in range(2):

            @pl.when(place // pieces == core)
            def _():
                unpack(near_ref, core)
                unpack(far_ref, 1 - core)

        for i in range(blocks):
            for j in range(blocks):
                held = (j - i) % blocks < half or ((j - i) % blocks == half and i < half)
                if not held and i * LANES // tile <= j * LANES // tile:
                    scaled[block_at(i, j)] = scaled[block_at(j, i)].T

        panels = []
        for t in range(embed // tile):
            panels.append((slice(0, (t + 1) * tile), slice(t * tile, (t + 1) * tile)))

        def mirror(out, panel, value):
            rows_at, columns_at = panel
            value = value.astype(BF16)
            out[panel] = value
            above = columns_at.start
            if above:
                out[columns_at, 0:above] = value[0:above].T

        squares = jnp.zeros((1, tile), F32)
        for panel in panels:
            rows_at, columns_at = panel
            between = dot(shift_left[:, rows_at], shift_right[:, columns_at], (0, 0))
            covariance = (scaled[panel] + rows * between) * (1.0 / total_rows)
            scaled[panel] = covariance
            mirror(first, panel, covariance)
            above = columns_at.start
            square = covariance * covariance
            squares = squares + jnp.sum(square[above:], axis=0, keepdims=True)
            if above:
                squares = squares + 2.0 * jnp.sum(square[:above], axis=0, keepdims=True)
        frobenius = jnp.sqrt(jnp.sum(squares, axis=1, keepdims=True))
        inverse = 1.0 / frobenius
        root = lax.rsqrt(frobenius)

        def product(one, two, finish):
            for panel in panels:
                finish(panel, dot(one[panel[0], :], two[:, panel[1]]))

        def second(panel, value):
            value = value * (inverse * inverse)
            own = scaled[panel] * inverse
            scaled[panel] = own
            rest[panel] = 27.0 * value - 39.0 * own
            mirror(left, panel, value)
            mirror(right, panel, value - 9.0 * own)

        product(first, first, second)

        def fourth(panel, value):
            value = (value + rest[panel]) * (1.0 / 16.0)
            rest[panel] = value
            mirror(whitener_ref, panel, value)

        product(left, right, fourth)

        def moved(panel, value):
            value = value * inverse
            scaled[panel] = 2.25 * 2.25 * scaled[panel] + 4.5 * value
            mirror(right, panel, value)

        product(first, whitener_ref, moved)

        def quad(panel, value):
            value = value + scaled[panel]
            rest[panel] = 3.0 * rest[panel] - 2.25 * value
            mirror(left, panel, value)

        product(whitener_ref, right, quad)
        first[...] = whitener_ref[...]

        def last(panel, value):
            at = lax.broadcasted_iota(jnp.int32, value.shape, 0)
            eye = at == lax.broadcasted_iota(jnp.int32, value.shape, 1) + panel[1].start
            value = 0.5 * (rest[panel] - value)
            value = value + jnp.where(eye, 0.5 * 3.0 * 2.25, 0.0)
            mirror(whitener_ref, panel, value * root)

        product(first, left, last)

    return kernel


def whiten(ids, near, far, sums, count, stages, rows, embed):
    square = (embed, embed)
    return pl.pallas_call(
        make_whiten_kernel(rows, count, stages),
        in_specs=[smem()] + [vmem()] * (2 + len(sums)),
        out_specs=[vmem(), vmem()],
        out_shape=[
            jax.ShapeDtypeStruct(square, BF16),
            jax.ShapeDtypeStruct((1, embed), F32),
        ],
        scratch_shapes=[pltpu.VMEM(square, F32)] * 2 + [pltpu.VMEM(square, BF16)] * 3,
        compiler_params=params(24),
        cost_estimate=pl.CostEstimate(
            flops=5 * 2 * embed**3, bytes_accessed=2 * embed**2, transcendentals=0
        ),
        name="whiten",
    )(ids, near, far, *sums)


def contrast_kernel(order, ids_ref, mean_ref, whitener_ref, *refs):
    loss_ref, grad_ref, white, tables, numbers, offsets_ref, sem = refs[-11:-4]
    even, odd = (refs[-4], refs[-3]), (refs[-2], refs[-1])
    block_refs = [ref.at[i] for ref in refs[:-11] for i in range(ref.shape[0])]
    block_refs = [block_refs[order.index(k)] for k in range(len(order))]
    groups, rows, embed = white.shape
    group = ids_ref[0]

    for k in range(0, groups, 2):
        pair = block_refs[k : k + 2]
        centered = [(ref[0:rows, :].astype(F32) - mean_ref[...]).astype(BF16) for ref in pair]
        value = dot(jnp.concatenate(centered, axis=0), whitener_ref[...]).astype(BF16)
        for side, ref in enumerate(pair):
            white[group ^ (k + side)] = value[side * rows : (side + 1) * rows]
            table = ref[rows:, :].astype(F32)[0:8]
            tables[group ^ (k + side)] = table
            numbers[group ^ (k + side)] = table[:, 0:LANES].astype(jnp.int32)
    copy = pltpu.make_async_copy(numbers, offsets_ref, sem)
    copy.start()
    copy.wait()

    places = lax.broadcasted_iota(jnp.int32, (rows, rows), 0).astype(F32)
    log2e = 1.4426950408889634

    def partner(g, k):
        return white[(g + offsets_ref[g, 1, k]) % groups]

    def scores(g, buffers):
        own = white[g]
        for k in range(PARTNERS):
            buffers[0][k * rows : (k + 1) * rows, :] = dot(partner(g, k), own, (1, 1))

    def softmax(g, buffers):
        loss = jnp.zeros((1, rows), F32)
        for k in range(PARTNERS):
            at = slice(k * rows, (k + 1) * rows)
            own = buffers[0][at, :]
            peak = jnp.max(own, axis=0, keepdims=True)
            powers = jnp.exp2((own - peak) * (LOGIT_SCALE * log2e))
            sums = jnp.sum(powers, axis=0, keepdims=True)
            hit = places == tables[g, 0:1, at]
            picked = jnp.sum(jnp.where(hit, own, 0.0), axis=0, keepdims=True)
            loss = loss + ((peak - picked) * LOGIT_SCALE + jnp.log(sums))
            share = powers * (1.0 / (PARTNERS * sums))
            weights = share - jnp.where(hit, 1.0 / PARTNERS, 0.0)
            buffers[1][at, :] = weights.astype(BF16)
        return loss * (1.0 / PARTNERS)

    def gradient(g, buffers):
        grad = dot(buffers[1][0:rows, :], partner(g, 0), (0, 0))
        for k in range(1, PARTNERS):
            grad = grad + dot(buffers[1][k * rows : (k + 1) * rows, :], partner(g, k), (0, 0))
        grad_ref[g] = (grad * LOGIT_SCALE).astype(BF16)

    scores(0, even)

    @pl.loop(0, groups // 2)
    def _(pair):
        g = 2 * pair
        scores(g + 1, odd)
        first = softmax(g, even)
        gradient(g, even)
        second = softmax(g + 1, odd)
        scores(lax.rem(g + 2, groups), even)
        gradient(g + 1, odd)

        @pl.when(pair == group // 2)
        def _():
            loss_ref[...] = jnp.where(group % 2 == 0, first, second)


def contrast(ids, blocks, order, mean, whitener):
    groups = len(order)
    rows, embed = blocks[0].shape[1:]
    rows -= TAIL
    return pl.pallas_call(
        functools.partial(contrast_kernel, order),
        in_specs=[smem()] + [vmem()] * (2 + len(blocks)),
        out_specs=[vmem()] * 2,
        out_shape=[
            jax.ShapeDtypeStruct((1, rows), F32),
            jax.ShapeDtypeStruct((groups, rows, embed), BF16),
        ],
        scratch_shapes=[
            pltpu.VMEM((groups, rows, embed), BF16),
            pltpu.VMEM((groups, 8, embed), F32),
            pltpu.VMEM((groups, 8, LANES), jnp.int32),
            pltpu.SMEM((groups, 8, LANES), jnp.int32),
            pltpu.SemaphoreType.DMA,
        ]
        + [pltpu.VMEM((PARTNERS * rows, rows), F32), pltpu.VMEM((PARTNERS * rows, rows), BF16)] * 2,
        compiler_params=params(min(58, 12 + 6 * groups * rows * embed // 2**20)),
        cost_estimate=pl.CostEstimate(
            flops=groups * rows * 2 * embed * (embed + 2 * PARTNERS * rows),
            bytes_accessed=4 * groups * rows * embed,
            transcendentals=groups * PARTNERS * rows * rows,
        ),
        name="contrast",
    )(ids, mean, whitener, *blocks)


def pieces_kernel(share, masks, order, ids_ref, grad_ref, *refs):
    groups = grad_ref.shape[0]
    features, (keep_ref, send_ref, total) = refs[:groups], refs[groups:]

    def columns(at):
        value = None
        for k, feature_ref in zip(order, features):
            term = dot(feature_ref[:, at], grad_ref[ids_ref[0] ^ k], (0, 0))
            value = term if value is None else value + term
        return value

    if share % LANES:
        total[...] = columns(slice(None))
    for n, mask in enumerate(masks):
        at = pl.ds(pl.multiple_of((ids_ref[1] ^ mask) * share, share), share)
        value = total[at, :] if share % LANES else columns(at)
        out, n = (send_ref, n - len(masks) // 2) if n >= len(masks) // 2 else (keep_ref, n)
        out[n * share : (n + 1) * share, :] = value.astype(out.dtype)


def weight_pieces(ids, grad, slices, order, shares, masks):
    groups, rows, embed = grad.shape
    columns = slices[0].shape[1]
    share = columns // shares
    half = len(masks) // 2 * share
    return pl.pallas_call(
        functools.partial(pieces_kernel, share, masks, order),
        in_specs=[smem()] + [vmem()] * (1 + len(slices)),
        out_specs=[vmem()] * 2,
        out_shape=[
            jax.ShapeDtypeStruct((half, embed), F32),
            jax.ShapeDtypeStruct((half, embed), BF16),
        ],
        scratch_shapes=[pltpu.VMEM((columns if share % LANES else 8, embed), F32)],
        compiler_params=params(24),
        cost_estimate=pl.CostEstimate(
            flops=groups * rows * 2 * embed * share * len(masks),
            bytes_accessed=2 * groups * rows * (embed + columns),
            transcendentals=0,
        ),
        name="weight_pieces",
    )(ids, grad, *slices)


def join_kernel(keep_ref, arrived_ref, out_ref):
    out_ref[...] = (keep_ref[...] + arrived_ref[...].astype(F32)).astype(BF16)


def join(keep, arrived):
    return pl.pallas_call(
        join_kernel,
        in_specs=[vmem()] * 2,
        out_specs=vmem(),
        out_shape=jax.ShapeDtypeStruct(keep.shape, BF16),
        compiler_params=params(8),
        name="join",
    )(keep, arrived)


def finish_kernel(*refs):
    keep_ref, whitener_ref, out_ref = refs[0], refs[-2], refs[-1]
    value = keep_ref[...]
    for ref in refs[1:-2]:
        value = value + ref[...].astype(F32)
    high, low = split(value)
    both = dot(jnp.concatenate([high, low], axis=0), whitener_ref[...], (1, 1))
    out_ref[...] = both[: value.shape[0]] + both[value.shape[0] :]


def finish(pieces, whitener):
    return pl.pallas_call(
        finish_kernel,
        in_specs=[vmem()] * (len(pieces) + 1),
        out_specs=vmem(),
        out_shape=jax.ShapeDtypeStruct(pieces[0].shape, F32),
        compiler_params=params(12),
        name="finish",
    )(*pieces, whitener)


def shards(features, proj_weight, partner_offsets, ortholog_index):
    rows, depth = features.shape
    embed = proj_weight.shape[1]
    groups = lax.axis_size("sp")
    shares = lax.axis_size("win")
    devices = groups * shares
    group = lax.axis_index("sp").astype(jnp.int32)
    window = lax.axis_index("win").astype(jnp.int32)
    me = group * shares + window
    ids = jnp.stack([group, window, me])

    direct = groups == 8
    by_x, by_near, by_far = shares, 2 * shares, 4 * shares
    if not direct:
        slices = features.reshape(rows, groups, depth // groups).transpose(1, 0, 2)
        slices = lax.all_to_all(slices, "sp", 0, 0)
        slices = [
            lax.dynamic_index_in_dim(slices, group ^ k, 0, keepdims=False) for k in range(groups)
        ]

    block, send, keep = project(
        ids, partner_offsets, features, proj_weight, ortholog_index.T
    )
    block = block[None]
    if direct:
        block_x = xor_permute(block, by_x)
        block_far = xor_permute(block, by_far)
        block_near = xor_permute(block, by_near)
    else:
        gathered = lax.all_gather(block, "sp", tiled=True)

    arrived = [xor_permute(send, 1)]
    if direct:
        arrived[0], block_x = lax.optimization_barrier((arrived[0], block_x))
    sent = send
    seen = 1
    stages = []
    low = 1
    while keep.shape[0] > 32:
        count = 4
        keep, sends, seen = stage(ids, keep, sent, arrived, seen, low, count, embed)
        if direct and stages:
            *sends, block_near, block_far = lax.optimization_barrier(
                (*sends, block_near, block_far)
            )
            pair_x = xor_permute(jnp.concatenate([block_far, block_near]), by_x)
        arrived = [xor_permute(piece, (r + 1) << low) for r, piece in enumerate(sends)]
        sent = sends[0]
        stages.append((low, count))
        low += 2
    size = keep.shape[0]
    part = keep
    for piece in arrived:
        part = part + piece[:size].astype(F32)
    sums = [sent, *arrived]
    extra = devices >> low
    if extra > 1:
        mine = jnp.concatenate([part.astype(BF16)] + [piece[size:] for piece in sums])
        others = [xor_permute(mine, r << low) for r in range(1, extra)]
        for piece in others:
            part = part + piece[:size].astype(F32)
        sums = [mine, *others]
    part = part.astype(BF16)
    for number, (low, count) in enumerate(reversed(stages)):
        if direct and number == 1:
            part, block_far = lax.optimization_barrier((part, block_far))
            block_far_near = xor_permute(block_far, by_near)
            part, pair_x = lax.optimization_barrier((part, pair_x))
        part = jnp.concatenate(
            [part] + [xor_permute(part, r << low) for r in range(1, count)], axis=0
        )
    part = part.reshape(-1, size, part.shape[1])
    if direct:
        part, block_far_near, ids = lax.optimization_barrier((part, block_far_near, ids))
        slices = cut(ids, features, groups)
        far_near_x = xor_permute(block_far_near, by_x)
        blocks = [block, block_x, block_near, block_far, pair_x, block_far_near, far_near_x]
        order = [0, 1, 2, 4, 5, 3, 6, 7]
    else:
        order = slice_order = list(range(groups))
        blocks = [
            lax.dynamic_index_in_dim(gathered, group ^ k, 0, keepdims=True) for k in order
        ]
    other = xor_permute(part, 1)
    if direct:
        other, *slices = lax.optimization_barrier((other, *slices))
        slice_order = [0, 4, 2, 6, 1, 3, 5, 7]
        slices = [xor_permute(slices[k], k * shares) if k else slices[k] for k in slice_order]

    whitener, mean = whiten(ids, part, other, sums, seen, tuple(stages), rows, embed)
    loss, grad = contrast(ids, blocks, order, mean, whitener)
    pieces = []
    for mask in reversed(range(0, shares, 2)):
        keep, send = weight_pieces(
            ids, grad, slices, slice_order, shares, (mask, mask + 1)
        )
        arrived = xor_permute(send, 1)
        if mask:
            pieces.append(xor_permute(join(keep, arrived), mask))
        else:
            pieces = [keep, arrived] + pieces
    return loss[0], finish(pieces, whitener)


def solution(mesh):
    return jax.shard_map(
        shards,
        mesh=mesh,
        in_specs=(P(("sp", "win"), None), P(), P("sp", None), P(("sp", "win"), None)),
        out_specs=(P(("sp", "win")), P(("sp", "win"), None)),
        check_vma=False,
    )
```

```python
import functools

import jax
import jax.numpy as jnp
from jax import lax
from jax.experimental import pallas as pl
from jax.experimental.pallas import tpu as pltpu
from jax.sharding import PartitionSpec as P

PARTNERS = 4
LOGIT_SCALE = 0.125
AXES = ("sp", "win")
LANES = 128
TAIL = 16
CHUNKS = 8
F32 = jnp.float32
BF16 = jnp.bfloat16
HIGHEST = lax.Precision.HIGHEST


def dot(a, b, contract=(1, 0), precision=None):
    return lax.dot_general(
        a,
        b,
        (((contract[0],), (contract[1],)), ((), ())),
        precision=precision,
        preferred_element_type=F32,
    )


def params(mebibytes, semantics=None):
    return pltpu.CompilerParams(
        vmem_limit_bytes=mebibytes * 2**20, dimension_semantics=semantics
    )


def vmem():
    return pl.BlockSpec(memory_space=pltpu.VMEM)


def smem():
    return pl.BlockSpec(memory_space=pltpu.SMEM)


def xor_permute(piece, mask):
    devices = lax.axis_size(AXES)
    return lax.ppermute(piece, AXES, [(i, i ^ mask) for i in range(devices)])


def split(value):
    high = value.astype(BF16)
    return high, (value - high.astype(F32)).astype(BF16)


def cut_kernel(ids_ref, features_hbm, *refs):
    outs, sems = refs[:-1], refs[-1]
    columns = outs[0].shape[1]
    copies = []
    for k, out in enumerate(outs):
        start = pl.multiple_of((ids_ref[0] ^ k) * columns, columns)
        copies.append(
            pltpu.make_async_copy(features_hbm.at[:, pl.ds(start, columns)], out, sems.at[k])
        )
        copies[k].start()
    for copy in copies:
        copy.wait()


def cut(ids, features, groups):
    rows, depth = features.shape
    return pl.pallas_call(
        cut_kernel,
        in_specs=[smem(), pl.BlockSpec(memory_space=pltpu.HBM)],
        out_specs=[vmem()] * groups,
        out_shape=[jax.ShapeDtypeStruct((rows, depth // groups), BF16)] * groups,
        scratch_shapes=[pltpu.SemaphoreType.DMA((groups,))],
        compiler_params=params(8),
        name="cut",
    )(ids, features)


def pack_sums(sums, packed, rows):
    high = sums.astype(BF16).astype(F32)
    pad = jnp.zeros((sums.shape[0], 2 * packed - sums.shape[1]), F32)
    lines = []
    for half in (high, sums - high):
        lines += [half[:, :packed], jnp.concatenate([half[:, packed:], pad], axis=1)]
    if rows > 4 * sums.shape[0]:
        lines.append(jnp.zeros((rows - 4 * sums.shape[0], packed), F32))
    return jnp.concatenate(lines, axis=0).astype(BF16)


def unpack_sums(block, count, embed):
    wide = block.astype(F32)
    packed = wide.shape[1]
    low = 2 * count
    left = wide[0:count] + wide[low : low + count]
    right = wide[count:low] + wide[low + count : low + 2 * count]
    return jnp.concatenate([left, right[:, : embed - packed]], axis=1)


def project_kernel(
    ids_ref,
    offsets_ref,
    features_hbm,
    weight_hbm,
    ortholog_hbm,
    block_ref,
    send_ref,
    keep_ref,
    features_ref,
    weight_ref,
    ortholog_ref,
    means,
    wide,
    sems,
):
    rows = features_ref.shape[0]
    depth, embed = weight_ref.shape
    half, packed = keep_ref.shape
    blocks = embed // LANES
    tile = depth // CHUNKS

    copies = []
    for n in range(CHUNKS):
        at = pl.ds(n * tile, tile)
        copies.append(
            (
                pltpu.make_async_copy(features_hbm.at[:, at], features_ref.at[:, at], sems.at[0, n]),
                pltpu.make_async_copy(weight_hbm.at[at, :], weight_ref.at[at, :], sems.at[1, n]),
            )
        )
        for copy in copies[-1]:
            copy.start()
    table_copy = pltpu.make_async_copy(ortholog_hbm, ortholog_ref, sems.at[0, CHUNKS])
    table_copy.start()

    total = jnp.zeros((rows, embed), F32)
    for n in range(CHUNKS):
        for copy in copies[n]:
            copy.wait()
        at = slice(n * tile, (n + 1) * tile)
        total = total + dot(features_ref[:, at], weight_ref[at, :])
    projected = total.astype(BF16)
    block_ref[0:rows, :] = projected

    table_copy.wait()
    line = lax.broadcasted_iota(jnp.int32, (TAIL, embed), 0)
    lane = lax.broadcasted_iota(jnp.int32, (TAIL, embed), 1)
    table = jnp.zeros((TAIL, embed), F32)
    for k in range(PARTNERS):
        table = jnp.where((line == 1) & (lane == k), offsets_ref[0, k].astype(F32), table)
    hits = jnp.concatenate(
        [ortholog_ref[k : k + 1, :].astype(F32) for k in range(PARTNERS)]
        + ([jnp.zeros((1, embed - PARTNERS * rows), F32)] if embed > PARTNERS * rows else []),
        axis=1,
    )
    block_ref[rows:, :] = jnp.where(line == 0, hits, table).astype(BF16)

    sums = jnp.sum(projected.astype(F32), axis=0, keepdims=True)
    send_ref[half:, :] = pack_sums(sums, packed, TAIL)
    wide[:, :embed] = projected
    wide[:, embed:] = projected[:, : packed - LANES]
    ones = jnp.ones((rows, LANES), BF16)
    means[...] = jnp.broadcast_to(sums * (1.0 / rows), means.shape)
    core = ids_ref[2] & 1
    for side, out in ((1, send_ref), (0, keep_ref)):
        for r in range(blocks // 2):
            block = (core ^ side) * (blocks // 2) + r
            start = pl.multiple_of(block * LANES, LANES)
            own = wide[:, pl.ds(start, LANES)]
            gram = dot(own, wide[:, pl.ds(start, packed)], (0, 0))
            sums = dot(own, ones, (0, 0))
            for k in range(packed // LANES):
                other = pl.multiple_of((block + k) % blocks * LANES, LANES)
                at = slice(k * LANES, (k + 1) * LANES)
                value = gram[:, at] - sums * means[0:1, pl.ds(other, LANES)]
                out[r * LANES : (r + 1) * LANES, at] = value.astype(out.dtype)


def project(ids, offsets, features, weight, ortholog):
    rows, depth = features.shape
    embed = weight.shape[1]
    packed = embed // 2 + LANES
    hbm = pl.BlockSpec(memory_space=pltpu.HBM)
    return pl.pallas_call(
        project_kernel,
        in_specs=[smem(), smem(), hbm, hbm, hbm],
        out_specs=[vmem()] * 3,
        out_shape=[
            jax.ShapeDtypeStruct((rows + TAIL, embed), BF16),
            jax.ShapeDtypeStruct((embed // 2 + TAIL, packed), BF16),
            jax.ShapeDtypeStruct((embed // 2, packed), F32),
        ],
        scratch_shapes=[
            pltpu.VMEM((rows, depth), BF16),
            pltpu.VMEM((depth, embed), BF16),
            pltpu.VMEM((PARTNERS, rows), jnp.int32),
            pltpu.VMEM((8, embed), F32),
            pltpu.VMEM((rows, embed + packed - LANES), BF16),
            pltpu.SemaphoreType.DMA((2, CHUNKS + 1)),
        ],
        compiler_params=params(51),
        cost_estimate=pl.CostEstimate(
            flops=2 * rows * depth * embed, bytes_accessed=2 * depth * embed, transcendentals=0
        ),
        name="project",
    )(ids, offsets, features, weight, ortholog)


def make_stage_kernel(seen, arrivals, low, count, embed):
    def kernel(ids_ref, keep_ref, sent_ref, *refs):
        arrived, next_keep, outs = refs[:arrivals], refs[arrivals], refs[arrivals + 1 :]
        full, packed = keep_ref.shape
        share = full // count
        own = (ids_ref[2] >> low) & (count - 1)
        sums = [unpack_sums(ref[full:, :], seen, embed) for ref in (sent_ref, *arrived)]
        block = pack_sums(jnp.concatenate(sums, axis=0), packed, outs[0].shape[0] - share)
        for r in range(count):
            at = pl.ds(pl.multiple_of((own ^ r) * share, share), share)
            value = keep_ref[at, :]
            for ref in arrived:
                value = value + ref[at, :].astype(F32)
            if r == 0:
                next_keep[...] = value
            else:
                outs[r - 1][:share, :] = value.astype(BF16)
                outs[r - 1][share:, :] = block

    return kernel


def stage(ids, keep, sent, arrived, seen, low, count, embed):
    full, packed = keep.shape
    share = full // count
    held = seen * (1 + len(arrived))
    tail = -(-4 * held // TAIL) * TAIL
    out = pl.pallas_call(
        make_stage_kernel(seen, len(arrived), low, count, embed),
        in_specs=[smem()] + [vmem()] * (2 + len(arrived)),
        out_specs=[vmem()] * count,
        out_shape=[jax.ShapeDtypeStruct((share, packed), F32)]
        + [jax.ShapeDtypeStruct((share + tail, packed), BF16)] * (count - 1),
        compiler_params=params(16),
        cost_estimate=pl.CostEstimate(
            flops=full * packed, bytes_accessed=4 * full * packed, transcendentals=0
        ),
        name="stage",
    )(ids, keep, sent, *arrived)
    return out[0], out[1:], held


def make_whiten_kernel(rows, count, stages):
    def kernel(
        ids_ref,
        near_ref,
        far_ref,
        *refs,
    ):
        sums_refs = refs[:-7]
        whitener_ref, mean_ref, scaled, rest, first, left, right = refs[-7:]
        me = ids_ref[2]
        place = me & 1
        for low, size in stages:
            place = place * size + ((me >> low) & (size - 1))
        embed = scaled.shape[0]
        blocks = embed // LANES
        half = blocks // 2
        pieces, depth = near_ref.shape[:2]
        per_block = LANES // depth
        totals = jnp.concatenate(
            [
                unpack_sums(ref[start : start + 4 * count, :], count, embed)
                for ref in sums_refs
                for start in range(depth, ref.shape[0], 4 * count)
            ],
            axis=0,
        )
        total_rows = rows * totals.shape[0]
        tile = 256

        mean = jnp.sum(totals, axis=0, keepdims=True) * (1.0 / total_rows)
        mean_ref[...] = mean
        shift_high, shift_low = split(totals * (1.0 / rows) - mean)
        shift_left = jnp.concatenate([shift_high, shift_high, shift_low], axis=0)
        shift_right = jnp.concatenate([shift_high, shift_low, shift_high], axis=0)

        def block_at(i, j):
            return slice(i * LANES, (i + 1) * LANES), slice(j * LANES, (j + 1) * LANES)

        def unpack(source_ref, side):
            for i in range(side * half, (side + 1) * half):
                for part in range(per_block):
                    piece = ((i - side * half) * per_block + part) ^ (place % pieces)
                    wide = source_ref[piece].astype(F32)
                    lines = pl.ds(i * LANES + part * depth, depth)
                    for k in range(half + 1):
                        if k == half and side:
                            continue
                        j = (i + k) % blocks
                        scaled[lines, j * LANES : (j + 1) * LANES] = wide[
                            :, k * LANES : (k + 1) * LANES
                        ]

        for core in range(2):

            @pl.when(place // pieces == core)
            def _():
                unpack(near_ref, core)
                unpack(far_ref, 1 - core)

        for i in range(blocks):
            for j in range(blocks):
                held = (j - i) % blocks < half or ((j - i) % blocks == half and i < half)
                if not held and i * LANES // tile <= j * LANES // tile:
                    scaled[block_at(i, j)] = scaled[block_at(j, i)].T

        panels = []
        for t in range(embed // tile):
            panels.append((slice(0, (t + 1) * tile), slice(t * tile, (t + 1) * tile)))

        def mirror(out, panel, value):
            rows_at, columns_at = panel
            value = value.astype(BF16)
            out[panel] = value
            above = columns_at.start
            if above:
                out[columns_at, 0:above] = value[0:above].T

        squares = jnp.zeros((1, tile), F32)
        for panel in panels:
            rows_at, columns_at = panel
            between = dot(shift_left[:, rows_at], shift_right[:, columns_at], (0, 0))
            covariance = (scaled[panel] + rows * between) * (1.0 / total_rows)
            scaled[panel] = covariance
            mirror(first, panel, covariance)
            above = columns_at.start
            square = covariance * covariance
            squares = squares + jnp.sum(square[above:], axis=0, keepdims=True)
            if above:
                squares = squares + 2.0 * jnp.sum(square[:above], axis=0, keepdims=True)
        frobenius = jnp.sqrt(jnp.sum(squares, axis=1, keepdims=True))
        inverse = 1.0 / frobenius
        root = lax.rsqrt(frobenius)

        def product(one, two, finish):
            for panel in panels:
                finish(panel, dot(one[panel[0], :], two[:, panel[1]]))

        def second(panel, value):
            value = value * (inverse * inverse)
            own = scaled[panel] * inverse
            scaled[panel] = own
            rest[panel] = 27.0 * value - 39.0 * own
            mirror(left, panel, value)
            mirror(right, panel, value - 9.0 * own)

        product(first, first, second)

        def fourth(panel, value):
            value = (value + rest[panel]) * (1.0 / 16.0)
            rest[panel] = value
            mirror(whitener_ref, panel, value)

        product(left, right, fourth)

        def moved(panel, value):
            value = value * inverse
            scaled[panel] = 2.25 * 2.25 * scaled[panel] + 4.5 * value
            mirror(right, panel, value)

        product(first, whitener_ref, moved)

        def quad(panel, value):
            value = value + scaled[panel]
            rest[panel] = 3.0 * rest[panel] - 2.25 * value
            mirror(left, panel, value)

        product(whitener_ref, right, quad)
        first[...] = whitener_ref[...]

        def last(panel, value):
            at = lax.broadcasted_iota(jnp.int32, value.shape, 0)
            eye = at == lax.broadcasted_iota(jnp.int32, value.shape, 1) + panel[1].start
            value = 0.5 * (rest[panel] - value)
            value = value + jnp.where(eye, 0.5 * 3.0 * 2.25, 0.0)
            mirror(whitener_ref, panel, value * root)

        product(first, left, last)

    return kernel


def whiten(ids, near, far, sums, count, stages, rows, embed):
    square = (embed, embed)
    return pl.pallas_call(
        make_whiten_kernel(rows, count, stages),
        in_specs=[smem()] + [vmem()] * (2 + len(sums)),
        out_specs=[vmem(), vmem()],
        out_shape=[
            jax.ShapeDtypeStruct(square, BF16),
            jax.ShapeDtypeStruct((1, embed), F32),
        ],
        scratch_shapes=[pltpu.VMEM(square, F32)] * 2 + [pltpu.VMEM(square, BF16)] * 3,
        compiler_params=params(24),
        cost_estimate=pl.CostEstimate(
            flops=5 * 2 * embed**3, bytes_accessed=2 * embed**2, transcendentals=0
        ),
        name="whiten",
    )(ids, near, far, *sums)


def contrast_kernel(order, ids_ref, mean_ref, whitener_ref, *refs):
    loss_ref, grad_ref, white, tables, numbers, offsets_ref, sem = refs[-11:-4]
    even, odd = (refs[-4], refs[-3]), (refs[-2], refs[-1])
    block_refs = [ref.at[i] for ref in refs[:-11] for i in range(ref.shape[0])]
    block_refs = [block_refs[order.index(k)] for k in range(len(order))]
    groups, rows, embed = white.shape
    group = ids_ref[0]

    for k in range(0, groups, 2):
        pair = block_refs[k : k + 2]
        centered = [(ref[0:rows, :].astype(F32) - mean_ref[...]).astype(BF16) for ref in pair]
        value = dot(jnp.concatenate(centered, axis=0), whitener_ref[...]).astype(BF16)
        for side, ref in enumerate(pair):
            white[group ^ (k + side)] = value[side * rows : (side + 1) * rows]
            table = ref[rows:, :].astype(F32)[0:8]
            tables[group ^ (k + side)] = table
            numbers[group ^ (k + side)] = table[:, 0:LANES].astype(jnp.int32)
    copy = pltpu.make_async_copy(numbers, offsets_ref, sem)
    copy.start()
    copy.wait()

    places = lax.broadcasted_iota(jnp.int32, (rows, rows), 0).astype(F32)
    log2e = 1.4426950408889634

    def partner(g, k):
        return white[(g + offsets_ref[g, 1, k]) % groups]

    def scores(g, buffers):
        own = white[g]
        for k in range(PARTNERS):
            buffers[0][k * rows : (k + 1) * rows, :] = dot(partner(g, k), own, (1, 1))

    def softmax(g, buffers):
        loss = jnp.zeros((1, rows), F32)
        for k in range(PARTNERS):
            at = slice(k * rows, (k + 1) * rows)
            own = buffers[0][at, :]
            peak = jnp.max(own, axis=0, keepdims=True)
            powers = jnp.exp2((own - peak) * (LOGIT_SCALE * log2e))
            sums = jnp.sum(powers, axis=0, keepdims=True)
            hit = places == tables[g, 0:1, at]
            picked = jnp.sum(jnp.where(hit, own, 0.0), axis=0, keepdims=True)
            loss = loss + ((peak - picked) * LOGIT_SCALE + jnp.log(sums))
            share = powers * (1.0 / (PARTNERS * sums))
            weights = share - jnp.where(hit, 1.0 / PARTNERS, 0.0)
            buffers[1][at, :] = weights.astype(BF16)
        return loss * (1.0 / PARTNERS)

    def gradient(g, buffers):
        grad = dot(buffers[1][0:rows, :], partner(g, 0), (0, 0))
        for k in range(1, PARTNERS):
            grad = grad + dot(buffers[1][k * rows : (k + 1) * rows, :], partner(g, k), (0, 0))
        grad_ref[g] = (grad * LOGIT_SCALE).astype(BF16)

    scores(0, even)

    @pl.loop(0, groups // 2)
    def _(pair):
        g = 2 * pair
        scores(g + 1, odd)
        first = softmax(g, even)
        gradient(g, even)
        second = softmax(g + 1, odd)
        scores(lax.rem(g + 2, groups), even)
        gradient(g + 1, odd)

        @pl.when(pair == group // 2)
        def _():
            loss_ref[...] = jnp.where(group % 2 == 0, first, second)


def contrast(ids, blocks, order, mean, whitener):
    groups = len(order)
    rows, embed = blocks[0].shape[1:]
    rows -= TAIL
    return pl.pallas_call(
        functools.partial(contrast_kernel, order),
        in_specs=[smem()] + [vmem()] * (2 + len(blocks)),
        out_specs=[vmem()] * 2,
        out_shape=[
            jax.ShapeDtypeStruct((1, rows), F32),
            jax.ShapeDtypeStruct((groups, rows, embed), BF16),
        ],
        scratch_shapes=[
            pltpu.VMEM((groups, rows, embed), BF16),
            pltpu.VMEM((groups, 8, embed), F32),
            pltpu.VMEM((groups, 8, LANES), jnp.int32),
            pltpu.SMEM((groups, 8, LANES), jnp.int32),
            pltpu.SemaphoreType.DMA,
        ]
        + [pltpu.VMEM((PARTNERS * rows, rows), F32), pltpu.VMEM((PARTNERS * rows, rows), BF16)] * 2,
        compiler_params=params(min(58, 12 + 6 * groups * rows * embed // 2**20)),
        cost_estimate=pl.CostEstimate(
            flops=groups * rows * 2 * embed * (embed + 2 * PARTNERS * rows),
            bytes_accessed=4 * groups * rows * embed,
            transcendentals=groups * PARTNERS * rows * rows,
        ),
        name="contrast",
    )(ids, mean, whitener, *blocks)


def pieces_kernel(share, masks, order, ids_ref, grad_ref, *refs):
    groups = grad_ref.shape[0]
    features, (keep_ref, send_ref, total) = refs[:groups], refs[groups:]

    def columns(at):
        value = None
        for k, feature_ref in zip(order, features):
            term = dot(feature_ref[:, at], grad_ref[ids_ref[0] ^ k], (0, 0))
            value = term if value is None else value + term
        return value

    if share % LANES:
        total[...] = columns(slice(None))
    for n, mask in enumerate(masks):
        at = pl.ds(pl.multiple_of((ids_ref[1] ^ mask) * share, share), share)
        value = total[at, :] if share % LANES else columns(at)
        out, n = (send_ref, n - len(masks) // 2) if n >= len(masks) // 2 else (keep_ref, n)
        out[n * share : (n + 1) * share, :] = value.astype(out.dtype)


def weight_pieces(ids, grad, slices, order, shares, masks):
    groups, rows, embed = grad.shape
    columns = slices[0].shape[1]
    share = columns // shares
    half = len(masks) // 2 * share
    return pl.pallas_call(
        functools.partial(pieces_kernel, share, masks, order),
        in_specs=[smem()] + [vmem()] * (1 + len(slices)),
        out_specs=[vmem()] * 2,
        out_shape=[
            jax.ShapeDtypeStruct((half, embed), F32),
            jax.ShapeDtypeStruct((half, embed), BF16),
        ],
        scratch_shapes=[pltpu.VMEM((columns if share % LANES else 8, embed), F32)],
        compiler_params=params(24),
        cost_estimate=pl.CostEstimate(
            flops=groups * rows * 2 * embed * share * len(masks),
            bytes_accessed=2 * groups * rows * (embed + columns),
            transcendentals=0,
        ),
        name="weight_pieces",
    )(ids, grad, *slices)


def join_kernel(keep_ref, arrived_ref, out_ref):
    out_ref[...] = (keep_ref[...] + arrived_ref[...].astype(F32)).astype(BF16)


def join(keep, arrived):
    return pl.pallas_call(
        join_kernel,
        in_specs=[vmem()] * 2,
        out_specs=vmem(),
        out_shape=jax.ShapeDtypeStruct(keep.shape, BF16),
        compiler_params=params(8),
        name="join",
    )(keep, arrived)


def finish_kernel(*refs):
    keep_ref, whitener_ref, out_ref = refs[0], refs[-2], refs[-1]
    value = keep_ref[...]
    for ref in refs[1:-2]:
        value = value + ref[...].astype(F32)
    high, low = split(value)
    both = dot(jnp.concatenate([high, low], axis=0), whitener_ref[...], (1, 1))
    out_ref[...] = both[: value.shape[0]] + both[value.shape[0] :]


def finish(pieces, whitener):
    return pl.pallas_call(
        finish_kernel,
        in_specs=[vmem()] * (len(pieces) + 1),
        out_specs=vmem(),
        out_shape=jax.ShapeDtypeStruct(pieces[0].shape, F32),
        compiler_params=params(12),
        name="finish",
    )(*pieces, whitener)


def shards(features, proj_weight, partner_offsets, ortholog_index):
    rows, depth = features.shape
    embed = proj_weight.shape[1]
    groups = lax.axis_size("sp")
    shares = lax.axis_size("win")
    devices = groups * shares
    group = lax.axis_index("sp").astype(jnp.int32)
    window = lax.axis_index("win").astype(jnp.int32)
    me = group * shares + window
    ids = jnp.stack([group, window, me])

    direct = groups == 8
    by_x, by_near, by_far = shares, 2 * shares, 4 * shares
    if not direct:
        slices = features.reshape(rows, groups, depth // groups).transpose(1, 0, 2)
        slices = lax.all_to_all(slices, "sp", 0, 0)
        slices = [
            lax.dynamic_index_in_dim(slices, group ^ k, 0, keepdims=False) for k in range(groups)
        ]

    block, send, keep = project(
        ids, partner_offsets, features, proj_weight, ortholog_index.T
    )
    block = block[None]
    if direct:
        block_x = xor_permute(block, by_x)
        block_far = xor_permute(block, by_far)
        block_near = xor_permute(block, by_near)
    else:
        gathered = lax.all_gather(block, "sp", tiled=True)

    arrived = [xor_permute(send, 1)]
    if direct:
        arrived[0], block_x = lax.optimization_barrier((arrived[0], block_x))
    sent = send
    seen = 1
    stages = []
    low = 1
    while keep.shape[0] > 32:
        count = 4
        keep, sends, seen = stage(ids, keep, sent, arrived, seen, low, count, embed)
        if direct and stages:
            *sends, block_near, block_far = lax.optimization_barrier(
                (*sends, block_near, block_far)
            )
            pair_x = xor_permute(jnp.concatenate([block_far, block_near]), by_x)
        arrived = [xor_permute(piece, (r + 1) << low) for r, piece in enumerate(sends)]
        sent = sends[0]
        stages.append((low, count))
        low += 2
    size = keep.shape[0]
    part = keep
    for piece in arrived:
        part = part + piece[:size].astype(F32)
    sums = [sent, *arrived]
    extra = devices >> low
    if extra > 1:
        mine = jnp.concatenate([part.astype(BF16)] + [piece[size:] for piece in sums])
        others = [xor_permute(mine, r << low) for r in range(1, extra)]
        for piece in others:
            part = part + piece[:size].astype(F32)
        sums = [mine, *others]
    part = part.astype(BF16)
    for number, (low, count) in enumerate(reversed(stages)):
        if direct and number == 1:
            part, block_far = lax.optimization_barrier((part, block_far))
            block_far_near = xor_permute(block_far, by_near)
            part, pair_x = lax.optimization_barrier((part, pair_x))
        part = jnp.concatenate(
            [part] + [xor_permute(part, r << low) for r in range(1, count)], axis=0
        )
    part = part.reshape(-1, size, part.shape[1])
    if direct:
        part, block_far_near, ids = lax.optimization_barrier((part, block_far_near, ids))
        slices = cut(ids, features, groups)
        far_near_x = xor_permute(block_far_near, by_x)
        blocks = [block, block_x, block_near, block_far, pair_x, block_far_near, far_near_x]
        order = [0, 1, 2, 4, 5, 3, 6, 7]
    else:
        order = slice_order = list(range(groups))
        blocks = [
            lax.dynamic_index_in_dim(gathered, group ^ k, 0, keepdims=True) for k in order
        ]
    other = xor_permute(part, 1)
    if direct:
        other, *slices = lax.optimization_barrier((other, *slices))
        slice_order = [0, 4, 2, 6, 5, 7, 1, 3]
        slices = [xor_permute(slices[k], k * shares) if k else slices[k] for k in slice_order]

    whitener, mean = whiten(ids, part, other, sums, seen, tuple(stages), rows, embed)
    loss, grad = contrast(ids, blocks, order, mean, whitener)
    pieces = []
    for mask in reversed(range(0, shares, 2)):
        keep, send = weight_pieces(
            ids, grad, slices, slice_order, shares, (mask, mask + 1)
        )
        arrived = xor_permute(send, 1)
        if mask:
            pieces.append(xor_permute(join(keep, arrived), mask))
        else:
            pieces = [keep, arrived] + pieces
    return loss[0], finish(pieces, whitener)


def solution(mesh):
    return jax.shard_map(
        shards,
        mesh=mesh,
        in_specs=(P(("sp", "win"), None), P(), P("sp", None), P(("sp", "win"), None)),
        out_specs=(P(("sp", "win")), P(("sp", "win"), None)),
        check_vma=False,
    )
```

```python
import functools

import jax
import jax.numpy as jnp
from jax import lax
from jax.experimental import pallas as pl
from jax.experimental.pallas import tpu as pltpu
from jax.sharding import PartitionSpec as P

PARTNERS = 4
LOGIT_SCALE = 0.125
AXES = ("sp", "win")
LANES = 128
TAIL = 16
CHUNKS = 8
F32 = jnp.float32
BF16 = jnp.bfloat16
HIGHEST = lax.Precision.HIGHEST


def dot(a, b, contract=(1, 0), precision=None):
    return lax.dot_general(
        a,
        b,
        (((contract[0],), (contract[1],)), ((), ())),
        precision=precision,
        preferred_element_type=F32,
    )


def params(mebibytes, semantics=None):
    return pltpu.CompilerParams(
        vmem_limit_bytes=mebibytes * 2**20, dimension_semantics=semantics
    )


def vmem():
    return pl.BlockSpec(memory_space=pltpu.VMEM)


def smem():
    return pl.BlockSpec(memory_space=pltpu.SMEM)


def xor_permute(piece, mask):
    devices = lax.axis_size(AXES)
    return lax.ppermute(piece, AXES, [(i, i ^ mask) for i in range(devices)])


def split(value):
    high = value.astype(BF16)
    return high, (value - high.astype(F32)).astype(BF16)


def cut_kernel(ids_ref, features_hbm, *refs):
    outs, sems = refs[:-1], refs[-1]
    columns = outs[0].shape[1]
    copies = []
    for k, out in enumerate(outs):
        start = pl.multiple_of((ids_ref[0] ^ k) * columns, columns)
        copies.append(
            pltpu.make_async_copy(features_hbm.at[:, pl.ds(start, columns)], out, sems.at[k])
        )
        copies[k].start()
    for copy in copies:
        copy.wait()


def cut(ids, features, groups):
    rows, depth = features.shape
    return pl.pallas_call(
        cut_kernel,
        in_specs=[smem(), pl.BlockSpec(memory_space=pltpu.HBM)],
        out_specs=[vmem()] * groups,
        out_shape=[jax.ShapeDtypeStruct((rows, depth // groups), BF16)] * groups,
        scratch_shapes=[pltpu.SemaphoreType.DMA((groups,))],
        compiler_params=params(8),
        name="cut",
    )(ids, features)


def pack_sums(sums, packed, rows):
    high = sums.astype(BF16).astype(F32)
    pad = jnp.zeros((sums.shape[0], 2 * packed - sums.shape[1]), F32)
    lines = []
    for half in (high, sums - high):
        lines += [half[:, :packed], jnp.concatenate([half[:, packed:], pad], axis=1)]
    if rows > 4 * sums.shape[0]:
        lines.append(jnp.zeros((rows - 4 * sums.shape[0], packed), F32))
    return jnp.concatenate(lines, axis=0).astype(BF16)


def unpack_sums(block, count, embed):
    wide = block.astype(F32)
    packed = wide.shape[1]
    low = 2 * count
    left = wide[0:count] + wide[low : low + count]
    right = wide[count:low] + wide[low + count : low + 2 * count]
    return jnp.concatenate([left, right[:, : embed - packed]], axis=1)


def project_kernel(
    ids_ref,
    offsets_ref,
    features_hbm,
    weight_hbm,
    ortholog_hbm,
    block_ref,
    send_ref,
    keep_ref,
    features_ref,
    weight_ref,
    ortholog_ref,
    means,
    wide,
    sems,
):
    rows = features_ref.shape[0]
    depth, embed = weight_ref.shape
    half, packed = keep_ref.shape
    blocks = embed // LANES
    tile = depth // CHUNKS

    copies = []
    for n in range(CHUNKS):
        at = pl.ds(n * tile, tile)
        copies.append(
            (
                pltpu.make_async_copy(features_hbm.at[:, at], features_ref.at[:, at], sems.at[0, n]),
                pltpu.make_async_copy(weight_hbm.at[at, :], weight_ref.at[at, :], sems.at[1, n]),
            )
        )
        for copy in copies[-1]:
            copy.start()
    table_copy = pltpu.make_async_copy(ortholog_hbm, ortholog_ref, sems.at[0, CHUNKS])
    table_copy.start()

    total = jnp.zeros((rows, embed), F32)
    for n in range(CHUNKS):
        for copy in copies[n]:
            copy.wait()
        at = slice(n * tile, (n + 1) * tile)
        total = total + dot(features_ref[:, at], weight_ref[at, :])
    projected = total.astype(BF16)
    block_ref[0:rows, :] = projected

    table_copy.wait()
    line = lax.broadcasted_iota(jnp.int32, (TAIL, embed), 0)
    lane = lax.broadcasted_iota(jnp.int32, (TAIL, embed), 1)
    table = jnp.zeros((TAIL, embed), F32)
    for k in range(PARTNERS):
        table = jnp.where((line == 1) & (lane == k), offsets_ref[0, k].astype(F32), table)
    hits = jnp.concatenate(
        [ortholog_ref[k : k + 1, :].astype(F32) for k in range(PARTNERS)]
        + ([jnp.zeros((1, embed - PARTNERS * rows), F32)] if embed > PARTNERS * rows else []),
        axis=1,
    )
    block_ref[rows:, :] = jnp.where(line == 0, hits, table).astype(BF16)

    sums = jnp.sum(projected.astype(F32), axis=0, keepdims=True)
    send_ref[half:, :] = pack_sums(sums, packed, TAIL)
    wide[:, :embed] = projected
    wide[:, embed:] = projected[:, : packed - LANES]
    ones = jnp.ones((rows, LANES), BF16)
    means[...] = jnp.broadcast_to(sums * (1.0 / rows), means.shape)
    core = ids_ref[2] & 1
    for side, out in ((1, send_ref), (0, keep_ref)):
        for r in range(blocks // 2):
            block = (core ^ side) * (blocks // 2) + r
            start = pl.multiple_of(block * LANES, LANES)
            own = wide[:, pl.ds(start, LANES)]
            gram = dot(own, wide[:, pl.ds(start, packed)], (0, 0))
            sums = dot(own, ones, (0, 0))
            for k in range(packed // LANES):
                other = pl.multiple_of((block + k) % blocks * LANES, LANES)
                at = slice(k * LANES, (k + 1) * LANES)
                value = gram[:, at] - sums * means[0:1, pl.ds(other, LANES)]
                out[r * LANES : (r + 1) * LANES, at] = value.astype(out.dtype)


def project(ids, offsets, features, weight, ortholog):
    rows, depth = features.shape
    embed = weight.shape[1]
    packed = embed // 2 + LANES
    hbm = pl.BlockSpec(memory_space=pltpu.HBM)
    return pl.pallas_call(
        project_kernel,
        in_specs=[smem(), smem(), hbm, hbm, hbm],
        out_specs=[vmem()] * 3,
        out_shape=[
            jax.ShapeDtypeStruct((rows + TAIL, embed), BF16),
            jax.ShapeDtypeStruct((embed // 2 + TAIL, packed), BF16),
            jax.ShapeDtypeStruct((embed // 2, packed), F32),
        ],
        scratch_shapes=[
            pltpu.VMEM((rows, depth), BF16),
            pltpu.VMEM((depth, embed), BF16),
            pltpu.VMEM((PARTNERS, rows), jnp.int32),
            pltpu.VMEM((8, embed), F32),
            pltpu.VMEM((rows, embed + packed - LANES), BF16),
            pltpu.SemaphoreType.DMA((2, CHUNKS + 1)),
        ],
        compiler_params=params(51),
        cost_estimate=pl.CostEstimate(
            flops=2 * rows * depth * embed, bytes_accessed=2 * depth * embed, transcendentals=0
        ),
        name="project",
    )(ids, offsets, features, weight, ortholog)


def make_stage_kernel(seen, arrivals, low, count, embed):
    def kernel(ids_ref, keep_ref, sent_ref, *refs):
        arrived, next_keep, outs = refs[:arrivals], refs[arrivals], refs[arrivals + 1 :]
        full, packed = keep_ref.shape
        share = full // count
        own = (ids_ref[2] >> low) & (count - 1)
        sums = [unpack_sums(ref[full:, :], seen, embed) for ref in (sent_ref, *arrived)]
        block = pack_sums(jnp.concatenate(sums, axis=0), packed, outs[0].shape[0] - share)
        for r in range(count):
            at = pl.ds(pl.multiple_of((own ^ r) * share, share), share)
            value = keep_ref[at, :]
            for ref in arrived:
                value = value + ref[at, :].astype(F32)
            if r == 0:
                next_keep[...] = value
            else:
                outs[r - 1][:share, :] = value.astype(BF16)
                outs[r - 1][share:, :] = block

    return kernel


def stage(ids, keep, sent, arrived, seen, low, count, embed):
    full, packed = keep.shape
    share = full // count
    held = seen * (1 + len(arrived))
    tail = -(-4 * held // TAIL) * TAIL
    out = pl.pallas_call(
        make_stage_kernel(seen, len(arrived), low, count, embed),
        in_specs=[smem()] + [vmem()] * (2 + len(arrived)),
        out_specs=[vmem()] * count,
        out_shape=[jax.ShapeDtypeStruct((share, packed), F32)]
        + [jax.ShapeDtypeStruct((share + tail, packed), BF16)] * (count - 1),
        compiler_params=params(16),
        cost_estimate=pl.CostEstimate(
            flops=full * packed, bytes_accessed=4 * full * packed, transcendentals=0
        ),
        name="stage",
    )(ids, keep, sent, *arrived)
    return out[0], out[1:], held


def make_whiten_kernel(rows, count, stages):
    def kernel(
        ids_ref,
        near_ref,
        far_ref,
        *refs,
    ):
        sums_refs = refs[:-7]
        whitener_ref, mean_ref, scaled, rest, first, left, right = refs[-7:]
        me = ids_ref[2]
        place = me & 1
        for low, size in stages:
            place = place * size + ((me >> low) & (size - 1))
        embed = scaled.shape[0]
        blocks = embed // LANES
        half = blocks // 2
        pieces, depth = near_ref.shape[:2]
        per_block = LANES // depth
        totals = jnp.concatenate(
            [
                unpack_sums(ref[start : start + 4 * count, :], count, embed)
                for ref in sums_refs
                for start in range(depth, ref.shape[0], 4 * count)
            ],
            axis=0,
        )
        total_rows = rows * totals.shape[0]
        tile = 256

        mean = jnp.sum(totals, axis=0, keepdims=True) * (1.0 / total_rows)
        mean_ref[...] = mean
        shift_high, shift_low = split(totals * (1.0 / rows) - mean)
        shift_left = jnp.concatenate([shift_high, shift_high, shift_low], axis=0)
        shift_right = jnp.concatenate([shift_high, shift_low, shift_high], axis=0)

        def block_at(i, j):
            return slice(i * LANES, (i + 1) * LANES), slice(j * LANES, (j + 1) * LANES)

        def unpack(source_ref, side):
            for i in range(side * half, (side + 1) * half):
                for part in range(per_block):
                    piece = ((i - side * half) * per_block + part) ^ (place % pieces)
                    wide = source_ref[piece].astype(F32)
                    lines = pl.ds(i * LANES + part * depth, depth)
                    for k in range(half + 1):
                        if k == half and side:
                            continue
                        j = (i + k) % blocks
                        scaled[lines, j * LANES : (j + 1) * LANES] = wide[
                            :, k * LANES : (k + 1) * LANES
                        ]

        for core in range(2):

            @pl.when(place // pieces == core)
            def _():
                unpack(near_ref, core)
                unpack(far_ref, 1 - core)

        for i in range(blocks):
            for j in range(blocks):
                held = (j - i) % blocks < half or ((j - i) % blocks == half and i < half)
                if not held and i * LANES // tile <= j * LANES // tile:
                    scaled[block_at(i, j)] = scaled[block_at(j, i)].T

        panels = []
        for t in range(embed // tile):
            panels.append((slice(0, (t + 1) * tile), slice(t * tile, (t + 1) * tile)))

        def mirror(out, panel, value):
            rows_at, columns_at = panel
            value = value.astype(BF16)
            out[panel] = value
            above = columns_at.start
            if above:
                out[columns_at, 0:above] = value[0:above].T

        squares = jnp.zeros((1, tile), F32)
        for panel in panels:
            rows_at, columns_at = panel
            between = dot(shift_left[:, rows_at], shift_right[:, columns_at], (0, 0))
            covariance = (scaled[panel] + rows * between) * (1.0 / total_rows)
            scaled[panel] = covariance
            mirror(first, panel, covariance)
            above = columns_at.start
            square = covariance * covariance
            squares = squares + jnp.sum(square[above:], axis=0, keepdims=True)
            if above:
                squares = squares + 2.0 * jnp.sum(square[:above], axis=0, keepdims=True)
        frobenius = jnp.sqrt(jnp.sum(squares, axis=1, keepdims=True))
        inverse = 1.0 / frobenius
        root = lax.rsqrt(frobenius)

        def product(one, two, finish):
            for panel in panels:
                finish(panel, dot(one[panel[0], :], two[:, panel[1]]))

        def second(panel, value):
            value = value * (inverse * inverse)
            own = scaled[panel] * inverse
            scaled[panel] = own
            rest[panel] = 27.0 * value - 39.0 * own
            mirror(left, panel, value)
            mirror(right, panel, value - 9.0 * own)

        product(first, first, second)

        def fourth(panel, value):
            value = (value + rest[panel]) * (1.0 / 16.0)
            rest[panel] = value
            mirror(whitener_ref, panel, value)

        product(left, right, fourth)

        def moved(panel, value):
            value = value * inverse
            scaled[panel] = 2.25 * 2.25 * scaled[panel] + 4.5 * value
            mirror(right, panel, value)

        product(first, whitener_ref, moved)

        def quad(panel, value):
            value = value + scaled[panel]
            rest[panel] = 3.0 * rest[panel] - 2.25 * value
            mirror(left, panel, value)

        product(whitener_ref, right, quad)
        first[...] = whitener_ref[...]

        def last(panel, value):
            at = lax.broadcasted_iota(jnp.int32, value.shape, 0)
            eye = at == lax.broadcasted_iota(jnp.int32, value.shape, 1) + panel[1].start
            value = 0.5 * (rest[panel] - value)
            value = value + jnp.where(eye, 0.5 * 3.0 * 2.25, 0.0)
            mirror(whitener_ref, panel, value * root)

        product(first, left, last)

    return kernel


def whiten(ids, near, far, sums, count, stages, rows, embed):
    square = (embed, embed)
    return pl.pallas_call(
        make_whiten_kernel(rows, count, stages),
        in_specs=[smem()] + [vmem()] * (2 + len(sums)),
        out_specs=[vmem(), vmem()],
        out_shape=[
            jax.ShapeDtypeStruct(square, BF16),
            jax.ShapeDtypeStruct((1, embed), F32),
        ],
        scratch_shapes=[pltpu.VMEM(square, F32)] * 2 + [pltpu.VMEM(square, BF16)] * 3,
        compiler_params=params(24),
        cost_estimate=pl.CostEstimate(
            flops=5 * 2 * embed**3, bytes_accessed=2 * embed**2, transcendentals=0
        ),
        name="whiten",
    )(ids, near, far, *sums)


def contrast_kernel(order, ids_ref, mean_ref, whitener_ref, *refs):
    loss_ref, grad_ref, white, tables, numbers, offsets_ref, sem = refs[-11:-4]
    even, odd = (refs[-4], refs[-3]), (refs[-2], refs[-1])
    block_refs = [ref.at[i] for ref in refs[:-11] for i in range(ref.shape[0])]
    block_refs = [block_refs[order.index(k)] for k in range(len(order))]
    groups, rows, embed = white.shape
    group = ids_ref[0]

    for k in range(0, groups, 2):
        pair = block_refs[k : k + 2]
        centered = [(ref[0:rows, :].astype(F32) - mean_ref[...]).astype(BF16) for ref in pair]
        value = dot(jnp.concatenate(centered, axis=0), whitener_ref[...]).astype(BF16)
        for side, ref in enumerate(pair):
            white[group ^ (k + side)] = value[side * rows : (side + 1) * rows]
            table = ref[rows:, :].astype(F32)[0:8]
            tables[group ^ (k + side)] = table
            numbers[group ^ (k + side)] = table[:, 0:LANES].astype(jnp.int32)
    copy = pltpu.make_async_copy(numbers, offsets_ref, sem)
    copy.start()
    copy.wait()

    places = lax.broadcasted_iota(jnp.int32, (rows, rows), 0).astype(F32)
    log2e = 1.4426950408889634

    def partner(g, k):
        return white[(g + offsets_ref[g, 1, k]) % groups]

    def scores(g, buffers):
        own = white[g]
        for k in range(PARTNERS):
            buffers[0][k * rows : (k + 1) * rows, :] = dot(partner(g, k), own, (1, 1))

    def softmax(g, buffers):
        loss = jnp.zeros((1, rows), F32)
        for k in range(PARTNERS):
            at = slice(k * rows, (k + 1) * rows)
            own = buffers[0][at, :]
            peak = jnp.max(own, axis=0, keepdims=True)
            powers = jnp.exp2((own - peak) * (LOGIT_SCALE * log2e))
            sums = jnp.sum(powers, axis=0, keepdims=True)
            hit = places == tables[g, 0:1, at]
            picked = jnp.sum(jnp.where(hit, own, 0.0), axis=0, keepdims=True)
            loss = loss + ((peak - picked) * LOGIT_SCALE + jnp.log(sums))
            share = powers * (1.0 / (PARTNERS * sums))
            weights = share - jnp.where(hit, 1.0 / PARTNERS, 0.0)
            buffers[1][at, :] = weights.astype(BF16)
        return loss * (1.0 / PARTNERS)

    def gradient(g, buffers):
        grad = dot(buffers[1][0:rows, :], partner(g, 0), (0, 0))
        for k in range(1, PARTNERS):
            grad = grad + dot(buffers[1][k * rows : (k + 1) * rows, :], partner(g, k), (0, 0))
        grad_ref[g] = (grad * LOGIT_SCALE).astype(BF16)

    scores(0, even)

    @pl.loop(0, groups // 2)
    def _(pair):
        g = 2 * pair
        scores(g + 1, odd)
        first = softmax(g, even)
        gradient(g, even)
        second = softmax(g + 1, odd)
        scores(lax.rem(g + 2, groups), even)
        gradient(g + 1, odd)

        @pl.when(pair == group // 2)
        def _():
            loss_ref[...] = jnp.where(group % 2 == 0, first, second)


def contrast(ids, blocks, order, mean, whitener):
    groups = len(order)
    rows, embed = blocks[0].shape[1:]
    rows -= TAIL
    return pl.pallas_call(
        functools.partial(contrast_kernel, order),
        in_specs=[smem()] + [vmem()] * (2 + len(blocks)),
        out_specs=[vmem()] * 2,
        out_shape=[
            jax.ShapeDtypeStruct((1, rows), F32),
            jax.ShapeDtypeStruct((groups, rows, embed), BF16),
        ],
        scratch_shapes=[
            pltpu.VMEM((groups, rows, embed), BF16),
            pltpu.VMEM((groups, 8, embed), F32),
            pltpu.VMEM((groups, 8, LANES), jnp.int32),
            pltpu.SMEM((groups, 8, LANES), jnp.int32),
            pltpu.SemaphoreType.DMA,
        ]
        + [pltpu.VMEM((PARTNERS * rows, rows), F32), pltpu.VMEM((PARTNERS * rows, rows), BF16)] * 2,
        compiler_params=params(min(58, 12 + 6 * groups * rows * embed // 2**20)),
        cost_estimate=pl.CostEstimate(
            flops=groups * rows * 2 * embed * (embed + 2 * PARTNERS * rows),
            bytes_accessed=4 * groups * rows * embed,
            transcendentals=groups * PARTNERS * rows * rows,
        ),
        name="contrast",
    )(ids, mean, whitener, *blocks)


def pieces_kernel(share, masks, order, ids_ref, grad_ref, *refs):
    groups = grad_ref.shape[0]
    features, (keep_ref, send_ref, total) = refs[:groups], refs[groups:]

    def columns(at):
        value = None
        for k, feature_ref in zip(order, features):
            term = dot(feature_ref[:, at], grad_ref[ids_ref[0] ^ k], (0, 0))
            value = term if value is None else value + term
        return value

    if share % LANES:
        total[...] = columns(slice(None))
    for n, mask in enumerate(masks):
        at = pl.ds(pl.multiple_of((ids_ref[1] ^ mask) * share, share), share)
        value = total[at, :] if share % LANES else columns(at)
        out, n = (send_ref, n - len(masks) // 2) if n >= len(masks) // 2 else (keep_ref, n)
        out[n * share : (n + 1) * share, :] = value.astype(out.dtype)


def weight_pieces(ids, grad, slices, order, shares, masks):
    groups, rows, embed = grad.shape
    columns = slices[0].shape[1]
    share = columns // shares
    half = len(masks) // 2 * share
    return pl.pallas_call(
        functools.partial(pieces_kernel, share, masks, order),
        in_specs=[smem()] + [vmem()] * (1 + len(slices)),
        out_specs=[vmem()] * 2,
        out_shape=[
            jax.ShapeDtypeStruct((half, embed), F32),
            jax.ShapeDtypeStruct((half, embed), BF16),
        ],
        scratch_shapes=[pltpu.VMEM((columns if share % LANES else 8, embed), F32)],
        compiler_params=params(24),
        cost_estimate=pl.CostEstimate(
            flops=groups * rows * 2 * embed * share * len(masks),
            bytes_accessed=2 * groups * rows * (embed + columns),
            transcendentals=0,
        ),
        name="weight_pieces",
    )(ids, grad, *slices)


def join_kernel(keep_ref, arrived_ref, out_ref):
    out_ref[...] = (keep_ref[...] + arrived_ref[...].astype(F32)).astype(BF16)


def join(keep, arrived):
    return pl.pallas_call(
        join_kernel,
        in_specs=[vmem()] * 2,
        out_specs=vmem(),
        out_shape=jax.ShapeDtypeStruct(keep.shape, BF16),
        compiler_params=params(8),
        name="join",
    )(keep, arrived)


def finish_kernel(*refs):
    keep_ref, whitener_ref, out_ref = refs[0], refs[-2], refs[-1]
    value = keep_ref[...]
    for ref in refs[1:-2]:
        value = value + ref[...].astype(F32)
    high, low = split(value)
    both = dot(jnp.concatenate([high, low], axis=0), whitener_ref[...], (1, 1))
    out_ref[...] = both[: value.shape[0]] + both[value.shape[0] :]


def finish(pieces, whitener):
    return pl.pallas_call(
        finish_kernel,
        in_specs=[vmem()] * (len(pieces) + 1),
        out_specs=vmem(),
        out_shape=jax.ShapeDtypeStruct(pieces[0].shape, F32),
        compiler_params=params(12),
        name="finish",
    )(*pieces, whitener)


def shards(features, proj_weight, partner_offsets, ortholog_index):
    rows, depth = features.shape
    embed = proj_weight.shape[1]
    groups = lax.axis_size("sp")
    shares = lax.axis_size("win")
    devices = groups * shares
    group = lax.axis_index("sp").astype(jnp.int32)
    window = lax.axis_index("win").astype(jnp.int32)
    me = group * shares + window
    ids = jnp.stack([group, window, me])

    direct = groups == 8
    by_x, by_near, by_far = shares, 2 * shares, 4 * shares
    if not direct:
        slices = features.reshape(rows, groups, depth // groups).transpose(1, 0, 2)
        slices = lax.all_to_all(slices, "sp", 0, 0)
        slices = [
            lax.dynamic_index_in_dim(slices, group ^ k, 0, keepdims=False) for k in range(groups)
        ]

    block, send, keep = project(
        ids, partner_offsets, features, proj_weight, ortholog_index.T
    )
    block = block[None]
    if direct:
        block_x = xor_permute(block, by_x)
        block_far = xor_permute(block, by_far)
        block_near = xor_permute(block, by_near)
    else:
        gathered = lax.all_gather(block, "sp", tiled=True)

    arrived = [xor_permute(send, 1)]
    if direct:
        arrived[0], block_x = lax.optimization_barrier((arrived[0], block_x))
    sent = send
    seen = 1
    stages = []
    low = 1
    while keep.shape[0] > 32:
        count = 4
        keep, sends, seen = stage(ids, keep, sent, arrived, seen, low, count, embed)
        if direct and stages:
            *sends, block_near, block_far = lax.optimization_barrier(
                (*sends, block_near, block_far)
            )
            far_x = xor_permute(block_far, by_x)
        arrived = [xor_permute(piece, (r + 1) << low) for r, piece in enumerate(sends)]
        sent = sends[0]
        stages.append((low, count))
        low += 2
    size = keep.shape[0]
    part = keep
    for piece in arrived:
        part = part + piece[:size].astype(F32)
    sums = [sent, *arrived]
    extra = devices >> low
    if extra > 1:
        mine = jnp.concatenate([part.astype(BF16)] + [piece[size:] for piece in sums])
        others = [xor_permute(mine, r << low) for r in range(1, extra)]
        for piece in others:
            part = part + piece[:size].astype(F32)
        sums = [mine, *others]
    part = part.astype(BF16)
    for number, (low, count) in enumerate(reversed(stages)):
        if direct and number == 1:
            part, block_far = lax.optimization_barrier((part, block_far))
            far_near = xor_permute(block_far, by_near)
            part, far_x = lax.optimization_barrier((part, far_x))
        part = jnp.concatenate(
            [part] + [xor_permute(part, r << low) for r in range(1, count)], axis=0
        )
    part = part.reshape(-1, size, part.shape[1])
    if direct:
        part, far_near, block_near, ids = lax.optimization_barrier(
            (part, far_near, block_near, ids)
        )
        near_x = xor_permute(block_near, by_x)
        far_near_x = xor_permute(far_near, by_x)
        slices = cut(ids, features, groups)
    else:
        order = slice_order = list(range(groups))
        blocks = [
            lax.dynamic_index_in_dim(gathered, group ^ k, 0, keepdims=True) for k in order
        ]
    other = xor_permute(part, 1)
    if direct:
        other, *slices = lax.optimization_barrier((other, *slices))
        slice_order = [0, 2, 4, 6, 5, 7, 1, 3]
        slices = [xor_permute(slices[k], k * shares) if k else slices[k] for k in slice_order]

    whitener, mean = whiten(ids, part, other, sums, seen, tuple(stages), rows, embed)
    if direct:
        mean, near_x = lax.optimization_barrier((mean, near_x))
        blocks = [block, block_x, block_near, near_x, block_far, far_x, far_near, far_near_x]
        order = list(range(groups))
    loss, grad = contrast(ids, blocks, order, mean, whitener)
    pieces = []
    for mask in reversed(range(0, shares, 2)):
        keep, send = weight_pieces(
            ids, grad, slices, slice_order, shares, (mask, mask + 1)
        )
        arrived = xor_permute(send, 1)
        if mask:
            pieces.append(xor_permute(join(keep, arrived), mask))
        else:
            pieces = [keep, arrived] + pieces
    return loss[0], finish(pieces, whitener)


def solution(mesh):
    return jax.shard_map(
        shards,
        mesh=mesh,
        in_specs=(P(("sp", "win"), None), P(), P("sp", None), P(("sp", "win"), None)),
        out_specs=(P(("sp", "win")), P(("sp", "win"), None)),
        check_vma=False,
    )
```

```python
import functools

import jax
import jax.numpy as jnp
from jax import lax
from jax.experimental import pallas as pl
from jax.experimental.pallas import tpu as pltpu
from jax.sharding import PartitionSpec as P

PARTNERS = 4
LOGIT_SCALE = 0.125
AXES = ("sp", "win")
LANES = 128
TAIL = 16
CHUNKS = 8
F32 = jnp.float32
BF16 = jnp.bfloat16
HIGHEST = lax.Precision.HIGHEST


def dot(a, b, contract=(1, 0), precision=None):
    return lax.dot_general(
        a,
        b,
        (((contract[0],), (contract[1],)), ((), ())),
        precision=precision,
        preferred_element_type=F32,
    )


def params(mebibytes, semantics=None):
    return pltpu.CompilerParams(
        vmem_limit_bytes=mebibytes * 2**20, dimension_semantics=semantics
    )


def vmem():
    return pl.BlockSpec(memory_space=pltpu.VMEM)


def smem():
    return pl.BlockSpec(memory_space=pltpu.SMEM)


def xor_permute(piece, mask):
    devices = lax.axis_size(AXES)
    return lax.ppermute(piece, AXES, [(i, i ^ mask) for i in range(devices)])


def split(value):
    high = value.astype(BF16)
    return high, (value - high.astype(F32)).astype(BF16)


def cut_kernel(ids_ref, features_hbm, *refs):
    outs, sems = refs[:-1], refs[-1]
    columns = outs[0].shape[1]
    copies = []
    for k, out in enumerate(outs):
        start = pl.multiple_of((ids_ref[0] ^ k) * columns, columns)
        copies.append(
            pltpu.make_async_copy(features_hbm.at[:, pl.ds(start, columns)], out, sems.at[k])
        )
        copies[k].start()
    for copy in copies:
        copy.wait()


def cut(ids, features, groups):
    rows, depth = features.shape
    return pl.pallas_call(
        cut_kernel,
        in_specs=[smem(), pl.BlockSpec(memory_space=pltpu.HBM)],
        out_specs=[vmem()] * groups,
        out_shape=[jax.ShapeDtypeStruct((rows, depth // groups), BF16)] * groups,
        scratch_shapes=[pltpu.SemaphoreType.DMA((groups,))],
        compiler_params=params(8),
        name="cut",
    )(ids, features)


def pack_sums(sums, packed, rows):
    high = sums.astype(BF16).astype(F32)
    pad = jnp.zeros((sums.shape[0], 2 * packed - sums.shape[1]), F32)
    lines = []
    for half in (high, sums - high):
        lines += [half[:, :packed], jnp.concatenate([half[:, packed:], pad], axis=1)]
    if rows > 4 * sums.shape[0]:
        lines.append(jnp.zeros((rows - 4 * sums.shape[0], packed), F32))
    return jnp.concatenate(lines, axis=0).astype(BF16)


def unpack_sums(block, count, embed):
    wide = block.astype(F32)
    packed = wide.shape[1]
    low = 2 * count
    left = wide[0:count] + wide[low : low + count]
    right = wide[count:low] + wide[low + count : low + 2 * count]
    return jnp.concatenate([left, right[:, : embed - packed]], axis=1)


def project_kernel(
    ids_ref,
    offsets_ref,
    features_hbm,
    weight_hbm,
    ortholog_hbm,
    block_ref,
    send_ref,
    keep_ref,
    features_ref,
    weight_ref,
    ortholog_ref,
    means,
    wide,
    sems,
):
    rows = features_ref.shape[0]
    depth, embed = weight_ref.shape
    half, packed = keep_ref.shape
    blocks = embed // LANES
    tile = depth // CHUNKS

    copies = []
    for n in range(CHUNKS):
        at = pl.ds(n * tile, tile)
        copies.append(
            (
                pltpu.make_async_copy(features_hbm.at[:, at], features_ref.at[:, at], sems.at[0, n]),
                pltpu.make_async_copy(weight_hbm.at[at, :], weight_ref.at[at, :], sems.at[1, n]),
            )
        )
        for copy in copies[-1]:
            copy.start()
    table_copy = pltpu.make_async_copy(ortholog_hbm, ortholog_ref, sems.at[0, CHUNKS])
    table_copy.start()

    total = jnp.zeros((rows, embed), F32)
    for n in range(CHUNKS):
        for copy in copies[n]:
            copy.wait()
        at = slice(n * tile, (n + 1) * tile)
        total = total + dot(features_ref[:, at], weight_ref[at, :])
    projected = total.astype(BF16)
    block_ref[0:rows, :] = projected

    table_copy.wait()
    line = lax.broadcasted_iota(jnp.int32, (TAIL, embed), 0)
    lane = lax.broadcasted_iota(jnp.int32, (TAIL, embed), 1)
    table = jnp.zeros((TAIL, embed), F32)
    for k in range(PARTNERS):
        table = jnp.where((line == 1) & (lane == k), offsets_ref[0, k].astype(F32), table)
    hits = jnp.concatenate(
        [ortholog_ref[k : k + 1, :].astype(F32) for k in range(PARTNERS)]
        + ([jnp.zeros((1, embed - PARTNERS * rows), F32)] if embed > PARTNERS * rows else []),
        axis=1,
    )
    block_ref[rows:, :] = jnp.where(line == 0, hits, table).astype(BF16)

    sums = jnp.sum(projected.astype(F32), axis=0, keepdims=True)
    send_ref[half:, :] = pack_sums(sums, packed, TAIL)
    wide[:, :embed] = projected
    wide[:, embed:] = projected[:, : packed - LANES]
    ones = jnp.ones((rows, LANES), BF16)
    means[...] = jnp.broadcast_to(sums * (1.0 / rows), means.shape)
    core = ids_ref[2] & 1
    for side, out in ((1, send_ref), (0, keep_ref)):
        for r in range(blocks // 2):
            block = (core ^ side) * (blocks // 2) + r
            start = pl.multiple_of(block * LANES, LANES)
            own = wide[:, pl.ds(start, LANES)]
            gram = dot(own, wide[:, pl.ds(start, packed)], (0, 0))
            sums = dot(own, ones, (0, 0))
            for k in range(packed // LANES):
                other = pl.multiple_of((block + k) % blocks * LANES, LANES)
                at = slice(k * LANES, (k + 1) * LANES)
                value = gram[:, at] - sums * means[0:1, pl.ds(other, LANES)]
                out[r * LANES : (r + 1) * LANES, at] = value.astype(out.dtype)


def project(ids, offsets, features, weight, ortholog):
    rows, depth = features.shape
    embed = weight.shape[1]
    packed = embed // 2 + LANES
    hbm = pl.BlockSpec(memory_space=pltpu.HBM)
    return pl.pallas_call(
        project_kernel,
        in_specs=[smem(), smem(), hbm, hbm, hbm],
        out_specs=[vmem()] * 3,
        out_shape=[
            jax.ShapeDtypeStruct((rows + TAIL, embed), BF16),
            jax.ShapeDtypeStruct((embed // 2 + TAIL, packed), BF16),
            jax.ShapeDtypeStruct((embed // 2, packed), F32),
        ],
        scratch_shapes=[
            pltpu.VMEM((rows, depth), BF16),
            pltpu.VMEM((depth, embed), BF16),
            pltpu.VMEM((PARTNERS, rows), jnp.int32),
            pltpu.VMEM((8, embed), F32),
            pltpu.VMEM((rows, embed + packed - LANES), BF16),
            pltpu.SemaphoreType.DMA((2, CHUNKS + 1)),
        ],
        compiler_params=params(51),
        cost_estimate=pl.CostEstimate(
            flops=2 * rows * depth * embed, bytes_accessed=2 * depth * embed, transcendentals=0
        ),
        name="project",
    )(ids, offsets, features, weight, ortholog)


def make_stage_kernel(seen, arrivals, low, count, embed):
    def kernel(ids_ref, keep_ref, sent_ref, *refs):
        arrived, next_keep, outs = refs[:arrivals], refs[arrivals], refs[arrivals + 1 :]
        full, packed = keep_ref.shape
        share = full // count
        own = (ids_ref[2] >> low) & (count - 1)
        sums = [unpack_sums(ref[full:, :], seen, embed) for ref in (sent_ref, *arrived)]
        block = pack_sums(jnp.concatenate(sums, axis=0), packed, outs[0].shape[0] - share)
        for r in range(count):
            at = pl.ds(pl.multiple_of((own ^ r) * share, share), share)
            value = keep_ref[at, :]
            for ref in arrived:
                value = value + ref[at, :].astype(F32)
            if r == 0:
                next_keep[...] = value
            else:
                outs[r - 1][:share, :] = value.astype(BF16)
                outs[r - 1][share:, :] = block

    return kernel


def stage(ids, keep, sent, arrived, seen, low, count, embed):
    full, packed = keep.shape
    share = full // count
    held = seen * (1 + len(arrived))
    tail = -(-4 * held // TAIL) * TAIL
    out = pl.pallas_call(
        make_stage_kernel(seen, len(arrived), low, count, embed),
        in_specs=[smem()] + [vmem()] * (2 + len(arrived)),
        out_specs=[vmem()] * count,
        out_shape=[jax.ShapeDtypeStruct((share, packed), F32)]
        + [jax.ShapeDtypeStruct((share + tail, packed), BF16)] * (count - 1),
        compiler_params=params(16),
        cost_estimate=pl.CostEstimate(
            flops=full * packed, bytes_accessed=4 * full * packed, transcendentals=0
        ),
        name="stage",
    )(ids, keep, sent, *arrived)
    return out[0], out[1:], held


def make_whiten_kernel(rows, count, stages):
    def kernel(
        ids_ref,
        near_ref,
        far_ref,
        *refs,
    ):
        sums_refs = refs[:-7]
        whitener_ref, mean_ref, scaled, rest, first, left, right = refs[-7:]
        me = ids_ref[2]
        place = me & 1
        for low, size in stages:
            place = place * size + ((me >> low) & (size - 1))
        embed = scaled.shape[0]
        blocks = embed // LANES
        half = blocks // 2
        pieces, depth = near_ref.shape[:2]
        per_block = LANES // depth
        totals = jnp.concatenate(
            [
                unpack_sums(ref[start : start + 4 * count, :], count, embed)
                for ref in sums_refs
                for start in range(depth, ref.shape[0], 4 * count)
            ],
            axis=0,
        )
        total_rows = rows * totals.shape[0]
        tile = 256

        mean = jnp.sum(totals, axis=0, keepdims=True) * (1.0 / total_rows)
        mean_ref[...] = mean
        shift_high, shift_low = split(totals * (1.0 / rows) - mean)
        shift_left = jnp.concatenate([shift_high, shift_high, shift_low], axis=0)
        shift_right = jnp.concatenate([shift_high, shift_low, shift_high], axis=0)

        def block_at(i, j):
            return slice(i * LANES, (i + 1) * LANES), slice(j * LANES, (j + 1) * LANES)

        def unpack(source_ref, side):
            for i in range(side * half, (side + 1) * half):
                for part in range(per_block):
                    piece = ((i - side * half) * per_block + part) ^ (place % pieces)
                    wide = source_ref[piece].astype(F32)
                    lines = pl.ds(i * LANES + part * depth, depth)
                    for k in range(half + 1):
                        if k == half and side:
                            continue
                        j = (i + k) % blocks
                        scaled[lines, j * LANES : (j + 1) * LANES] = wide[
                            :, k * LANES : (k + 1) * LANES
                        ]

        for core in range(2):

            @pl.when(place // pieces == core)
            def _():
                unpack(near_ref, core)
                unpack(far_ref, 1 - core)

        for i in range(blocks):
            for j in range(blocks):
                held = (j - i) % blocks < half or ((j - i) % blocks == half and i < half)
                if not held and i * LANES // tile <= j * LANES // tile:
                    scaled[block_at(i, j)] = scaled[block_at(j, i)].T

        panels = []
        for t in range(embed // tile):
            panels.append((slice(0, (t + 1) * tile), slice(t * tile, (t + 1) * tile)))

        def mirror(out, panel, value):
            rows_at, columns_at = panel
            value = value.astype(BF16)
            out[panel] = value
            above = columns_at.start
            if above:
                out[columns_at, 0:above] = value[0:above].T

        squares = jnp.zeros((1, tile), F32)
        for panel in panels:
            rows_at, columns_at = panel
            between = dot(shift_left[:, rows_at], shift_right[:, columns_at], (0, 0))
            covariance = (scaled[panel] + rows * between) * (1.0 / total_rows)
            scaled[panel] = covariance
            mirror(first, panel, covariance)
            above = columns_at.start
            square = covariance * covariance
            squares = squares + jnp.sum(square[above:], axis=0, keepdims=True)
            if above:
                squares = squares + 2.0 * jnp.sum(square[:above], axis=0, keepdims=True)
        frobenius = jnp.sqrt(jnp.sum(squares, axis=1, keepdims=True))
        inverse = 1.0 / frobenius
        root = lax.rsqrt(frobenius)

        def product(one, two, finish):
            for panel in panels:
                finish(panel, dot(one[panel[0], :], two[:, panel[1]]))

        def second(panel, value):
            value = value * (inverse * inverse)
            own = scaled[panel] * inverse
            scaled[panel] = own
            rest[panel] = 27.0 * value - 39.0 * own
            mirror(left, panel, value)
            mirror(right, panel, value - 9.0 * own)

        product(first, first, second)

        def fourth(panel, value):
            value = (value + rest[panel]) * (1.0 / 16.0)
            rest[panel] = value
            mirror(whitener_ref, panel, value)

        product(left, right, fourth)

        def moved(panel, value):
            value = value * inverse
            scaled[panel] = 2.25 * 2.25 * scaled[panel] + 4.5 * value
            mirror(right, panel, value)

        product(first, whitener_ref, moved)

        def quad(panel, value):
            value = value + scaled[panel]
            rest[panel] = 3.0 * rest[panel] - 2.25 * value
            mirror(left, panel, value)

        product(whitener_ref, right, quad)
        first[...] = whitener_ref[...]

        def last(panel, value):
            at = lax.broadcasted_iota(jnp.int32, value.shape, 0)
            eye = at == lax.broadcasted_iota(jnp.int32, value.shape, 1) + panel[1].start
            value = 0.5 * (rest[panel] - value)
            value = value + jnp.where(eye, 0.5 * 3.0 * 2.25, 0.0)
            mirror(whitener_ref, panel, value * root)

        product(first, left, last)

    return kernel


def whiten(ids, near, far, sums, count, stages, rows, embed):
    square = (embed, embed)
    return pl.pallas_call(
        make_whiten_kernel(rows, count, stages),
        in_specs=[smem()] + [vmem()] * (2 + len(sums)),
        out_specs=[vmem(), vmem()],
        out_shape=[
            jax.ShapeDtypeStruct(square, BF16),
            jax.ShapeDtypeStruct((1, embed), F32),
        ],
        scratch_shapes=[pltpu.VMEM(square, F32)] * 2 + [pltpu.VMEM(square, BF16)] * 3,
        compiler_params=params(24),
        cost_estimate=pl.CostEstimate(
            flops=5 * 2 * embed**3, bytes_accessed=2 * embed**2, transcendentals=0
        ),
        name="whiten",
    )(ids, near, far, *sums)


def contrast_kernel(order, ids_ref, mean_ref, whitener_ref, *refs):
    loss_ref, grad_ref, white, tables, numbers, offsets_ref, sem = refs[-11:-4]
    even, odd = (refs[-4], refs[-3]), (refs[-2], refs[-1])
    block_refs = [ref.at[i] for ref in refs[:-11] for i in range(ref.shape[0])]
    block_refs = [block_refs[order.index(k)] for k in range(len(order))]
    groups, rows, embed = white.shape
    group = ids_ref[0]

    for k in range(0, groups, 2):
        pair = block_refs[k : k + 2]
        centered = [(ref[0:rows, :].astype(F32) - mean_ref[...]).astype(BF16) for ref in pair]
        value = dot(jnp.concatenate(centered, axis=0), whitener_ref[...]).astype(BF16)
        for side, ref in enumerate(pair):
            white[group ^ (k + side)] = value[side * rows : (side + 1) * rows]
            table = ref[rows:, :].astype(F32)[0:8]
            tables[group ^ (k + side)] = table
            numbers[group ^ (k + side)] = table[:, 0:LANES].astype(jnp.int32)
    copy = pltpu.make_async_copy(numbers, offsets_ref, sem)
    copy.start()
    copy.wait()

    places = lax.broadcasted_iota(jnp.int32, (rows, rows), 0).astype(F32)
    log2e = 1.4426950408889634

    def partner(g, k):
        return white[(g + offsets_ref[g, 1, k]) % groups]

    def scores(g, buffers):
        own = white[g]
        for k in range(PARTNERS):
            buffers[0][k * rows : (k + 1) * rows, :] = dot(partner(g, k), own, (1, 1))

    def softmax(g, buffers):
        loss = jnp.zeros((1, rows), F32)
        for k in range(PARTNERS):
            at = slice(k * rows, (k + 1) * rows)
            own = buffers[0][at, :]
            peak = jnp.max(own, axis=0, keepdims=True)
            powers = jnp.exp2((own - peak) * (LOGIT_SCALE * log2e))
            sums = jnp.sum(powers, axis=0, keepdims=True)
            hit = places == tables[g, 0:1, at]
            picked = jnp.sum(jnp.where(hit, own, 0.0), axis=0, keepdims=True)
            loss = loss + ((peak - picked) * LOGIT_SCALE + jnp.log(sums))
            share = powers * (1.0 / (PARTNERS * sums))
            weights = share - jnp.where(hit, 1.0 / PARTNERS, 0.0)
            buffers[1][at, :] = weights.astype(BF16)
        return loss * (1.0 / PARTNERS)

    def gradient(g, buffers):
        grad = dot(buffers[1][0:rows, :], partner(g, 0), (0, 0))
        for k in range(1, PARTNERS):
            grad = grad + dot(buffers[1][k * rows : (k + 1) * rows, :], partner(g, k), (0, 0))
        grad_ref[g] = (grad * LOGIT_SCALE).astype(BF16)

    scores(0, even)

    @pl.loop(0, groups // 2)
    def _(pair):
        g = 2 * pair
        scores(g + 1, odd)
        first = softmax(g, even)
        gradient(g, even)
        second = softmax(g + 1, odd)
        scores(lax.rem(g + 2, groups), even)
        gradient(g + 1, odd)

        @pl.when(pair == group // 2)
        def _():
            loss_ref[...] = jnp.where(group % 2 == 0, first, second)


def contrast(ids, blocks, order, mean, whitener):
    groups = len(order)
    rows, embed = blocks[0].shape[1:]
    rows -= TAIL
    return pl.pallas_call(
        functools.partial(contrast_kernel, order),
        in_specs=[smem()] + [vmem()] * (2 + len(blocks)),
        out_specs=[vmem()] * 2,
        out_shape=[
            jax.ShapeDtypeStruct((1, rows), F32),
            jax.ShapeDtypeStruct((groups, rows, embed), BF16),
        ],
        scratch_shapes=[
            pltpu.VMEM((groups, rows, embed), BF16),
            pltpu.VMEM((groups, 8, embed), F32),
            pltpu.VMEM((groups, 8, LANES), jnp.int32),
            pltpu.SMEM((groups, 8, LANES), jnp.int32),
            pltpu.SemaphoreType.DMA,
        ]
        + [pltpu.VMEM((PARTNERS * rows, rows), F32), pltpu.VMEM((PARTNERS * rows, rows), BF16)] * 2,
        compiler_params=params(min(58, 12 + 6 * groups * rows * embed // 2**20)),
        cost_estimate=pl.CostEstimate(
            flops=groups * rows * 2 * embed * (embed + 2 * PARTNERS * rows),
            bytes_accessed=4 * groups * rows * embed,
            transcendentals=groups * PARTNERS * rows * rows,
        ),
        name="contrast",
    )(ids, mean, whitener, *blocks)


def pieces_kernel(share, masks, order, ids_ref, grad_ref, *refs):
    groups = grad_ref.shape[0]
    features, (keep_ref, send_ref, total) = refs[:groups], refs[groups:]

    def columns(at):
        value = None
        for k, feature_ref in zip(order, features):
            term = dot(feature_ref[:, at], grad_ref[ids_ref[0] ^ k], (0, 0))
            value = term if value is None else value + term
        return value

    if share % LANES:
        total[...] = columns(slice(None))
    for n, mask in enumerate(masks):
        at = pl.ds(pl.multiple_of((ids_ref[1] ^ mask) * share, share), share)
        value = total[at, :] if share % LANES else columns(at)
        out, n = (send_ref, n - len(masks) // 2) if n >= len(masks) // 2 else (keep_ref, n)
        out[n * share : (n + 1) * share, :] = value.astype(out.dtype)


def weight_pieces(ids, grad, slices, order, shares, masks):
    groups, rows, embed = grad.shape
    columns = slices[0].shape[1]
    share = columns // shares
    half = len(masks) // 2 * share
    return pl.pallas_call(
        functools.partial(pieces_kernel, share, masks, order),
        in_specs=[smem()] + [vmem()] * (1 + len(slices)),
        out_specs=[vmem()] * 2,
        out_shape=[
            jax.ShapeDtypeStruct((half, embed), F32),
            jax.ShapeDtypeStruct((half, embed), BF16),
        ],
        scratch_shapes=[pltpu.VMEM((columns if share % LANES else 8, embed), F32)],
        compiler_params=params(24),
        cost_estimate=pl.CostEstimate(
            flops=groups * rows * 2 * embed * share * len(masks),
            bytes_accessed=2 * groups * rows * (embed + columns),
            transcendentals=0,
        ),
        name="weight_pieces",
    )(ids, grad, *slices)


def join_kernel(keep_ref, arrived_ref, out_ref):
    out_ref[...] = (keep_ref[...] + arrived_ref[...].astype(F32)).astype(BF16)


def join(keep, arrived):
    return pl.pallas_call(
        join_kernel,
        in_specs=[vmem()] * 2,
        out_specs=vmem(),
        out_shape=jax.ShapeDtypeStruct(keep.shape, BF16),
        compiler_params=params(8),
        name="join",
    )(keep, arrived)


def finish_kernel(*refs):
    keep_ref, whitener_ref, out_ref = refs[0], refs[-2], refs[-1]
    value = keep_ref[...]
    for ref in refs[1:-2]:
        value = value + ref[...].astype(F32)
    high, low = split(value)
    both = dot(jnp.concatenate([high, low], axis=0), whitener_ref[...], (1, 1))
    out_ref[...] = both[: value.shape[0]] + both[value.shape[0] :]


def finish(pieces, whitener):
    return pl.pallas_call(
        finish_kernel,
        in_specs=[vmem()] * (len(pieces) + 1),
        out_specs=vmem(),
        out_shape=jax.ShapeDtypeStruct(pieces[0].shape, F32),
        compiler_params=params(12),
        name="finish",
    )(*pieces, whitener)


def shards(features, proj_weight, partner_offsets, ortholog_index):
    rows, depth = features.shape
    embed = proj_weight.shape[1]
    groups = lax.axis_size("sp")
    shares = lax.axis_size("win")
    devices = groups * shares
    group = lax.axis_index("sp").astype(jnp.int32)
    window = lax.axis_index("win").astype(jnp.int32)
    me = group * shares + window
    ids = jnp.stack([group, window, me])

    direct = groups == 8
    by_x, by_near, by_far = shares, 2 * shares, 4 * shares
    if not direct:
        slices = features.reshape(rows, groups, depth // groups).transpose(1, 0, 2)
        slices = lax.all_to_all(slices, "sp", 0, 0)
        slices = [
            lax.dynamic_index_in_dim(slices, group ^ k, 0, keepdims=False) for k in range(groups)
        ]

    block, send, keep = project(
        ids, partner_offsets, features, proj_weight, ortholog_index.T
    )
    block = block[None]
    if direct:
        block_x = xor_permute(block, by_x)
        block_far = xor_permute(block, by_far)
        block_near = xor_permute(block, by_near)
    else:
        gathered = lax.all_gather(block, "sp", tiled=True)

    arrived = [xor_permute(send, 1)]
    if direct:
        arrived[0], block_x = lax.optimization_barrier((arrived[0], block_x))
    sent = send
    seen = 1
    stages = []
    low = 1
    while keep.shape[0] > 32:
        count = 4
        keep, sends, seen = stage(ids, keep, sent, arrived, seen, low, count, embed)
        if direct and stages:
            *sends, block_near, block_far = lax.optimization_barrier(
                (*sends, block_near, block_far)
            )
            far_x = xor_permute(block_far, by_x)
        arrived = [xor_permute(piece, (r + 1) << low) for r, piece in enumerate(sends)]
        sent = sends[0]
        stages.append((low, count))
        low += 2
    size = keep.shape[0]
    part = keep
    for piece in arrived:
        part = part + piece[:size].astype(F32)
    sums = [sent, *arrived]
    extra = devices >> low
    if extra > 1:
        mine = jnp.concatenate([part.astype(BF16)] + [piece[size:] for piece in sums])
        others = [xor_permute(mine, r << low) for r in range(1, extra)]
        for piece in others:
            part = part + piece[:size].astype(F32)
        sums = [mine, *others]
    part = part.astype(BF16)
    for number, (low, count) in enumerate(reversed(stages)):
        if direct and number == 1:
            part, block_far = lax.optimization_barrier((part, block_far))
            far_near = xor_permute(block_far, by_near)
            part, far_x = lax.optimization_barrier((part, far_x))
        part = jnp.concatenate(
            [part] + [xor_permute(part, r << low) for r in range(1, count)], axis=0
        )
    part = part.reshape(-1, size, part.shape[1])
    if direct:
        part, far_near, block_near, ids = lax.optimization_barrier(
            (part, far_near, block_near, ids)
        )
        near_x = xor_permute(block_near, by_x)
        slices = cut(ids, features, groups)
    else:
        order = slice_order = list(range(groups))
        blocks = [
            lax.dynamic_index_in_dim(gathered, group ^ k, 0, keepdims=True) for k in order
        ]
    other = xor_permute(part, 1)
    if direct:
        other, *slices = lax.optimization_barrier((other, *slices))
        slice_order = [0, 2, 4, 6, 5, 7, 1, 3]
        for k in (2, 4, 6, 5):
            slices[k] = xor_permute(slices[k], k * shares)
        for k, before in ((7, 2), (1, 4)):
            slices[k], slices[before] = lax.optimization_barrier((slices[k], slices[before]))
            slices[k] = xor_permute(slices[k], k * shares)
        slices[3] = xor_permute(slices[3], 3 * shares)
        slices = [slices[k] for k in slice_order]
        far_near_x = xor_permute(far_near, by_x)

    whitener, mean = whiten(ids, part, other, sums, seen, tuple(stages), rows, embed)
    if direct:
        mean, near_x = lax.optimization_barrier((mean, near_x))
        blocks = [block, block_x, block_near, near_x, block_far, far_x, far_near, far_near_x]
        order = list(range(groups))
    loss, grad = contrast(ids, blocks, order, mean, whitener)
    pieces = []
    for mask in reversed(range(0, shares, 2)):
        keep, send = weight_pieces(
            ids, grad, slices, slice_order, shares, (mask, mask + 1)
        )
        arrived = xor_permute(send, 1)
        if mask:
            pieces.append(xor_permute(join(keep, arrived), mask))
        else:
            pieces = [keep, arrived] + pieces
    return loss[0], finish(pieces, whitener)


def solution(mesh):
    return jax.shard_map(
        shards,
        mesh=mesh,
        in_specs=(P(("sp", "win"), None), P(), P("sp", None), P(("sp", "win"), None)),
        out_specs=(P(("sp", "win")), P(("sp", "win"), None)),
        check_vma=False,
    )
```
